128 devices in a mesh: lat: 8 (over x_hi, z), lon: 16 (over y, x_lo, core).
Axes of the slice: x: 4 (x_hi: 2, x_lo: 2; x = x_hi * 2 + x_lo), y: 4, z: 4, core: 2. Of those that a mesh axis runs over, the one named last changes fastest.
Arguments:
- tokens: bfloat16 [2, 128, 384, 1024], P(None, 'lat', 'lon'), may hold values from -6 to 6
- qkv_weight: bfloat16 [1024, 3072], replicated, may hold values from -0.1875 to 0.1875
- out_weight: bfloat16 [1024, 1024], replicated, may hold values from -0.1875 to 0.1875
- merge_weight: bfloat16 [4096, 1024], replicated, may hold values from -0.09375 to 0.09375
- merged_grad: bfloat16 [2, 64, 192, 1024], P(None, 'lat', 'lon'), may hold values from -6 to 6
Outputs:
- merged: bfloat16 [2, 64, 192, 1024], P(None, 'lat', 'lon')
- tokens_grad: bfloat16 [2, 128, 384, 1024], P(None, 'lat', 'lon')
- qkv_weight_grad: float32 [1024, 3072], P(('lat', 'lon'))
- out_weight_grad: float32 [1024, 1024], P(('lat', 'lon'))
The draws below stay inside these ranges and needn't reach their ends.
All inputs are finite; a program needn't handle non-finite values.
Results may differ from the reference program's by a relative error of at most 0.02.
Values may be sent and summed in bfloat16 or wider, within the bound.
A program may use at most 192 MiB of HBM per device.

```python
import jax
import jax.numpy as jnp
from jax import lax

C = 1024
HEADS = 32
MERGED = 1024
LEV = 2
WIN = 8
SHIFT = 4
GRID_LAT = 128
GRID_LON = 384


def steps_of(own_key, dims, shards, least, largest):
    factor_of, own = 1.0, jax.random.fold_in(own_key, 6)
    for position, blocks in shards:
        draws = jnp.exp(jax.random.uniform(jax.random.fold_in(own, position), (blocks,), jnp.float32, least / len(shards), largest / len(shards)))
        factor_of = factor_of * jnp.repeat(draws, dims[position] // blocks).reshape([-1 if axis == position else 1 for axis in range(len(dims))])
    return factor_of


def normal_values(own_key, extent, scale, most, cuts=(), dtype=jnp.bfloat16):
    drawn = scale * jax.random.normal(own_key, extent, jnp.float32)
    if cuts:
        drawn = drawn * steps_of(own_key, extent, cuts, -0.22, 0.18)
    return jnp.clip(drawn, -most, most).astype(dtype)


def setup_inputs(seed: int = 0) -> dict:
    seeds = jax.random.split(jax.random.key(seed), 6)
    tokens = normal_values(seeds[0], (LEV, GRID_LAT, GRID_LON, C), 1.0, 6.0, ((1, 8), (2, 16)))
    qkv_weight = normal_values(seeds[1], (C, 3 * C), C ** -0.5, 0.1875)
    out_weight = normal_values(seeds[2], (C, C), C ** -0.5, 0.1875)
    merge_weight = normal_values(seeds[3], (4 * C, MERGED), (4 * C) ** -0.5, 0.09375)
    merged_grad = normal_values(seeds[4], (LEV, GRID_LAT // 2, GRID_LON // 2, MERGED), 1.0, 6.0, ((1, 8), (2, 16)))
    return dict(tokens=tokens, qkv_weight=qkv_weight, out_weight=out_weight, merge_weight=merge_weight, merged_grad=merged_grad)


epsilon = 1e-05

def normalize(grid_field):
    values = grid_field.astype(jnp.float32)
    center = lax.optimization_barrier(jnp.mean(values, axis=-1, keepdims=True))
    spread = lax.optimization_barrier(jnp.mean(jnp.square(values - center), axis=-1, keepdims=True))
    return ((values - center) * lax.rsqrt(spread + epsilon)).astype(jnp.bfloat16)

def window_attention(window_values, region_marks):
    windows = window_values.shape[0]
    places = window_values.shape[1]
    channels = window_values.shape[2] // 3
    head_dim = channels // HEADS
    pieces = window_values.reshape(windows, places, 3, HEADS, head_dim)
    queries = pieces[:, :, 0].astype(jnp.float32)
    keys_part = pieces[:, :, 1].astype(jnp.float32)
    values_part = pieces[:, :, 2].astype(jnp.float32)
    scores = jnp.einsum('bqhd,bkhd->bhqk', queries, keys_part) * head_dim ** (-0.5)
    same_region = region_marks[:, None, :, None] == region_marks[:, None, None, :]
    weights = jnp.where(same_region, jnp.exp(scores), 0.0)
    attention = (weights / lax.optimization_barrier(jnp.sum(weights, axis=-1, keepdims=True))).astype(jnp.bfloat16)
    mixture = jnp.einsum('bhqk,bkhd->bqhd', attention.astype(jnp.float32), values_part)
    return mixture.astype(jnp.bfloat16).reshape(windows, places, channels)

def to_windows(grid_field):
    lev_count, lat_rows, lon_cols, channels = grid_field.shape
    blocks = grid_field.reshape(lev_count, lat_rows // WIN, WIN, lon_cols // WIN, WIN, channels)
    blocks = blocks.transpose(1, 3, 0, 2, 4, 5)
    return blocks.reshape(lat_rows // WIN, lon_cols // WIN, lev_count * WIN * WIN, channels)

def from_windows(blocks, lev_count, lat_rows, lon_cols):
    channels = blocks.shape[-1]
    grid_field = blocks.reshape(lat_rows // WIN, lon_cols // WIN, lev_count, WIN, WIN, channels)
    return grid_field.transpose(2, 0, 3, 1, 4, 5).reshape(lev_count, lat_rows, lon_cols, channels)

def attend_all(projected, region):
    blocks = to_windows(projected)
    region_blocks = to_windows(region[..., None])[..., 0]
    window_step = jax.checkpoint(lambda window_pair: window_attention(window_pair[0], window_pair[1]))
    mixture = lax.map(window_step, (blocks, region_blocks))
    return from_windows(mixture, LEV, GRID_LAT, GRID_LON)

def merge(grid_field, merge_weight):
    lev_count, lat_rows, lon_cols, channels = grid_field.shape
    groups = grid_field.reshape(lev_count, lat_rows // 2, 2, lon_cols // 2, 2, channels)
    groups = groups.transpose(0, 1, 3, 4, 2, 5).reshape(lev_count, lat_rows // 2, lon_cols // 2, 4 * channels)
    normed = normalize(groups)
    result = jnp.dot(normed.reshape(-1, 4 * channels), merge_weight, preferred_element_type=jnp.float32)
    return result.astype(jnp.bfloat16).reshape(lev_count, lat_rows // 2, lon_cols // 2, merge_weight.shape[1])

def reference(tokens, qkv_weight, out_weight, merge_weight, merged_grad):
    channels = tokens.shape[-1]
    rolled = jnp.roll(tokens, (-SHIFT, -SHIFT), axis=(1, 2))
    normed, norm_back = jax.vjp(normalize, rolled)
    flat_norm = normed.reshape(-1, channels)
    projected = jnp.dot(flat_norm, qkv_weight, preferred_element_type=jnp.float32).astype(jnp.bfloat16)
    projected = projected.reshape(LEV, GRID_LAT, GRID_LON, 3 * channels)
    region_rows = (jnp.arange(GRID_LAT) >= GRID_LAT - SHIFT).astype(jnp.int32)
    region = jnp.broadcast_to(region_rows[None, :, None], (LEV, GRID_LAT, GRID_LON))
    mixture, attend_back = jax.vjp(lambda grid_values: attend_all(grid_values, region), projected)
    mixture_flat = mixture.reshape(-1, channels)
    branch = jnp.dot(mixture_flat, out_weight, preferred_element_type=jnp.float32)
    shifted_out = (rolled.reshape(-1, channels).astype(jnp.float32) + branch).astype(jnp.bfloat16)
    block_out = jnp.roll(shifted_out.reshape(rolled.shape), (SHIFT, SHIFT), axis=(1, 2))
    merged, merge_back = jax.vjp(lambda grid_values: merge(grid_values, merge_weight), block_out)
    block_grad = merge_back(merged_grad)[0]
    grad_rolled = jnp.roll(block_grad, (-SHIFT, -SHIFT), axis=(1, 2)).reshape(-1, channels)
    mixture_grad = lax.dot_general(grad_rolled, out_weight, (((1,), (1,)), ((), ())), preferred_element_type=jnp.float32).astype(jnp.bfloat16)
    out_weight_grad = lax.dot_general(mixture_flat, grad_rolled, (((0,), (0,)), ((), ())), preferred_element_type=jnp.float32)
    projected_grad = attend_back(mixture_grad.reshape(mixture.shape))[0].reshape(-1, 3 * channels)
    qkv_weight_grad = lax.dot_general(flat_norm, projected_grad, (((0,), (0,)), ((), ())), preferred_element_type=jnp.float32)
    normed_grad = lax.dot_general(projected_grad, qkv_weight, (((1,), (1,)), ((), ())), preferred_element_type=jnp.float32).astype(jnp.bfloat16)
    input_part = norm_back(normed_grad.reshape(normed.shape))[0].reshape(-1, channels)
    rolled_grad = (grad_rolled.astype(jnp.float32) + input_part.astype(jnp.float32)).astype(jnp.bfloat16)
    tokens_grad = jnp.roll(rolled_grad.reshape(rolled.shape), (SHIFT, SHIFT), axis=(1, 2))
    return (merged, tokens_grad, qkv_weight_grad, out_weight_grad)
```

```python
import jax
import jax.numpy as jnp
from jax import lax
from jax.experimental import pallas as pl
from jax.experimental.pallas import tpu as pltpu
from jax.sharding import PartitionSpec as P

HEADS = 32
WIN = 8
SHIFT = 4


epsilon = 1e-05


MESH = pl.DeviceIdType.MESH
CHUNKS = 4
LANES = 512
WIDTH = 256


def place():
    lat, lon = lax.axis_index("lat"), lax.axis_index("lon")
    return (lat // 4) * 2 + (lon // 2) % 2, lon // 4, lat % 4, lon % 2


def device_at(x, y, z, core):
    return ((x // 2) * 4 + z, y * 4 + (x % 2) * 2 + core)


def reduce_kernel(g, qkv_out, out_out, from_core, acc_a, in_a, acc_b, in_b, acc_c, in_c, send, recv):
    x, y, z, core = place()
    here = (x, y, z)

    def moved(axis, step):
        there = list(here)
        there[axis] = (here[axis] + step) % 4
        return device_at(there[0], there[1], there[2], core)

    sibling = device_at(x, y, z, 1 - core)
    barrier = pltpu.get_barrier_semaphore()
    partners = [sibling] + [moved(axis, step) for axis in range(3) for step in (1, 2, 3)]
    for partner in partners:
        pl.semaphore_signal(barrier, inc=1, device_id=partner, device_id_type=MESH)
    pl.semaphore_wait(barrier, len(partners))

    started = []

    def push(stream, slot, source, target, partner):
        copy = pltpu.make_async_remote_copy(
            src_ref=source, dst_ref=target, send_sem=send.at[stream, slot],
            recv_sem=recv.at[stream, slot], device_id=partner, device_id_type=MESH)
        copy.start()
        started.append(copy)
        return copy

    def run(stream):
        chunk, part = stream // 2, stream % 2
        lanes = pl.ds(part * WIDTH, WIDTH)
        order = [(stream + k) % 3 for k in range(3)]
        mine = [here[axis] for axis in order]
        copy = push(stream, 0, g.at[chunk, :, 1 - core, :, lanes], from_core.at[stream], sibling)
        yield
        copy.wait_recv()

        def add_block(index, carry):
            a, b = index // 4, index % 4
            for c in range(4):
                at = [None, None, None]
                for axis, value in zip(order, (a, b, c)):
                    at[axis] = value
                row = ((at[0] // 2) * 4 + at[2]) * 8 + at[1] * 2 + at[0] % 2
                total = g[chunk, row, core, :, lanes].astype(jnp.float32) + from_core[stream, row].astype(jnp.float32)
                acc_a[stream, a, b * 4 + c] = total.astype(jnp.bfloat16)
            return carry

        lax.fori_loop(0, 16, add_block, 0)
        for level, (acc, arrived, blocks) in enumerate(((acc_a, in_a, 16), (acc_b, in_b, 4))):
            axis, p = order[level], mine[level]
            half = blocks // 2
            low, high = pl.ds(0, half), pl.ds(half, half)
            base = 1 + level * 6
            right, left = moved(axis, 1), moved(axis, 3)
            after, before, across = (p + 1) % 4, (p + 3) % 4, (p + 2) % 4
            relay_up = push(stream, base, acc.at[stream, across, high], arrived.at[stream, 0], right)
            relay_down = push(stream, base + 1, acc.at[stream, across, low], arrived.at[stream, 1], left)
            own_up = push(stream, base + 2, acc.at[stream, after, low], arrived.at[stream, 2], right)
            own_down = push(stream, base + 3, acc.at[stream, before, high], arrived.at[stream, 3], left)
            yield
            relay_up.wait_recv()
            acc[stream, after, high] = (acc[stream, after, high].astype(jnp.float32)
                                        + arrived[stream, 0].astype(jnp.float32)).astype(jnp.bfloat16)
            sum_up = push(stream, base + 4, acc.at[stream, after, high], arrived.at[stream, 4], right)
            relay_down.wait_recv()
            acc[stream, before, low] = (acc[stream, before, low].astype(jnp.float32)
                                        + arrived[stream, 1].astype(jnp.float32)).astype(jnp.bfloat16)
            sum_down = push(stream, base + 5, acc.at[stream, before, low], arrived.at[stream, 5], left)
            yield
            own_up.wait_recv()
            own_down.wait_recv()
            sum_up.wait_recv()
            sum_down.wait_recv()
            total_low = (acc[stream, p, low].astype(jnp.float32) + arrived[stream, 2].astype(jnp.float32)
                         + arrived[stream, 5].astype(jnp.float32)).astype(jnp.bfloat16)
            total_high = (acc[stream, p, high].astype(jnp.float32) + arrived[stream, 3].astype(jnp.float32)
                          + arrived[stream, 4].astype(jnp.float32)).astype(jnp.bfloat16)
            if level == 0:
                for i in range(2):
                    acc_b[stream, i] = total_low[i * 4:i * 4 + 4]
                    acc_b[stream, i + 2] = total_high[i * 4:i * 4 + 4]
            else:
                for i in range(2):
                    acc_c[stream, i] = total_low[i]
                    acc_c[stream, i + 2] = total_high[i]
        axis, p = order[2], mine[2]
        last = [push(stream, 13 + k, acc_c.at[stream, (p + k + 1) % 4], in_c.at[stream, k], moved(axis, k + 1))
                for k in range(3)]
        yield
        total = acc_c[stream, p].astype(jnp.float32)
        for k in range(3):
            last[k].wait_recv()
            total = total + in_c[stream, k].astype(jnp.float32)
        columns = WIDTH * chunk
        if part == 0:
            qkv_out[:, columns:columns + WIDTH] = total[:8]
            qkv_out[:, 2048 + columns:2048 + columns + WIDTH] = total[8:]
        else:
            qkv_out[:, 1024 + columns:1024 + columns + WIDTH] = total[:8]
            out_out[:, columns:columns + WIDTH] = total[8:]

    running = [run(stream) for stream in range(2 * CHUNKS)]
    while running:
        kept = []
        for job in running:
            try:
                next(job)
                kept.append(job)
            except StopIteration:
                pass
        running = kept
    for copy in started:
        copy.wait_send()


def reduce_terms(terms):
    streams = 2 * CHUNKS
    bf16 = jnp.bfloat16
    return pl.pallas_call(
        reduce_kernel,
        out_shape=(jax.ShapeDtypeStruct((8, 3072), jnp.float32), jax.ShapeDtypeStruct((8, 1024), jnp.float32)),
        in_specs=[pl.BlockSpec(memory_space=pltpu.VMEM)],
        out_specs=(pl.BlockSpec(memory_space=pltpu.VMEM), pl.BlockSpec(memory_space=pltpu.VMEM)),
        scratch_shapes=[
            pltpu.VMEM((streams, 64, 16, WIDTH), bf16),
            pltpu.VMEM((streams, 4, 16, 16, WIDTH), bf16),
            pltpu.VMEM((streams, 6, 8, 16, WIDTH), bf16),
            pltpu.VMEM((streams, 4, 4, 16, WIDTH), bf16),
            pltpu.VMEM((streams, 6, 2, 16, WIDTH), bf16),
            pltpu.VMEM((streams, 4, 16, WIDTH), bf16),
            pltpu.VMEM((streams, 3, 16, WIDTH), bf16),
            pltpu.SemaphoreType.DMA((streams, 16)),
            pltpu.SemaphoreType.DMA((streams, 16)),
        ],
        compiler_params=pltpu.CompilerParams(
            collective_id=0, has_side_effects=True, vmem_limit_bytes=60 * 1024 * 1024),
        name="reduce_terms",
    )(terms)


def shifted(block, axis, distance):
    devices = range(lax.axis_size(axis))
    route = [((i - distance) % len(devices), i) for i in devices]
    return lax.ppermute(block, axis, route)


def normalize(grid_field):
    values = grid_field.astype(jnp.float32)
    center = jnp.mean(values, axis=-1, keepdims=True)
    spread = jnp.mean(jnp.square(values - center), axis=-1, keepdims=True)
    return ((values - center) * lax.rsqrt(spread + epsilon)).astype(jnp.bfloat16)


def window_attention(window_values, region_marks):
    windows = window_values.shape[0]
    places = window_values.shape[1]
    channels = window_values.shape[2] // 3
    head_dim = channels // HEADS
    pieces = window_values.reshape(windows, places, 3, HEADS, head_dim)
    queries = pieces[:, :, 0]
    keys_part = pieces[:, :, 1]
    values_part = pieces[:, :, 2]
    scores = jnp.einsum(
        "bqhd,bkhd->bhqk", queries, keys_part, preferred_element_type=jnp.float32
    ) * head_dim ** (-0.5)
    same_region = region_marks[:, None, :, None] == region_marks[:, None, None, :]
    weights = jnp.where(same_region, jnp.exp(scores), 0.0)
    attention = (weights / jnp.sum(weights, axis=-1, keepdims=True)).astype(jnp.bfloat16)
    mixture = jnp.einsum(
        "bhqk,bkhd->bqhd", attention, values_part, preferred_element_type=jnp.float32
    )
    return mixture.astype(jnp.bfloat16).reshape(windows, places, channels)


def to_windows(grid_field):
    lev_count, lat_rows, lon_cols, channels = grid_field.shape
    blocks = grid_field.reshape(lev_count, lat_rows // WIN, WIN, lon_cols // WIN, WIN, channels)
    blocks = blocks.transpose(1, 3, 0, 2, 4, 5)
    return blocks.reshape(lat_rows // WIN * (lon_cols // WIN), lev_count * WIN * WIN, channels)


def from_windows(blocks, lev_count, lat_rows, lon_cols):
    channels = blocks.shape[-1]
    grid_field = blocks.reshape(lat_rows // WIN, lon_cols // WIN, lev_count, WIN, WIN, channels)
    return grid_field.transpose(2, 0, 3, 1, 4, 5).reshape(lev_count, lat_rows, lon_cols, channels)


def attend_local(projected, region):
    lev_count, lat_rows, lon_cols, channels = projected.shape
    blocks = to_windows(projected)
    region_blocks = to_windows(region[..., None])[..., 0]
    mixture = window_attention(blocks, region_blocks)
    return from_windows(mixture, lev_count, lat_rows, lon_cols)


def merge(grid_field, merge_weight):
    lev_count, lat_rows, lon_cols, channels = grid_field.shape
    groups = grid_field.reshape(lev_count, lat_rows // 2, 2, lon_cols // 2, 2, channels)
    groups = groups.transpose(0, 1, 3, 4, 2, 5).reshape(
        lev_count, lat_rows // 2, lon_cols // 2, 4 * channels
    )
    normed = normalize(groups)
    result = jnp.dot(
        normed.reshape(-1, 4 * channels), merge_weight, preferred_element_type=jnp.float32
    )
    return result.astype(jnp.bfloat16).reshape(
        lev_count, lat_rows // 2, lon_cols // 2, merge_weight.shape[1]
    )


def move_strips(grid_field, strip_width, offset):
    if offset == 1:
        outgoing = grid_field[:, :, -strip_width:]
    else:
        outgoing = grid_field[:, :, :strip_width]
    arrived = shifted(outgoing, "lon", offset)
    if offset == 1:
        middle = jnp.concatenate([arrived, grid_field[:, :, :-strip_width]], axis=2)
        outgoing_rows = middle[:, -strip_width:]
    else:
        middle = jnp.concatenate([grid_field[:, :, strip_width:], arrived], axis=2)
        outgoing_rows = middle[:, :strip_width]
    arrived_rows = shifted(outgoing_rows, "lat", offset)
    if offset == 1:
        return jnp.concatenate([arrived_rows, middle[:, :-strip_width]], axis=1)
    return jnp.concatenate([middle[:, strip_width:], arrived_rows], axis=1)


def shards(tokens, qkv_weight, out_weight, merge_weight, merged_grad):
    lev_count, lat_rows, lon_cols, channels = tokens.shape
    framed = move_strips(tokens, SHIFT, 1)
    normed, norm_back = jax.vjp(normalize, framed)
    flat_norm = normed.reshape(-1, channels)
    projected = jnp.dot(flat_norm, qkv_weight, preferred_element_type=jnp.float32).astype(
        jnp.bfloat16
    )
    projected = projected.reshape(lev_count, lat_rows, lon_cols, 3 * channels)
    edge_rows = (lax.axis_index("lat") == 0) & (jnp.arange(lat_rows) < SHIFT)
    region = jnp.broadcast_to(
        edge_rows.astype(jnp.int32)[None, :, None], (lev_count, lat_rows, lon_cols)
    )
    mixture, attend_back = jax.vjp(lambda grid_values: attend_local(grid_values, region), projected)
    mixture_flat = mixture.reshape(-1, channels)
    branch = jnp.dot(mixture_flat, out_weight, preferred_element_type=jnp.float32)
    shifted_out = (framed.reshape(-1, channels).astype(jnp.float32) + branch).astype(jnp.bfloat16)
    shifted_out = shifted_out.reshape(framed.shape)
    framed_merged, merge_back = jax.vjp(lambda grid_values: merge(grid_values, merge_weight), shifted_out)
    grad_rolled = merge_back(move_strips(merged_grad, SHIFT // 2, 1))[0].reshape(-1, channels)
    merged = move_strips(framed_merged, SHIFT // 2, -1)
    mixture_grad = lax.dot_general(
        grad_rolled, out_weight, (((1,), (1,)), ((), ())), preferred_element_type=jnp.float32
    ).astype(jnp.bfloat16)
    out_terms = lax.dot_general(
        mixture_flat, grad_rolled, (((0,), (0,)), ((), ())), preferred_element_type=jnp.float32
    )
    projected_grad = attend_back(mixture_grad.reshape(mixture.shape))[0].reshape(-1, 3 * channels)
    qkv_terms = lax.dot_general(
        flat_norm, projected_grad, (((0,), (0,)), ((), ())), preferred_element_type=jnp.float32
    )
    normed_grad = lax.dot_general(
        projected_grad, qkv_weight, (((1,), (1,)), ((), ())), preferred_element_type=jnp.float32
    ).astype(jnp.bfloat16)
    input_part = norm_back(normed_grad.reshape(normed.shape))[0].reshape(-1, channels)
    framed_grad = (grad_rolled.astype(jnp.float32) + input_part.astype(jnp.float32)).astype(
        jnp.bfloat16
    )
    tokens_grad = move_strips(framed_grad.reshape(framed.shape), SHIFT, -1)
    terms = jnp.concatenate([qkv_terms, out_terms], axis=1).astype(jnp.bfloat16)
    terms = terms.reshape(64, 2, 8, 2, 2, 4, 256).transpose(5, 0, 1, 3, 2, 4, 6).reshape(4, 64, 2, 16, 512)
    qkv_weight_grad, out_weight_grad = reduce_terms(terms)
    return (merged, tokens_grad, qkv_weight_grad, out_weight_grad)


def solution(mesh):
    in_specs = (P(None, "lat", "lon", None), P(), P(), P(), P(None, "lat", "lon", None))
    out_specs = (
        P(None, "lat", "lon", None),
        P(None, "lat", "lon", None),
        P(("lat", "lon"), None),
        P(("lat", "lon"), None),
    )
    return jax.shard_map(shards, mesh=mesh, in_specs=in_specs, out_specs=out_specs, check_vma=False)
```

```python
import jax
import jax.numpy as jnp
import numpy as np
from jax import lax
from jax.experimental import pallas as pl
from jax.experimental.pallas import tpu as pltpu
from jax.sharding import PartitionSpec as P

SHIFT = 4
F32, BF16 = jnp.float32, jnp.bfloat16
epsilon = 1e-05
SCALE = 32 ** -0.5
MIB = 1024 * 1024
NT = (((1,), (1,)), ((), ()))
TN = (((0,), (0,)), ((), ()))


def params(limit=60):
    return pltpu.CompilerParams(vmem_limit_bytes=limit * MIB)


def dot(left, right, dims=(((1,), (0,)), ((), ()))):
    return lax.dot_general(left, right, dims, preferred_element_type=F32)


def window_order():
    t = np.arange(128)
    quarter, level, a, b = t // 32, t // 16 % 2, t // 4 % 4, t % 4
    natural = (level * 8 + 2 * a + quarter % 2) * 8 + 2 * b + quarter // 2
    return (natural[:, None] == t[None, :]).astype(np.float32)


def statistics(values):
    center = jnp.mean(values, axis=-1, keepdims=True)
    shifted_values = values - center
    spread = jnp.mean(jnp.square(shifted_values), axis=-1, keepdims=True)
    return shifted_values, lax.rsqrt(spread + epsilon)


def prepare_kernel(framed, order, x_out, normed_out, normed_turned):
    natural = framed[...].astype(F32).reshape(128, 1024).astype(BF16)
    values = dot(order[...], natural)
    x_out[...] = values.astype(BF16)
    centered, inverse = statistics(values)
    normed = centered * inverse
    normed_out[...] = normed.astype(BF16)
    normed_turned[...] = normed.T.astype(BF16)


def prepare(framed, order):
    return pl.pallas_call(
        prepare_kernel,
        grid=(6,),
        out_shape=(jax.ShapeDtypeStruct((768, 1024), BF16), jax.ShapeDtypeStruct((768, 1024), BF16),
                   jax.ShapeDtypeStruct((1024, 768), BF16)),
        in_specs=[pl.BlockSpec((2, 8, 8, 1024), lambda w: (0, w // 3, w % 3, 0)),
                  pl.BlockSpec((128, 128), lambda w: (0, 0))],
        out_specs=(pl.BlockSpec((128, 1024), lambda w: (w, 0)), pl.BlockSpec((128, 1024), lambda w: (w, 0)),
                   pl.BlockSpec((1024, 128), lambda w: (0, w))),
        compiler_params=params(), name="prepare",
    )(framed, order)


def head_masks(rows):
    lane = lax.broadcasted_iota(jnp.int32, (rows, 128), 1)
    return [lane // 32 == head for head in range(4)]


def spread_heads(values, masks):
    zero = jnp.zeros_like(values)
    return jnp.concatenate([jnp.where(mask, values, zero) for mask in masks], axis=0)


def edge_marks(edge):
    row = (lax.broadcasted_iota(jnp.int32, (128, 1), 0) // 4 % 4 < 2) & edge
    column = (lax.broadcasted_iota(jnp.int32, (1, 512), 1) // 4 % 4 < 2) & edge
    return row.astype(jnp.int32) != column.astype(jnp.int32)


def attend_kernel(normed, wq, wk, wv, q_out, k_out, v_out, p_out, mix_out, mix_turned):
    for out, weight in ((q_out, wq), (k_out, wk), (v_out, wv)):
        out[...] = dot(normed[...], weight[...]).astype(BF16)
    masks = head_masks(128)
    edge = lax.axis_index("lat") == 0

    def column(wb, carry):
        for wa in range(2):
            w = wa * 3 + wb
            rows = pl.ds(pl.multiple_of(w * 128, 128), 128)
            for group in range(2):
                lanes = pl.ds(group * 128, 128)
                queries, keys, values = q_out[rows, lanes], k_out[rows, lanes], v_out[rows, lanes]
                scores = dot(queries, spread_heads(keys, masks), NT)
                weights = jnp.exp(scores * SCALE)
                if wa == 0:
                    weights = jnp.where(edge_marks(edge), 0.0, weights)
                pieces = []
                for head in range(4):
                    piece = weights[:, head * 128:head * 128 + 128]
                    pieces.append(piece * (1.0 / jnp.sum(piece, axis=-1, keepdims=True)))
                attention = jnp.concatenate(pieces, axis=1).astype(BF16)
                p_out[w, group] = attention
                mixture = dot(attention, spread_heads(values, masks))
                mix_out[rows, lanes] = mixture.astype(BF16)
                mix_turned[lanes, rows] = mixture.T.astype(BF16)
        return carry

    lax.fori_loop(0, 3, column, 0)


def attend(normed, qkv_weight):
    tokens = jax.ShapeDtypeStruct((768, 1024), BF16)
    block = pl.BlockSpec((768, 256), lambda c: (0, c))
    weight = lambda third: pl.BlockSpec((1024, 256), lambda c: (0, third * 4 + c))
    return pl.pallas_call(
        attend_kernel,
        grid=(4,),
        out_shape=(tokens, tokens, tokens, jax.ShapeDtypeStruct((6, 8, 128, 512), BF16), tokens,
                   jax.ShapeDtypeStruct((1024, 768), BF16)),
        in_specs=[pl.BlockSpec((768, 1024), lambda c: (0, 0)), weight(0), weight(1), weight(2)],
        out_specs=(block, block, block, pl.BlockSpec((6, 2, 128, 512), lambda c: (0, c, 0, 0)), block,
                   pl.BlockSpec((256, 768), lambda c: (c, 0))),
        compiler_params=params(), name="attend",
    )(normed, qkv_weight, qkv_weight, qkv_weight)


def merge_kernel(x, mixture, merged_grad, out_weight, merge_weight, merged_out, grad_out, mixture_grad,
                 normed, total, normed_grad):
    step = pl.program_id(0)

    @pl.when(step == 0)
    def _():
        for w in range(6):
            rows = pl.ds(w * 128, 128)
            values = x[rows].astype(F32) + dot(mixture[rows], out_weight[...])
            values = values.astype(BF16).astype(F32)
            quarters = [values[32 * j:32 * j + 32] for j in range(4)]
            center = sum(jnp.sum(part, axis=-1, keepdims=True) for part in quarters) * (1 / 4096)
            quarters = [part - center for part in quarters]
            spread = sum(jnp.sum(jnp.square(part), axis=-1, keepdims=True) for part in quarters) * (1 / 4096)
            inverse = lax.rsqrt(spread + epsilon)
            for j in range(4):
                normed[j, pl.ds(w * 32, 32)] = quarters[j] * inverse
            total[1, pl.ds(w * 32, 32)] = jnp.broadcast_to(inverse, (32, 1024))
        total[0] = jnp.zeros((192, 1024), F32)

    total[0] += dot(normed[step].astype(BF16), merge_weight[...])
    normed_grad[step] = dot(merged_grad[...], merge_weight[...], NT).astype(BF16).astype(F32)

    @pl.when(step == 3)
    def _():
        merged_out[...] = total[0].astype(BF16)
        for w in range(6):
            part = pl.ds(w * 32, 32)
            first = sum(jnp.sum(normed_grad[j, part], axis=-1, keepdims=True) for j in range(4)) * (1 / 4096)
            second = sum(jnp.sum(normed_grad[j, part] * normed[j, part], axis=-1, keepdims=True)
                         for j in range(4)) * (1 / 4096)
            inverse = total[1, part]
            for j in range(4):
                value = inverse * (normed_grad[j, part] - first - normed[j, part] * second)
                grad_out[pl.ds(w * 128 + j * 32, 32)] = value.astype(BF16)
        mixture_grad[...] = dot(grad_out[...], out_weight[...], NT).astype(BF16)


def merge_both(x, mixture, merged_grad, out_weight, merge_weight):
    whole = lambda rows: pl.BlockSpec((rows, 1024), lambda j: (0, 0))
    tokens = jax.ShapeDtypeStruct((768, 1024), BF16)
    return pl.pallas_call(
        merge_kernel,
        grid=(4,),
        out_shape=(jax.ShapeDtypeStruct((192, 1024), BF16), tokens, tokens),
        in_specs=[whole(768), whole(768), whole(192), whole(1024), pl.BlockSpec((1024, 1024), lambda j: (j, 0))],
        out_specs=(whole(192), whole(768), whole(768)),
        scratch_shapes=[pltpu.VMEM((4, 192, 1024), F32), pltpu.VMEM((2, 192, 1024), F32),
                        pltpu.VMEM((4, 192, 1024), F32)],
        compiler_params=params(), name="merge_both",
    )(x, mixture, merged_grad, out_weight, merge_weight)


def attend_back_kernel(q, k, v, p, mixture, mixture_grad, dq, dk, dv):
    masks = head_masks(128)
    row = lax.broadcasted_iota(jnp.int32, (512, 128), 0) // 128
    lane = lax.broadcasted_iota(jnp.int32, (512, 128), 1) // 32
    minus_heads = jnp.where(row == lane, -1.0, 0.0).astype(BF16)

    def own_heads(turned):
        return jnp.concatenate([turned[32 * head:32 * head + 32, 128 * head:128 * head + 128] for head in range(4)],
                               axis=0).T

    def column(wb, carry):
        for wa in range(2):
            w = wa * 3 + wb
            rows = pl.ds(pl.multiple_of(w * 128, 128), 128)
            for group in range(2):
                lanes = pl.ds(group * 128, 128)
                queries, keys, values = q[rows, lanes], k[rows, lanes], v[rows, lanes]
                out_grad = mixture_grad[rows, lanes]
                product = (out_grad.astype(F32) * mixture[rows, lanes].astype(F32)).astype(BF16)
                attention = p[w, group]
                change = dot(jnp.concatenate([out_grad, product], axis=1),
                             jnp.concatenate([spread_heads(values, masks), minus_heads], axis=1), NT)
                scores_grad = (attention.astype(F32) * change).astype(BF16)
                dq[rows, lanes] = (dot(scores_grad, spread_heads(keys, masks)) * SCALE).astype(BF16)
                dk[rows, lanes] = (own_heads(dot(queries, scores_grad, TN)) * SCALE).astype(BF16)
                dv[rows, lanes] = own_heads(dot(out_grad, attention, TN)).astype(BF16)
        return carry

    lax.fori_loop(0, 3, column, 0)


def attend_back(q, k, v, p, mixture, mixture_grad):
    tokens = jax.ShapeDtypeStruct((768, 1024), BF16)
    block = pl.BlockSpec((768, 256), lambda c: (0, c))
    return pl.pallas_call(
        attend_back_kernel,
        grid=(4,),
        out_shape=(tokens, tokens, tokens),
        in_specs=[block, block, block, pl.BlockSpec((6, 2, 128, 512), lambda c: (0, c, 0, 0)), block, block],
        out_specs=(block, block, block),
        compiler_params=params(), name="attend_back",
    )(q, k, v, p, mixture, mixture_grad)


MESH = pl.DeviceIdType.MESH
CHUNKS = 4
LANES = 512
WIDTH = 256


def place():
    lat, lon = lax.axis_index("lat"), lax.axis_index("lon")
    return (lat // 4) * 2 + (lon // 2) % 2, lon // 4, lat % 4, lon % 2


def device_at(x, y, z, core):
    return ((x // 2) * 4 + z, y * 4 + (x % 2) * 2 + core)


def finish_kernel(normed_turned, mix_turned, dq, dk, dv, grad, x_in, qkv_weight, order, qkv_out, out_out, framed_out,
                  g, normed_grad, from_core, acc_a, in_a, acc_b, in_b, acc_c, in_c, send, recv):
    x, y, z, core = place()
    here = (x, y, z)

    def moved(axis, step):
        there = list(here)
        there[axis] = (here[axis] + step) % 4
        return device_at(there[0], there[1], there[2], core)

    sibling = device_at(x, y, z, 1 - core)
    barrier = pltpu.get_barrier_semaphore()
    partners = [sibling] + [moved(axis, step) for axis in range(3) for step in (1, 2, 3)]
    for partner in partners:
        pl.semaphore_signal(barrier, inc=1, device_id=partner, device_id_type=MESH)
    pl.semaphore_wait(barrier, len(partners))

    started = []

    def push(stream, slot, source, target, partner):
        copy = pltpu.make_async_remote_copy(
            src_ref=source, dst_ref=target, send_sem=send.at[stream, slot],
            recv_sem=recv.at[stream, slot], device_id=partner, device_id_type=MESH)
        copy.start()
        started.append(copy)
        return copy

    def run(stream):
        chunk, part = stream // 2, stream % 2
        lanes = pl.ds(part * WIDTH, WIDTH)
        order = [(stream + k) % 3 for k in range(3)]
        mine = [here[axis] for axis in order]
        copy = push(stream, 0, g.at[chunk, :, 1 - core, :, lanes], from_core.at[stream], sibling)
        yield
        copy.wait_recv()

        def add_block(index, carry):
            a, b = index // 4, index % 4
            for c in range(4):
                at = [None, None, None]
                for axis, value in zip(order, (a, b, c)):
                    at[axis] = value
                row = ((at[0] // 2) * 4 + at[2]) * 8 + at[1] * 2 + at[0] % 2
                total = g[chunk, row, core, :, lanes].astype(F32) + from_core[stream, row].astype(F32)
                acc_a[stream, a, b * 4 + c] = total.astype(BF16)
            return carry

        lax.fori_loop(0, 16, add_block, 0)
        for level, (acc, arrived, blocks) in enumerate(((acc_a, in_a, 16), (acc_b, in_b, 4))):
            axis, p = order[level], mine[level]
            half = blocks // 2
            low, high = pl.ds(0, half), pl.ds(half, half)
            base = 1 + level * 6
            right, left = moved(axis, 1), moved(axis, 3)
            after, before, across = (p + 1) % 4, (p + 3) % 4, (p + 2) % 4
            relay_up = push(stream, base, acc.at[stream, across, high], arrived.at[stream, 0], right)
            relay_down = push(stream, base + 1, acc.at[stream, across, low], arrived.at[stream, 1], left)
            own_up = push(stream, base + 2, acc.at[stream, after, low], arrived.at[stream, 2], right)
            own_down = push(stream, base + 3, acc.at[stream, before, high], arrived.at[stream, 3], left)
            yield
            relay_up.wait_recv()
            acc[stream, after, high] = (acc[stream, after, high].astype(F32)
                                        + arrived[stream, 0].astype(F32)).astype(BF16)
            sum_up = push(stream, base + 4, acc.at[stream, after, high], arrived.at[stream, 4], right)
            relay_down.wait_recv()
            acc[stream, before, low] = (acc[stream, before, low].astype(F32)
                                        + arrived[stream, 1].astype(F32)).astype(BF16)
            sum_down = push(stream, base + 5, acc.at[stream, before, low], arrived.at[stream, 5], left)
            yield
            own_up.wait_recv()
            own_down.wait_recv()
            sum_up.wait_recv()
            sum_down.wait_recv()
            total_low = (acc[stream, p, low].astype(F32) + arrived[stream, 2].astype(F32)
                         + arrived[stream, 5].astype(F32)).astype(BF16)
            total_high = (acc[stream, p, high].astype(F32) + arrived[stream, 3].astype(F32)
                          + arrived[stream, 4].astype(F32)).astype(BF16)
            if level == 0:
                for i in range(2):
                    acc_b[stream, i] = total_low[i * 4:i * 4 + 4]
                    acc_b[stream, i + 2] = total_high[i * 4:i * 4 + 4]
            else:
                for i in range(2):
                    acc_c[stream, i] = total_low[i]
                    acc_c[stream, i + 2] = total_high[i]
        axis, p = order[2], mine[2]
        last = [push(stream, 13 + k, acc_c.at[stream, (p + k + 1) % 4], in_c.at[stream, k], moved(axis, k + 1))
                for k in range(3)]
        yield
        total = acc_c[stream, p].astype(F32)
        for k in range(3):
            last[k].wait_recv()
            total = total + in_c[stream, k].astype(F32)
        columns = WIDTH * chunk
        if part == 0:
            qkv_out[:, columns:columns + WIDTH] = total[:8]
            qkv_out[:, 2048 + columns:2048 + columns + WIDTH] = total[8:]
        else:
            qkv_out[:, 1024 + columns:1024 + columns + WIDTH] = total[:8]
            out_out[:, columns:columns + WIDTH] = total[8:]

    running = []

    def advance():
        for job in list(running):
            try:
                next(job)
            except StopIteration:
                running.remove(job)

    for chunk in range(CHUNKS):
        columns = slice(chunk * 256, chunk * 256 + 256)

        def weight_rows(i, carry):
            rows = pl.ds(pl.multiple_of(i * 256, 256), 256)
            pairs = pl.ds(i * 16, 16)
            normed_part = normed_turned[rows]
            for part, (upper, lower) in enumerate((
                    (dot(normed_part, dq[:, columns]), dot(normed_part, dv[:, columns])),
                    (dot(normed_part, dk[:, columns]), dot(mix_turned[rows], grad[:, columns])))):
                both = jnp.concatenate([upper.reshape(32, 8, 256), lower.reshape(32, 8, 256)], axis=1)
                g[chunk, pairs, :, :, part * WIDTH:part * WIDTH + WIDTH] = both.astype(BF16).reshape(16, 2, 16, 256)
            return carry

        lax.fori_loop(0, 4, weight_rows, 0)
        running.append(run(2 * chunk))
        running.append(run(2 * chunk + 1))
        advance()
    for i in range(4):
        rows = slice(i * 256, i * 256 + 256)
        normed_grad[:, rows] = (dot(dq[...], qkv_weight[rows, 0:1024], NT) + dot(dk[...], qkv_weight[rows, 1024:2048], NT)
                                + dot(dv[...], qkv_weight[rows, 2048:3072], NT))
        advance()

    def window(w, carry):
        rows = pl.ds(pl.multiple_of(w * 128, 128), 128)
        change = normed_grad[rows].astype(BF16).astype(F32)
        centered, inverse = statistics(x_in[rows].astype(F32))
        normed = centered * inverse
        first = jnp.mean(change, axis=-1, keepdims=True)
        second = jnp.mean(change * normed, axis=-1, keepdims=True)
        value = (inverse * (change - first - normed * second)).astype(BF16).astype(F32) + grad[rows].astype(F32)
        natural = dot(order[...], value.astype(BF16), TN)
        framed_out[w] = natural.reshape(2, 8, 8, 1024).astype(BF16)
        return carry

    for i in range(3):
        lax.fori_loop(2 * i, 2 * i + 2, window, 0)
        advance()
    while running:
        advance()
    for copy in started:
        copy.wait_send()


def finish(normed_turned, mix_turned, dq, dk, dv, grad, x, qkv_weight, order):
    streams = 2 * CHUNKS
    vmem = pl.BlockSpec(memory_space=pltpu.VMEM)
    return pl.pallas_call(
        finish_kernel,
        out_shape=(jax.ShapeDtypeStruct((8, 3072), F32), jax.ShapeDtypeStruct((8, 1024), F32),
                   jax.ShapeDtypeStruct((6, 2, 8, 8, 1024), BF16)),
        in_specs=[vmem] * 9,
        out_specs=(vmem, vmem, vmem),
        scratch_shapes=[
            pltpu.VMEM((CHUNKS, 64, 2, 16, LANES), BF16),
            pltpu.VMEM((768, 1024), F32),
            pltpu.VMEM((streams, 64, 16, WIDTH), BF16),
            pltpu.VMEM((streams, 4, 16, 16, WIDTH), BF16),
            pltpu.VMEM((streams, 6, 8, 16, WIDTH), BF16),
            pltpu.VMEM((streams, 4, 4, 16, WIDTH), BF16),
            pltpu.VMEM((streams, 6, 2, 16, WIDTH), BF16),
            pltpu.VMEM((streams, 4, 16, WIDTH), BF16),
            pltpu.VMEM((streams, 3, 16, WIDTH), BF16),
            pltpu.SemaphoreType.DMA((streams, 16)),
            pltpu.SemaphoreType.DMA((streams, 16)),
        ],
        compiler_params=pltpu.CompilerParams(collective_id=0, has_side_effects=True, vmem_limit_bytes=62 * MIB),
        name="finish",
    )(normed_turned, mix_turned, dq, dk, dv, grad, x, qkv_weight, order)


def shifted(block, axis, distance):
    devices = range(lax.axis_size(axis))
    route = [((i - distance) % len(devices), i) for i in devices]
    return lax.ppermute(block, axis, route)


def move_strips(grid_field, strip_width, offset):
    if offset == 1:
        outgoing = grid_field[:, :, -strip_width:]
    else:
        outgoing = grid_field[:, :, :strip_width]
    arrived = shifted(outgoing, "lon", offset)
    if offset == 1:
        middle = jnp.concatenate([arrived, grid_field[:, :, :-strip_width]], axis=2)
        outgoing_rows = middle[:, -strip_width:]
    else:
        middle = jnp.concatenate([grid_field[:, :, strip_width:], arrived], axis=2)
        outgoing_rows = middle[:, :strip_width]
    arrived_rows = shifted(outgoing_rows, "lat", offset)
    if offset == 1:
        return jnp.concatenate([arrived_rows, middle[:, :-strip_width]], axis=1)
    return jnp.concatenate([middle[:, strip_width:], arrived_rows], axis=1)


def to_groups(grid_field):
    return grid_field.reshape(2, 2, 4, 3, 4, 1024).transpose(1, 3, 0, 2, 4, 5).reshape(192, 1024)


def from_groups(groups):
    return groups.reshape(2, 3, 2, 4, 4, 1024).transpose(2, 0, 3, 1, 4, 5).reshape(2, 8, 12, 1024)


def shards(tokens, qkv_weight, out_weight, merge_weight, merged_grad):
    framed = move_strips(tokens, SHIFT, 1)
    framed_merged_grad = move_strips(merged_grad, SHIFT // 2, 1)
    order = jnp.asarray(window_order(), BF16)
    x, normed, normed_turned = prepare(framed, order)
    q, k, v, p, mixture, mix_turned = attend(normed, qkv_weight)
    merged_groups, grad, mixture_grad = merge_both(x, mixture, to_groups(framed_merged_grad), out_weight, merge_weight)
    merged = move_strips(from_groups(merged_groups), SHIFT // 2, -1)
    dq, dk, dv = attend_back(q, k, v, p, mixture, mixture_grad)
    qkv_weight_grad, out_weight_grad, framed_grad = finish(
        normed_turned, mix_turned, dq, dk, dv, grad, x, qkv_weight, order)
    framed_grad = framed_grad.reshape(2, 3, 2, 8, 8, 1024).transpose(2, 0, 3, 1, 4, 5).reshape(2, 16, 24, 1024)
    tokens_grad = move_strips(framed_grad, SHIFT, -1)
    return (merged, tokens_grad, qkv_weight_grad, out_weight_grad)


def solution(mesh):
    in_specs = (P(None, "lat", "lon", None), P(), P(), P(), P(None, "lat", "lon", None))
    out_specs = (
        P(None, "lat", "lon", None),
        P(None, "lat", "lon", None),
        P(("lat", "lon"), None),
        P(("lat", "lon"), None),
    )
    return jax.shard_map(shards, mesh=mesh, in_specs=in_specs, out_specs=out_specs, check_vma=False)
```

```python
import jax
import jax.numpy as jnp
import numpy as np
from jax import lax
from jax.experimental import pallas as pl
from jax.experimental.pallas import tpu as pltpu
from jax.sharding import PartitionSpec as P

SHIFT = 4
CHUNKS = 4
LANES = 512
WIDTH = 256
MESH = pl.DeviceIdType.MESH
F32, BF16 = jnp.float32, jnp.bfloat16
epsilon = 1e-05
SCALE = 32 ** -0.5
MIB = 1024 * 1024
NT = (((1,), (1,)), ((), ()))
TN = (((0,), (0,)), ((), ()))


def params(limit=60):
    return pltpu.CompilerParams(vmem_limit_bytes=limit * MIB)


def dot(left, right, dims=(((1,), (0,)), ((), ()))):
    return lax.dot_general(left, right, dims, preferred_element_type=F32)


def picks(index):
    return (index[:, None] == np.arange(len(index))[None, :]).astype(np.float32)


def window_order():
    t = np.arange(128)
    quarter, level, a, b = t // 32, t // 16 % 2, t // 4 % 4, t % 4
    return picks((level * 8 + 2 * a + quarter % 2) * 8 + 2 * b + quarter // 2)


def orders():
    n = np.arange(128)
    level, i, j = n // 64, n // 8 % 8, n % 8
    to_natural = picks((((i // 4) * 2 + j // 4) * 2 + level) * 16 + (i % 4) * 4 + j % 4)
    to_quarters = window_order() @ to_natural
    n = np.arange(192)
    level, i, j = n // 96, n // 12 % 8, n % 12
    merged_natural = picks((((i // 2) * 6 + j // 2) * 2 + level) * 4 + (i % 2) * 2 + j % 2)
    window, level, a, b = n // 32, n // 16 % 2, n // 4 % 4, n % 4
    row, column = 2 * (window // 3) + a // 2, 2 * (window % 3) + b // 2
    merged_windows = picks(((row * 6 + column) * 2 + level) * 4 + (a % 2) * 2 + b % 2)
    return tuple(jnp.asarray(order, BF16) for order in (to_natural, to_quarters, merged_natural, merged_windows))


def statistics(values):
    center = jnp.mean(values, axis=-1, keepdims=True)
    shifted_values = values - center
    spread = jnp.mean(jnp.square(shifted_values), axis=-1, keepdims=True)
    return shifted_values, lax.rsqrt(spread + epsilon)


def prepare_kernel(framed, order, x_out, normed_out, normed_turned):
    natural = framed[...].astype(F32).reshape(128, 1024).astype(BF16)
    values = dot(order[...], natural)
    x_out[...] = values.astype(BF16)
    centered, inverse = statistics(values)
    normed = centered * inverse
    normed_out[...] = normed.astype(BF16)
    normed_turned[...] = normed.T.astype(BF16)


def prepare(framed, order):
    return pl.pallas_call(
        prepare_kernel,
        grid=(6,),
        out_shape=(jax.ShapeDtypeStruct((768, 1024), BF16), jax.ShapeDtypeStruct((768, 1024), BF16),
                   jax.ShapeDtypeStruct((1024, 768), BF16)),
        in_specs=[pl.BlockSpec((2, 8, 8, 1024), lambda w: (0, w // 3, w % 3, 0)),
                  pl.BlockSpec((128, 128), lambda w: (0, 0))],
        out_specs=(pl.BlockSpec((128, 1024), lambda w: (w, 0)), pl.BlockSpec((128, 1024), lambda w: (w, 0)),
                   pl.BlockSpec((1024, 128), lambda w: (0, w))),
        compiler_params=params(), name="prepare",
    )(framed, order)


def place():
    lat, lon = lax.axis_index("lat"), lax.axis_index("lon")
    return (lat // 4) * 2 + (lon // 2) % 2, lon // 4, lat % 4, lon % 2


def device_at(x, y, z, core):
    return ((x // 2) * 4 + z, y * 4 + (x % 2) * 2 + core)


def neighbours(step):
    lat, lon = lax.axis_index("lat"), lax.axis_index("lon")
    lat_there, lon_there = (lat + step + 8) % 8, (lon + step + 16) % 16
    return (lat_there, lon), (lat, lon_there), (lat_there, lon_there)


def greet(receive_from, send_to):
    barrier = pltpu.get_barrier_semaphore()
    for device in receive_from:
        pl.semaphore_signal(barrier, inc=1, device_id=device, device_id_type=MESH)
    pl.semaphore_wait(barrier, len(send_to))


def remote(source, target, send, recv, device):
    return pltpu.make_async_remote_copy(src_ref=source, dst_ref=target, send_sem=send, recv_sem=recv,
                                        device_id=device, device_id_type=MESH)


def frame_copies(units, first, last, send, recv, base, devices):
    row, column, corner = devices
    return [remote(units.at[first[0], 1:6], units.at[last[0], 1:6], send.at[base], recv.at[base], row),
            remote(units.at[1:4, first[1]], units.at[1:4, last[1]], send.at[base + 1], recv.at[base + 1], column),
            remote(units.at[first[0], first[1]], units.at[last[0], last[1]], send.at[base + 2], recv.at[base + 2], corner)]


def wide_masks():
    lane = lax.broadcasted_iota(jnp.int32, (128, 256), 1)
    return [lane % 128 // 32 == head for head in range(4)], [lane // 128 == group for group in range(2)]


def stack(values, masks):
    zero = jnp.zeros_like(values)
    return jnp.concatenate([jnp.where(mask, values, zero) for mask in masks], axis=0)


def select(stacked, masks):
    rows = [stacked[128 * head:128 * head + 128] for head in range(4)]
    return jnp.where(masks[0], rows[0], jnp.where(masks[1], rows[1], jnp.where(masks[2], rows[2], rows[3])))


def other_region(rows, columns, edge):
    row = (lax.broadcasted_iota(jnp.int32, (rows, 1), 0) // 4 % 4 < 2) & edge
    column = (lax.broadcasted_iota(jnp.int32, (1, columns), 1) // 4 % 4 < 2) & edge
    return row.astype(jnp.int32) != column.astype(jnp.int32)


def back_kernel(q_hbm, k_hbm, v_hbm, mix_hbm, mix_grad_hbm, normed_hbm, mix_turned_hbm, grad_hbm, x_hbm, weight_hbm,
                merged_in, to_natural, to_quarters, merged_natural, merged_windows,
                qkv_out, out_out, tokens_out, merged_out,
                q, k, v, mix, mix_grad, normed_turned, mix_turned, grad, x_in, qkv_weight,
                dq, dk, dv, g, normed_grad, units, merged_units,
                from_core, acc_a, in_a, acc_b, in_b, acc_c, in_c, load, send, recv, strip_send, strip_recv):
    loads = {}

    def fetch(name, index, source, target):
        loads[name] = pltpu.make_async_copy(source, target, load.at[index])
        loads[name].start()

    wide = ((q_hbm, q), (k_hbm, k), (v_hbm, v), (mix_hbm, mix), (mix_grad_hbm, mix_grad))
    for chunk in range(CHUNKS):
        columns = pl.ds(chunk * 256, 256)
        for i, (source, target) in enumerate(wide):
            fetch((chunk, i), chunk * 5 + i, source.at[:, columns], target.at[:, columns])
        if chunk == 0:
            fetch("normed", 20, normed_hbm, normed_turned)
            fetch("mix", 21, mix_turned_hbm, mix_turned)
            fetch("grad", 22, grad_hbm, grad)
    fetch("weight", 23, weight_hbm, qkv_weight)
    fetch("x", 24, x_hbm, x_in)

    x, y, z, core = place()
    here = (x, y, z)

    def moved(axis, step):
        there = list(here)
        there[axis] = (here[axis] + step) % 4
        return device_at(there[0], there[1], there[2], core)

    sibling = device_at(x, y, z, 1 - core)
    ring = [sibling] + [moved(axis, step) for axis in range(3) for step in (1, 2, 3)]
    before, after = neighbours(-1), neighbours(1)
    greet(ring + list(after), ring + list(before))

    started = []

    def push(copy):
        copy.start()
        started.append(copy)
        return copy

    units_in = dot(merged_windows[...], merged_in[...], TN).reshape(4, 6, 8, 1024)
    for i in range(4):
        merged_units[i, 0:6] = units_in[i]
    merged_copies = frame_copies(merged_units, (0, 0), (4, 6), strip_send, strip_recv, 0, before)
    for copy in merged_copies:
        push(copy)

    def run(stream):
        chunk, part = stream // 2, stream % 2
        slot = chunk % 2
        lanes = pl.ds(part * WIDTH, WIDTH)
        order = [(stream + i) % 3 for i in range(3)]
        mine = [here[axis] for axis in order]
        copy = push(remote(g.at[slot, :, 1 - core, :, lanes], from_core.at[stream],
                           send.at[stream, 0], recv.at[stream, 0], sibling))
        yield
        copy.wait_recv()

        def add_block(index, carry):
            a, b = index // 4, index % 4
            for c in range(4):
                at = [None, None, None]
                for axis, value in zip(order, (a, b, c)):
                    at[axis] = value
                row = ((at[0] // 2) * 4 + at[2]) * 8 + at[1] * 2 + at[0] % 2
                total = g[slot, row, core, :, lanes].astype(F32) + from_core[stream, row].astype(F32)
                acc_a[stream, a, b * 4 + c] = total.astype(BF16)
            return carry

        lax.fori_loop(0, 16, add_block, 0)
        for level, (acc, arrived) in enumerate(((acc_a, in_a), (acc_b, in_b), (acc_c, in_c))):
            axis, p = order[level], mine[level]
            copies = [push(remote(acc.at[stream, (p + i + 1) % 4], arrived.at[stream, i],
                                  send.at[stream, 1 + level * 3 + i], recv.at[stream, 1 + level * 3 + i],
                                  moved(axis, i + 1))) for i in range(3)]
            yield
            for copy in copies:
                copy.wait_recv()
            total = acc[stream, p].astype(F32)
            for i in range(3):
                total = total + arrived[stream, i].astype(F32)
            if level == 0:
                for i in range(4):
                    acc_b[stream, i] = total[i * 4:i * 4 + 4].astype(BF16)
            elif level == 1:
                for i in range(4):
                    acc_c[stream, i] = total[i].astype(BF16)
        columns = WIDTH * chunk
        if part == 0:
            qkv_out[:, columns:columns + WIDTH] = total[:8]
            qkv_out[:, 2048 + columns:2048 + columns + WIDTH] = total[8:]
        else:
            qkv_out[:, 1024 + columns:1024 + columns + WIDTH] = total[:8]
            out_out[:, columns:columns + WIDTH] = total[8:]

    running = []

    def advance():
        for job in list(running):
            try:
                next(job)
            except StopIteration:
                running.remove(job)

    head_mask, group_mask = wide_masks()
    row8 = lax.broadcasted_iota(jnp.int32, (8, 256), 0)
    lane8 = lax.broadcasted_iota(jnp.int32, (8, 256), 1) // 32
    own_head = jnp.where(lane8 == row8, 1.0, 0.0).astype(BF16)
    edge = lax.axis_index("lat") == 0
    first_send = {}
    for chunk in range(CHUNKS):
        columns = slice(chunk * 256, chunk * 256 + 256)
        for i in range(5):
            loads[(chunk, i)].wait()

        def window_back(wa):
            for wb in range(3):
                rows = pl.ds(pl.multiple_of(wa * 384 + wb * 128, 128), 128)
                queries, keys, values = q[rows, columns], k[rows, columns], v[rows, columns]
                out_grad = mix_grad[rows, columns]
                product = (out_grad.astype(F32) * mix[rows, columns].astype(F32)).astype(BF16)
                spread_queries, spread_grads = stack(queries, group_mask), stack(out_grad, group_mask)
                weights = jnp.exp(dot(stack(keys, head_mask), spread_queries, NT) * SCALE)
                weights = jnp.where(other_region(512, 256, edge & (wa == 0)), 0.0, weights)
                change = dot(stack(values, head_mask), spread_grads, NT)
                means = dot(own_head, product, NT)
                attention, scores_grad = [], []
                for head in range(4):
                    part = weights[128 * head:128 * head + 128]
                    part = part * (1.0 / jnp.sum(part, axis=0, keepdims=True))
                    mean = jnp.concatenate([means[head:head + 1], means[4 + head:5 + head]], axis=1)
                    attention.append(part.astype(BF16))
                    scores_grad.append((part * (change[128 * head:128 * head + 128] - mean)).astype(BF16))
                dv[rows, columns] = select(dot(jnp.concatenate(attention, axis=0), spread_grads), head_mask).astype(BF16)
                dk[rows, columns] = (select(dot(jnp.concatenate(scores_grad, axis=0), spread_queries), head_mask)
                                     * SCALE).astype(BF16)
                turned = keys.T
                pieces = []
                for group in range(2):
                    for head in range(4):
                        low = group * 128 + head * 32
                        pieces.append(dot(turned[low:low + 32], scores_grad[head][:, group * 128:group * 128 + 128]))
                dq[rows, columns] = (jnp.concatenate(pieces, axis=0).T * SCALE).astype(BF16)

        pl.loop(0, 2)(window_back)
        if chunk == 0:
            for name in ("normed", "mix", "grad"):
                loads[name].wait()
        slot = chunk % 2
        if chunk >= 2:
            for copy in first_send[chunk - 2]:
                copy.wait_send()

        def weight_rows(i, carry):
            rows = pl.ds(pl.multiple_of(i * 256, 256), 256)
            pairs = pl.ds(i * 16, 16)
            normed_part = normed_turned[rows]
            for part, (upper, lower) in enumerate((
                    (dot(normed_part, dq[:, columns]), dot(normed_part, dv[:, columns])),
                    (dot(normed_part, dk[:, columns]), dot(mix_turned[rows], grad[:, columns])))):
                both = jnp.concatenate([upper.reshape(32, 8, 256), lower.reshape(32, 8, 256)], axis=1)
                g[slot, pairs, :, :, part * WIDTH:part * WIDTH + WIDTH] = both.astype(BF16).reshape(16, 2, 16, 256)
            return carry

        lax.fori_loop(0, 4, weight_rows, 0)
        advance()
        for part in range(2):
            job = run(2 * chunk + part)
            next(job)
            running.append(job)
        first_send[chunk] = started[-2:]
        del started[-2:]
    loads["weight"].wait()
    loads["x"].wait()

    def finish_window(w):
        rows = pl.ds(w * 128, 128)
        change = normed_grad[rows].astype(BF16).astype(F32)
        centered, inverse = statistics(x_in[rows].astype(F32))
        normed = centered * inverse
        first = jnp.mean(change, axis=-1, keepdims=True)
        second = jnp.mean(change * normed, axis=-1, keepdims=True)
        value = (inverse * (change - first - normed * second)).astype(BF16).astype(F32) + grad[rows].astype(F32)
        quarters = dot(to_quarters[...], value.astype(BF16), TN).astype(BF16).reshape(4, 32, 1024)
        wa, wb = w // 3, w % 3
        for u in range(2):
            for side in range(2):
                units[2 * wa + u, 2 * wb + side] = quarters[2 * u + side]

    strips = frame_copies(units, (0, 0), (4, 6), strip_send, strip_recv, 3, before)
    for half in range(2):
        tokens = slice(half * 384, half * 384 + 384)
        for i in range(4):
            rows = slice(i * 256, i * 256 + 256)
            normed_grad[tokens, rows] = (dot(dq[tokens], qkv_weight[rows, 0:1024], NT)
                                         + dot(dk[tokens], qkv_weight[rows, 1024:2048], NT)
                                         + dot(dv[tokens], qkv_weight[rows, 2048:3072], NT))
            if i % 2 == 1 and (half, i) != (1, 1):
                advance()
        for wb in range(3):
            finish_window(half * 3 + wb)
            if half == 1 and wb == 0:
                push(strips[1])
        if half == 0:
            push(strips[0])
            push(strips[2])
    for copy in merged_copies:
        copy.wait_recv()
    merged_natural_units = jnp.concatenate([merged_units[i, 1:7].reshape(48, 1024) for i in range(1, 5)], axis=0)
    merged_out[...] = dot(merged_natural[...], merged_natural_units.astype(BF16)).astype(BF16)
    advance()
    for copy in strips:
        copy.wait_recv()
    for m in range(2):
        blocks = []
        for n in range(3):
            parts = [units[2 * m + 1 + u, 2 * n + 1 + side] for u in range(2) for side in range(2)]
            natural = dot(to_natural[...], jnp.concatenate(parts, axis=0)).reshape(2, 8, 8, 1024)
            blocks.append(natural)
        tokens_out[:, 8 * m:8 * m + 8] = jnp.concatenate(blocks, axis=2).astype(BF16)
    while running:
        advance()
    for chunk in range(2, CHUNKS):
        for copy in first_send[chunk]:
            copy.wait_send()
    for copy in started:
        copy.wait_send()


def back(q, k, v, mix, mix_grad, normed_turned, mix_turned, grad, x, qkv_weight, merged_groups):
    streams = 2 * CHUNKS
    vmem, anywhere = pl.BlockSpec(memory_space=pltpu.VMEM), pl.BlockSpec(memory_space=pl.ANY)
    tokens = pltpu.VMEM((768, 1024), BF16)
    turned = pltpu.VMEM((1024, 768), BF16)
    return pl.pallas_call(
        back_kernel,
        out_shape=(jax.ShapeDtypeStruct((8, 3072), F32), jax.ShapeDtypeStruct((8, 1024), F32),
                   jax.ShapeDtypeStruct((2, 16, 24, 1024), BF16), jax.ShapeDtypeStruct((192, 1024), BF16)),
        in_specs=[anywhere] * 10 + [vmem] * 5,
        out_specs=(vmem, vmem, vmem, vmem),
        scratch_shapes=[
            tokens, tokens, tokens, tokens, tokens, turned, turned, tokens, tokens, pltpu.VMEM((1024, 3072), BF16),
            tokens, tokens, tokens,
            pltpu.VMEM((2, 64, 2, 16, LANES), BF16),
            pltpu.VMEM((768, 1024), F32),
            pltpu.VMEM((5, 7, 32, 1024), BF16),
            pltpu.VMEM((5, 7, 8, 1024), F32),
            pltpu.VMEM((streams, 64, 16, WIDTH), BF16),
            pltpu.VMEM((streams, 4, 16, 16, WIDTH), BF16),
            pltpu.VMEM((streams, 3, 16, 16, WIDTH), BF16),
            pltpu.VMEM((streams, 4, 4, 16, WIDTH), BF16),
            pltpu.VMEM((streams, 3, 4, 16, WIDTH), BF16),
            pltpu.VMEM((streams, 4, 16, WIDTH), BF16),
            pltpu.VMEM((streams, 3, 16, WIDTH), BF16),
            pltpu.SemaphoreType.DMA((25,)),
            pltpu.SemaphoreType.DMA((streams, 10)),
            pltpu.SemaphoreType.DMA((streams, 10)),
            pltpu.SemaphoreType.DMA((6,)),
            pltpu.SemaphoreType.DMA((6,)),
        ],
        compiler_params=pltpu.CompilerParams(collective_id=0, has_side_effects=True, vmem_limit_bytes=62 * MIB),
        name="back",
    )(q, k, v, mix, mix_grad, normed_turned, mix_turned, grad, x, qkv_weight, merged_groups, *orders()[:2], *orders()[2:])


def attend_kernel(normed, wq, wk, wv, q_out, k_out, v_out, mix_out, mix_turned):
    for out, weight in ((q_out, wq), (k_out, wk), (v_out, wv)):
        out[...] = dot(normed[...], weight[...]).astype(BF16)
    lane = lax.broadcasted_iota(jnp.int32, (128, 128), 1)
    masks = [lane // 32 == head for head in range(4)]
    edge = lax.axis_index("lat") == 0
    for w in range(6):
        rows = pl.ds(w * 128, 128)
        for group in range(2):
            lanes = pl.ds(group * 128, 128)
            scores = dot(q_out[rows, lanes], stack(k_out[rows, lanes], masks), NT)
            weights = jnp.exp(scores * SCALE)
            if w < 3:
                weights = jnp.where(other_region(128, 512, edge), 0.0, weights)
            pieces = []
            for head in range(4):
                piece = weights[:, head * 128:head * 128 + 128]
                pieces.append((piece * (1.0 / jnp.sum(piece, axis=-1, keepdims=True))).astype(BF16))
            mixture = select(dot(jnp.concatenate(pieces, axis=0), v_out[rows, lanes]), masks)
            mix_out[rows, lanes] = mixture.astype(BF16)
            mix_turned[lanes, rows] = mixture.T.astype(BF16)


def attend(normed, qkv_weight):
    tokens = jax.ShapeDtypeStruct((768, 1024), BF16)
    block = pl.BlockSpec((768, 256), lambda c: (0, c))
    weight = lambda third: pl.BlockSpec((1024, 256), lambda c: (0, third * 4 + c))
    return pl.pallas_call(
        attend_kernel,
        grid=(4,),
        out_shape=(tokens, tokens, tokens, tokens, jax.ShapeDtypeStruct((1024, 768), BF16)),
        in_specs=[pl.BlockSpec((768, 1024), lambda c: (0, 0)), weight(0), weight(1), weight(2)],
        out_specs=(block, block, block, block, pl.BlockSpec((256, 768), lambda c: (c, 0))),
        compiler_params=params(), name="attend",
    )(normed, qkv_weight, qkv_weight, qkv_weight)


def merge_kernel(x, mixture, merged_grad, out_weight, merge_weight, merged_out, grad_out, mixture_grad,
                 normed, total, normed_grad):
    step = pl.program_id(0)

    @pl.when(step == 0)
    def _():
        for w in range(6):
            rows = pl.ds(w * 128, 128)
            values = x[rows].astype(F32) + dot(mixture[rows], out_weight[...])
            values = values.astype(BF16).astype(F32)
            quarters = [values[32 * j:32 * j + 32] for j in range(4)]
            center = sum(jnp.sum(part, axis=-1, keepdims=True) for part in quarters) * (1 / 4096)
            quarters = [part - center for part in quarters]
            spread = sum(jnp.sum(jnp.square(part), axis=-1, keepdims=True) for part in quarters) * (1 / 4096)
            inverse = lax.rsqrt(spread + epsilon)
            for j in range(4):
                normed[j, pl.ds(w * 32, 32)] = quarters[j] * inverse
            total[1, pl.ds(w * 32, 32)] = jnp.broadcast_to(inverse, (32, 1024))
        total[0] = jnp.zeros((192, 1024), F32)

    total[0] += dot(normed[step].astype(BF16), merge_weight[...])
    normed_grad[step] = dot(merged_grad[...], merge_weight[...], NT).astype(BF16).astype(F32)

    @pl.when(step == 3)
    def _():
        merged_out[...] = total[0].astype(BF16)
        for w in range(6):
            part = pl.ds(w * 32, 32)
            first = sum(jnp.sum(normed_grad[j, part], axis=-1, keepdims=True) for j in range(4)) * (1 / 4096)
            second = sum(jnp.sum(normed_grad[j, part] * normed[j, part], axis=-1, keepdims=True)
                         for j in range(4)) * (1 / 4096)
            inverse = total[1, part]
            for j in range(4):
                value = inverse * (normed_grad[j, part] - first - normed[j, part] * second)
                grad_out[pl.ds(w * 128 + j * 32, 32)] = value.astype(BF16)
        mixture_grad[...] = dot(grad_out[...], out_weight[...], NT).astype(BF16)


def merge_both(x, mixture, merged_grad, out_weight, merge_weight):
    whole = lambda rows: pl.BlockSpec((rows, 1024), lambda j: (0, 0))
    tokens = jax.ShapeDtypeStruct((768, 1024), BF16)
    return pl.pallas_call(
        merge_kernel,
        grid=(4,),
        out_shape=(jax.ShapeDtypeStruct((192, 1024), BF16), tokens, tokens),
        in_specs=[whole(768), whole(768), whole(192), whole(1024), pl.BlockSpec((1024, 1024), lambda j: (j, 0))],
        out_specs=(whole(192), whole(768), whole(768)),
        scratch_shapes=[pltpu.VMEM((4, 192, 1024), F32), pltpu.VMEM((2, 192, 1024), F32),
                        pltpu.VMEM((4, 192, 1024), F32)],
        compiler_params=params(), name="merge_both",
    )(x, mixture, merged_grad, out_weight, merge_weight)


def shifted(block, axis, distance):
    devices = range(lax.axis_size(axis))
    route = [((i - distance) % len(devices), i) for i in devices]
    return lax.ppermute(block, axis, route)


def move_strips(grid_field, strip_width, offset):
    if offset == 1:
        outgoing = grid_field[:, :, -strip_width:]
    else:
        outgoing = grid_field[:, :, :strip_width]
    arrived = shifted(outgoing, "lon", offset)
    if offset == 1:
        middle = jnp.concatenate([arrived, grid_field[:, :, :-strip_width]], axis=2)
        outgoing_rows = middle[:, -strip_width:]
    else:
        middle = jnp.concatenate([grid_field[:, :, strip_width:], arrived], axis=2)
        outgoing_rows = middle[:, :strip_width]
    arrived_rows = shifted(outgoing_rows, "lat", offset)
    if offset == 1:
        return jnp.concatenate([arrived_rows, middle[:, :-strip_width]], axis=1)
    return jnp.concatenate([middle[:, strip_width:], arrived_rows], axis=1)


def to_groups(grid_field):
    return grid_field.reshape(2, 2, 4, 3, 4, 1024).transpose(1, 3, 0, 2, 4, 5).reshape(192, 1024)


def shards(tokens, qkv_weight, out_weight, merge_weight, merged_grad):
    framed = move_strips(tokens, SHIFT, 1)
    framed_merged_grad = move_strips(merged_grad, SHIFT // 2, 1)
    x, normed, normed_turned = prepare(framed, jnp.asarray(window_order(), BF16))
    q, k, v, mixture, mix_turned = attend(normed, qkv_weight)
    merged_groups, grad, mixture_grad = merge_both(x, mixture, to_groups(framed_merged_grad), out_weight, merge_weight)
    qkv_weight_grad, out_weight_grad, tokens_grad, merged = back(
        q, k, v, mixture, mixture_grad, normed_turned, mix_turned, grad, x, qkv_weight, merged_groups)
    return (merged.reshape(2, 8, 12, 1024), tokens_grad, qkv_weight_grad, out_weight_grad)


def solution(mesh):
    in_specs = (P(None, "lat", "lon", None), P(), P(), P(), P(None, "lat", "lon", None))
    out_specs = (
        P(None, "lat", "lon", None),
        P(None, "lat", "lon", None),
        P(("lat", "lon"), None),
        P(("lat", "lon"), None),
    )
    return jax.shard_map(shards, mesh=mesh, in_specs=in_specs, out_specs=out_specs, check_vma=False)
```

```python
import jax
import jax.numpy as jnp
import numpy as np
from jax import lax
from jax.experimental import pallas as pl
from jax.experimental.pallas import tpu as pltpu
from jax.sharding import PartitionSpec as P

CHUNKS = 4
MESH = pl.DeviceIdType.MESH
F32, BF16 = jnp.float32, jnp.bfloat16
epsilon = 1e-05
SCALE = 32 ** -0.5
MIB = 1024 * 1024
NT = (((1,), (1,)), ((), ()))
TN = (((0,), (0,)), ((), ()))


def params(limit=60):
    return pltpu.CompilerParams(vmem_limit_bytes=limit * MIB)


def dot(left, right, dims=(((1,), (0,)), ((), ()))):
    return lax.dot_general(left, right, dims, preferred_element_type=F32)


def picks(index):
    return (index[:, None] == np.arange(len(index))[None, :]).astype(np.float32)


def window_order():
    t = np.arange(128)
    quarter, level, a, b = t // 32, t // 16 % 2, t // 4 % 4, t % 4
    return picks((level * 8 + 2 * a + quarter % 2) * 8 + 2 * b + quarter // 2)


def orders():
    n = np.arange(128)
    level, i, j = n // 64, n // 8 % 8, n % 8
    to_natural = picks((((i // 4) * 2 + j // 4) * 2 + level) * 16 + (i % 4) * 4 + j % 4)
    to_quarters = window_order() @ to_natural
    n = np.arange(192)
    level, i, j = n // 96, n // 12 % 8, n % 12
    merged_natural = picks((((i // 2) * 6 + j // 2) * 2 + level) * 4 + (i % 2) * 2 + j % 2)
    window, level, a, b = n // 32, n // 16 % 2, n // 4 % 4, n % 4
    row, column = 2 * (window // 3) + a // 2, 2 * (window % 3) + b // 2
    merged_windows = picks(((row * 6 + column) * 2 + level) * 4 + (a % 2) * 2 + b % 2)
    return tuple(jnp.asarray(order, BF16) for order in (to_natural, to_quarters, merged_natural, merged_windows))


def statistics(values):
    center = jnp.mean(values, axis=-1, keepdims=True)
    shifted_values = values - center
    spread = jnp.mean(jnp.square(shifted_values), axis=-1, keepdims=True)
    return shifted_values, lax.rsqrt(spread + epsilon)


def place():
    lat, lon = lax.axis_index("lat"), lax.axis_index("lon")
    return (lat // 4) * 2 + (lon // 2) % 2, lon // 4, lat % 4, lon % 2


def device_at(x, y, z, core):
    return ((x // 2) * 4 + z, y * 4 + (x % 2) * 2 + core)


def neighbours(step):
    lat, lon = lax.axis_index("lat"), lax.axis_index("lon")
    lat_there, lon_there = (lat + step + 8) % 8, (lon + step + 16) % 16
    return (lat_there, lon), (lat, lon_there), (lat_there, lon_there)


def greet(receive_from, send_to):
    barrier = pltpu.get_barrier_semaphore()
    for device in receive_from:
        pl.semaphore_signal(barrier, inc=1, device_id=device, device_id_type=MESH)
    pl.semaphore_wait(barrier, len(send_to))


def remote(source, target, send, recv, device):
    return pltpu.make_async_remote_copy(src_ref=source, dst_ref=target, send_sem=send, recv_sem=recv,
                                        device_id=device, device_id_type=MESH)


def frame_copies(units, first, last, send, recv, base, devices):
    row, column, corner = devices
    return [remote(units.at[first[0], 1:6], units.at[last[0], 1:6], send.at[base], recv.at[base], row),
            remote(units.at[1:4, first[1]], units.at[1:4, last[1]], send.at[base + 1], recv.at[base + 1], column),
            remote(units.at[first[0], first[1]], units.at[last[0], last[1]], send.at[base + 2], recv.at[base + 2], corner)]


def wide_masks():
    lane = lax.broadcasted_iota(jnp.int32, (128, 256), 1)
    return [lane % 128 // 32 == head for head in range(4)], [lane // 128 == group for group in range(2)]


def stack(values, masks):
    zero = jnp.zeros_like(values)
    return jnp.concatenate([jnp.where(mask, values, zero) for mask in masks], axis=0)


def select(stacked, masks):
    rows = [stacked[128 * head:128 * head + 128] for head in range(4)]
    return jnp.where(masks[0], rows[0], jnp.where(masks[1], rows[1], jnp.where(masks[2], rows[2], rows[3])))


def other_region(rows, columns, edge):
    row = (lax.broadcasted_iota(jnp.int32, (rows, 1), 0) // 4 % 4 < 2) & edge
    column = (lax.broadcasted_iota(jnp.int32, (1, columns), 1) // 4 % 4 < 2) & edge
    return row.astype(jnp.int32) != column.astype(jnp.int32)


def back_kernel(q_hbm, k_hbm, v_hbm, mix_hbm, mix_grad_hbm, normed_hbm, mix_turned_hbm, grad_hbm, x_hbm, weight_hbm,
                merged_in, to_natural, to_quarters, merged_natural, merged_windows,
                qkv_out, out_out, tokens_out, merged_out,
                q, k, v, mix, mix_grad, normed_turned, mix_turned, grad, x_in, qkv_weight,
                dq, dk, dv, g, normed_grad, units, merged_units,
                from_core, acc_a, in_a, acc_b, in_b, acc_c, in_c, load, send, recv, strip_send, strip_recv):
    loads = {}

    def fetch(name, index, source, target):
        loads[name] = pltpu.make_async_copy(source, target, load.at[index])
        loads[name].start()

    fetch("mix", 21, mix_turned_hbm, mix_turned)
    fetch("grad", 22, grad_hbm, grad)
    fetch("normed", 20, normed_hbm, normed_turned)
    wide = ((q_hbm, q), (k_hbm, k), (v_hbm, v), (mix_hbm, mix), (mix_grad_hbm, mix_grad))
    for chunk in range(CHUNKS):
        columns = pl.ds(chunk * 256, 256)
        for i, (source, target) in enumerate(wide):
            fetch((chunk, i), chunk * 5 + i, source.at[:, columns], target.at[:, columns])
    fetch("weight", 23, weight_hbm, qkv_weight)
    fetch("x", 24, x_hbm, x_in)

    x, y, z, core = place()
    here = (x, y, z)

    def moved(axis, step):
        there = list(here)
        there[axis] = (here[axis] + step) % 4
        return device_at(there[0], there[1], there[2], core)

    sibling = device_at(x, y, z, 1 - core)
    ring = [sibling] + [moved(axis, step) for axis in range(3) for step in (1, 2, 3)]
    before, after = neighbours(-1), neighbours(1)
    greet(ring + list(after), ring + list(before))

    started = []
    first_send = {}

    def push(copy):
        copy.start()
        started.append(copy)
        return copy

    units_in = dot(merged_windows[...], merged_in[...], TN).reshape(4, 6, 8, 1024)
    for i in range(4):
        merged_units[i, 0:6] = units_in[i]
    merged_copies = frame_copies(merged_units, (0, 0), (4, 6), strip_send, strip_recv, 0, before)
    for copy in merged_copies:
        push(copy)

    def run(kind, chunk):
        stream = kind * CHUNKS + chunk
        slot = 6 + chunk if kind == 3 else chunk % 2 * 3 + kind
        order = [(kind + chunk + i) % 3 for i in range(3)]
        mine = [here[axis] for axis in order]
        copy = remote(g.at[slot, :, 1 - core], from_core.at[stream], send.at[stream, 0], recv.at[stream, 0], sibling)
        copy.start()
        first_send[(kind, chunk)] = copy
        yield
        copy.wait_recv()

        def add_block(index, carry):
            a, b = index // 4, index % 4
            for c in range(4):
                at = [None, None, None]
                for axis, value in zip(order, (a, b, c)):
                    at[axis] = value
                row = ((at[0] // 2) * 4 + at[2]) * 8 + at[1] * 2 + at[0] % 2
                total = g[slot, row, core].astype(F32) + from_core[stream, row].astype(F32)
                acc_a[stream, a, b * 4 + c] = total.astype(BF16)
            return carry

        lax.fori_loop(0, 16, add_block, 0)
        for level, (acc, arrived) in enumerate(((acc_a, in_a), (acc_b, in_b), (acc_c, in_c))):
            axis, p = order[level], mine[level]
            copies = [push(remote(acc.at[stream, (p + i + 1) % 4], arrived.at[stream, i],
                                  send.at[stream, 1 + level * 3 + i], recv.at[stream, 1 + level * 3 + i],
                                  moved(axis, i + 1))) for i in range(3)]
            yield
            for copy in copies:
                copy.wait_recv()
            total = acc[stream, p].astype(F32)
            for i in range(3):
                total = total + arrived[stream, i].astype(F32)
            if level == 0:
                for i in range(4):
                    acc_b[stream, i] = total[i * 4:i * 4 + 4].astype(BF16)
            elif level == 1:
                for i in range(4):
                    acc_c[stream, i] = total[i].astype(BF16)
        target, base = (out_out, chunk * 256) if kind == 3 else (qkv_out, kind * 1024 + chunk * 256)
        target[:, base:base + 128] = total[:8]
        target[:, base + 128:base + 256] = total[8:]

    running = []

    def advance():
        for job in list(running):
            try:
                next(job)
            except StopIteration:
                running.remove(job)

    head_mask, group_mask = wide_masks()
    row8 = lax.broadcasted_iota(jnp.int32, (8, 256), 0)
    lane8 = lax.broadcasted_iota(jnp.int32, (8, 256), 1) // 32
    own_head = jnp.where(lane8 == row8, 1.0, 0.0).astype(BF16)
    edge = lax.axis_index("lat") == 0
    def weight_terms(kinds, chunk):
        def weight_rows(i, carry):
            rows = pl.ds(pl.multiple_of(i * 256, 256), 256)
            pairs = pl.ds(i * 16, 16)
            for kind in kinds:
                left, right = ((normed_turned, dq), (normed_turned, dk), (normed_turned, dv), (mix_turned, grad))[kind]
                terms = dot(left[rows], right[:, chunk * 256:chunk * 256 + 256]).reshape(32, 8, 256)
                both = jnp.concatenate([terms[:, :, :128], terms[:, :, 128:]], axis=1)
                slot = 6 + chunk if kind == 3 else chunk % 2 * 3 + kind
                g[slot, pairs] = both.astype(BF16).reshape(16, 2, 16, 128)
            return carry

        lax.fori_loop(0, 4, weight_rows, 0)
        for kind in kinds:
            job = run(kind, chunk)
            next(job)
            running.append(job)

    for name in ("normed", "mix", "grad"):
        loads[name].wait()
    for chunk in range(CHUNKS):
        weight_terms((3,), chunk)
    for chunk in range(CHUNKS):
        columns = slice(chunk * 256, chunk * 256 + 256)
        for i in range(5):
            loads[(chunk, i)].wait()

        def window_back(wa):
            for wb in range(3):
                rows = pl.ds(pl.multiple_of(wa * 384 + wb * 128, 128), 128)
                queries, keys, values = q[rows, columns], k[rows, columns], v[rows, columns]
                out_grad = mix_grad[rows, columns]
                product = (out_grad.astype(F32) * mix[rows, columns].astype(F32)).astype(BF16)
                spread_queries, spread_grads = stack(queries, group_mask), stack(out_grad, group_mask)
                weights = jnp.exp(dot(stack(keys, head_mask), spread_queries, NT) * SCALE)
                weights = jnp.where(other_region(512, 256, edge & (wa == 0)), 0.0, weights)
                change = dot(stack(values, head_mask), spread_grads, NT)
                means = dot(own_head, product, NT)
                attention, scores_grad = [], []
                for head in range(4):
                    part = weights[128 * head:128 * head + 128]
                    part = part * (1.0 / jnp.sum(part, axis=0, keepdims=True))
                    mean = jnp.concatenate([means[head:head + 1], means[4 + head:5 + head]], axis=1)
                    attention.append(part.astype(BF16))
                    scores_grad.append((part * (change[128 * head:128 * head + 128] - mean)).astype(BF16))
                dv[rows, columns] = select(dot(jnp.concatenate(attention, axis=0), spread_grads), head_mask).astype(BF16)
                dk[rows, columns] = (select(dot(jnp.concatenate(scores_grad, axis=0), spread_queries), head_mask)
                                     * SCALE).astype(BF16)
                turned = keys.T
                pieces = []
                for group in range(2):
                    for head in range(4):
                        low = group * 128 + head * 32
                        pieces.append(dot(turned[low:low + 32], scores_grad[head][:, group * 128:group * 128 + 128]))
                dq[rows, columns] = (jnp.concatenate(pieces, axis=0).T * SCALE).astype(BF16)

        pl.loop(0, 2)(window_back)
        advance()
        if chunk >= 2:
            for kind in range(3):
                first_send.pop((kind, chunk - 2)).wait_send()
        weight_terms((0, 1, 2), chunk)
    loads["weight"].wait()
    loads["x"].wait()

    def finish_window(w):
        rows = pl.ds(w * 128, 128)
        change = normed_grad[rows].astype(BF16).astype(F32)
        centered, inverse = statistics(x_in[rows].astype(F32))
        normed = centered * inverse
        first = jnp.mean(change, axis=-1, keepdims=True)
        second = jnp.mean(change * normed, axis=-1, keepdims=True)
        value = (inverse * (change - first - normed * second)).astype(BF16).astype(F32) + grad[rows].astype(F32)
        quarters = dot(to_quarters[...], value.astype(BF16), TN).astype(BF16).reshape(4, 32, 1024)
        wa, wb = w // 3, w % 3
        for u in range(2):
            for side in range(2):
                units[2 * wa + u, 2 * wb + side] = quarters[2 * u + side]

    strips = frame_copies(units, (0, 0), (4, 6), strip_send, strip_recv, 3, before)
    for half in range(2):
        tokens = slice(half * 384, half * 384 + 384)
        for i in range(4):
            rows = slice(i * 256, i * 256 + 256)
            normed_grad[tokens, rows] = (dot(dq[tokens], qkv_weight[rows, 0:1024], NT)
                                         + dot(dk[tokens], qkv_weight[rows, 1024:2048], NT)
                                         + dot(dv[tokens], qkv_weight[rows, 2048:3072], NT))
            if (half, i) in ((0, 1), (1, 3)):
                advance()
        for wb in range(3):
            finish_window(half * 3 + wb)
            if half == 1 and wb == 0:
                push(strips[1])
        if half == 0:
            push(strips[0])
            push(strips[2])
        advance()
    for copy in merged_copies:
        copy.wait_recv()
    merged_natural_units = jnp.concatenate([merged_units[i, 1:7].reshape(48, 1024) for i in range(1, 5)], axis=0)
    natural = dot(merged_natural[...], merged_natural_units.astype(BF16))
    for i in range(16):
        merged_out[i // 8, i % 8] = natural[12 * i:12 * i + 12].astype(BF16)
    for copy in strips:
        copy.wait_recv()
    for m in range(2):
        blocks = []
        for n in range(3):
            parts = [units[2 * m + 1 + u, 2 * n + 1 + side] for u in range(2) for side in range(2)]
            natural = dot(to_natural[...], jnp.concatenate(parts, axis=0)).reshape(2, 8, 8, 1024)
            blocks.append(natural)
        tokens_out[:, 8 * m:8 * m + 8] = jnp.concatenate(blocks, axis=2).astype(BF16)
    while running:
        advance()
    for copy in list(first_send.values()) + started:
        copy.wait_send()


def back(q, k, v, mix, mix_grad, normed_turned, mix_turned, grad, x, qkv_weight, merged_groups):
    streams = 4 * CHUNKS
    vmem, anywhere = pl.BlockSpec(memory_space=pltpu.VMEM), pl.BlockSpec(memory_space=pl.ANY)
    tokens = pltpu.VMEM((768, 1024), BF16)
    turned = pltpu.VMEM((1024, 768), BF16)
    return pl.pallas_call(
        back_kernel,
        out_shape=(jax.ShapeDtypeStruct((8, 3072), F32), jax.ShapeDtypeStruct((8, 1024), F32),
                   jax.ShapeDtypeStruct((2, 16, 24, 1024), BF16), jax.ShapeDtypeStruct((2, 8, 12, 1024), BF16)),
        in_specs=[anywhere] * 10 + [vmem] * 5,
        out_specs=(vmem, vmem, vmem, vmem),
        scratch_shapes=[
            tokens, tokens, tokens, tokens, tokens, turned, turned, tokens, tokens, pltpu.VMEM((1024, 3072), BF16),
            tokens, tokens, tokens,
            pltpu.VMEM((10, 64, 2, 16, 128), BF16),
            pltpu.VMEM((768, 1024), F32),
            pltpu.VMEM((5, 7, 32, 1024), BF16),
            pltpu.VMEM((5, 7, 8, 1024), F32),
            pltpu.VMEM((streams, 64, 16, 128), BF16),
            pltpu.VMEM((streams, 4, 16, 16, 128), BF16),
            pltpu.VMEM((streams, 3, 16, 16, 128), BF16),
            pltpu.VMEM((streams, 4, 4, 16, 128), BF16),
            pltpu.VMEM((streams, 3, 4, 16, 128), BF16),
            pltpu.VMEM((streams, 4, 16, 128), BF16),
            pltpu.VMEM((streams, 3, 16, 128), BF16),
            pltpu.SemaphoreType.DMA((25,)),
            pltpu.SemaphoreType.DMA((streams, 10)),
            pltpu.SemaphoreType.DMA((streams, 10)),
            pltpu.SemaphoreType.DMA((6,)),
            pltpu.SemaphoreType.DMA((6,)),
        ],
        compiler_params=pltpu.CompilerParams(collective_id=0, has_side_effects=True, vmem_limit_bytes=62 * MIB),
        name="back",
    )(q, k, v, mix, mix_grad, normed_turned, mix_turned, grad, x, qkv_weight, merged_groups, *orders())


def enter_kernel(tokens, merged_grad, to_natural, to_quarters, merged_natural, merged_windows,
                 x_out, normed_out, normed_turned, groups_out, units, merged_units, send, recv):
    before, after = neighbours(-1), neighbours(1)
    greet(before, after)
    copies = (frame_copies(units, (4, 6), (0, 0), send, recv, 0, after)
              + frame_copies(merged_units, (4, 6), (0, 0), send, recv, 3, after))
    for m in (1, 0):
        rows = tokens[:, 8 * m:8 * m + 8].astype(F32)
        for n in range(3):
            natural = rows[:, :, 8 * n:8 * n + 8].reshape(128, 1024).astype(BF16)
            quarters = dot(to_natural[...], natural, TN).astype(BF16).reshape(4, 32, 1024)
            for u in range(2):
                for side in range(2):
                    units[2 * m + 1 + u, 2 * n + 1 + side] = quarters[2 * u + side]
        if m == 1:
            copies[0].start()
            copies[2].start()
        else:
            copies[1].start()
    merged_in = dot(merged_natural[...], merged_grad[...], TN).reshape(4, 6, 8, 1024)
    for i in range(4):
        merged_units[i + 1, 1:7] = merged_in[i]
    for copy in copies[3:]:
        copy.start()

    def window(w):
        wa, wb = w // 3, w % 3
        quarters = [units[2 * wa + u, 2 * wb + side] for u in range(2) for side in range(2)]
        values = dot(to_quarters[...], jnp.concatenate(quarters, axis=0))
        rows = pl.ds(w * 128, 128)
        x_out[rows] = values.astype(BF16)
        centered, inverse = statistics(values)
        normed = centered * inverse
        normed_out[rows] = normed.astype(BF16)
        normed_turned[:, rows] = normed.T.astype(BF16)

    window(4)
    window(5)
    copies[1].wait_recv()
    window(3)
    for copy in copies[3:]:
        copy.wait_recv()
    groups = jnp.concatenate([merged_units[i, 0:6].reshape(48, 1024) for i in range(4)], axis=0)
    groups_out[...] = dot(merged_windows[...], groups.astype(BF16)).astype(BF16)
    copies[0].wait_recv()
    window(1)
    window(2)
    copies[2].wait_recv()
    window(0)
    for copy in copies:
        copy.wait_send()


def enter(tokens, merged_grad):
    vmem = pl.BlockSpec(memory_space=pltpu.VMEM)
    grid_tokens = jax.ShapeDtypeStruct((768, 1024), BF16)
    return pl.pallas_call(
        enter_kernel,
        out_shape=(grid_tokens, grid_tokens, jax.ShapeDtypeStruct((1024, 768), BF16),
                   jax.ShapeDtypeStruct((192, 1024), BF16)),
        in_specs=[vmem] * 6,
        out_specs=(vmem,) * 4,
        scratch_shapes=[
            pltpu.VMEM((5, 7, 32, 1024), BF16),
            pltpu.VMEM((5, 7, 8, 1024), F32),
            pltpu.SemaphoreType.DMA((6,)),
            pltpu.SemaphoreType.DMA((6,)),
        ],
        compiler_params=pltpu.CompilerParams(collective_id=1, has_side_effects=True, vmem_limit_bytes=48 * MIB),
        name="enter",
    )(tokens, merged_grad, *orders())


def attend_kernel(normed, wq, wk, wv, q_out, k_out, v_out, mix_out, mix_turned):
    for out, weight in ((q_out, wq), (k_out, wk), (v_out, wv)):
        out[...] = dot(normed[...], weight[...]).astype(BF16)
    lane = lax.broadcasted_iota(jnp.int32, (128, 128), 1)
    masks = [lane // 32 == head for head in range(4)]
    edge = lax.axis_index("lat") == 0
    for w in range(6):
        rows = pl.ds(w * 128, 128)
        for group in range(2):
            lanes = pl.ds(group * 128, 128)
            scores = dot(q_out[rows, lanes], stack(k_out[rows, lanes], masks), NT)
            weights = jnp.exp(scores * SCALE)
            if w < 3:
                weights = jnp.where(other_region(128, 512, edge), 0.0, weights)
            pieces = []
            for head in range(4):
                piece = weights[:, head * 128:head * 128 + 128]
                pieces.append((piece * (1.0 / jnp.sum(piece, axis=-1, keepdims=True))).astype(BF16))
            mixture = select(dot(jnp.concatenate(pieces, axis=0), v_out[rows, lanes]), masks)
            mix_out[rows, lanes] = mixture.astype(BF16)
            mix_turned[lanes, rows] = mixture.T.astype(BF16)


def attend(normed, qkv_weight):
    tokens = jax.ShapeDtypeStruct((768, 1024), BF16)
    block = pl.BlockSpec((768, 256), lambda c: (0, c))
    weight = lambda third: pl.BlockSpec((1024, 256), lambda c: (0, third * 4 + c))
    return pl.pallas_call(
        attend_kernel,
        grid=(4,),
        out_shape=(tokens, tokens, tokens, tokens, jax.ShapeDtypeStruct((1024, 768), BF16)),
        in_specs=[pl.BlockSpec((768, 1024), lambda c: (0, 0)), weight(0), weight(1), weight(2)],
        out_specs=(block, block, block, block, pl.BlockSpec((256, 768), lambda c: (c, 0))),
        compiler_params=params(), name="attend",
    )(normed, qkv_weight, qkv_weight, qkv_weight)


def merge_kernel(x, mixture, merged_grad, out_weight, merge_weight, merged_out, grad_out, mixture_grad,
                 normed, total, normed_grad):
    step = pl.program_id(0)

    @pl.when(step == 0)
    def _():
        for w in range(6):
            rows = pl.ds(w * 128, 128)
            values = x[rows].astype(F32) + dot(mixture[rows], out_weight[...])
            values = values.astype(BF16).astype(F32)
            quarters = [values[32 * j:32 * j + 32] for j in range(4)]
            center = sum(jnp.sum(part, axis=-1, keepdims=True) for part in quarters) * (1 / 4096)
            quarters = [part - center for part in quarters]
            spread = sum(jnp.sum(jnp.square(part), axis=-1, keepdims=True) for part in quarters) * (1 / 4096)
            inverse = lax.rsqrt(spread + epsilon)
            for j in range(4):
                normed[j, pl.ds(w * 32, 32)] = quarters[j] * inverse
            total[1, pl.ds(w * 32, 32)] = jnp.broadcast_to(inverse, (32, 1024))
        total[0] = jnp.zeros((192, 1024), F32)

    total[0] += dot(normed[step].astype(BF16), merge_weight[...])
    normed_grad[step] = dot(merged_grad[...], merge_weight[...], NT).astype(BF16).astype(F32)

    @pl.when(step == 3)
    def _():
        merged_out[...] = total[0].astype(BF16)
        for w in range(6):
            part = pl.ds(w * 32, 32)
            first = sum(jnp.sum(normed_grad[j, part], axis=-1, keepdims=True) for j in range(4)) * (1 / 4096)
            second = sum(jnp.sum(normed_grad[j, part] * normed[j, part], axis=-1, keepdims=True)
                         for j in range(4)) * (1 / 4096)
            inverse = total[1, part]
            for j in range(4):
                value = inverse * (normed_grad[j, part] - first - normed[j, part] * second)
                grad_out[pl.ds(w * 128 + j * 32, 32)] = value.astype(BF16)
        mixture_grad[...] = dot(grad_out[...], out_weight[...], NT).astype(BF16)


def merge_both(x, mixture, merged_grad, out_weight, merge_weight):
    whole = lambda rows: pl.BlockSpec((rows, 1024), lambda j: (0, 0))
    tokens = jax.ShapeDtypeStruct((768, 1024), BF16)
    return pl.pallas_call(
        merge_kernel,
        grid=(4,),
        out_shape=(jax.ShapeDtypeStruct((192, 1024), BF16), tokens, tokens),
        in_specs=[whole(768), whole(768), whole(192), whole(1024), pl.BlockSpec((1024, 1024), lambda j: (j, 0))],
        out_specs=(whole(192), whole(768), whole(768)),
        scratch_shapes=[pltpu.VMEM((4, 192, 1024), F32), pltpu.VMEM((2, 192, 1024), F32),
                        pltpu.VMEM((4, 192, 1024), F32)],
        compiler_params=params(), name="merge_both",
    )(x, mixture, merged_grad, out_weight, merge_weight)


def shards(tokens, qkv_weight, out_weight, merge_weight, merged_grad):
    x, normed, normed_turned, merged_grad_groups = enter(tokens, merged_grad.reshape(192, 1024))
    q, k, v, mixture, mix_turned = attend(normed, qkv_weight)
    merged_groups, grad, mixture_grad = merge_both(x, mixture, merged_grad_groups, out_weight, merge_weight)
    qkv_weight_grad, out_weight_grad, tokens_grad, merged = back(
        q, k, v, mixture, mixture_grad, normed_turned, mix_turned, grad, x, qkv_weight, merged_groups)
    return (merged, tokens_grad, qkv_weight_grad, out_weight_grad)


def solution(mesh):
    in_specs = (P(None, "lat", "lon", None), P(), P(), P(), P(None, "lat", "lon", None))
    out_specs = (
        P(None, "lat", "lon", None),
        P(None, "lat", "lon", None),
        P(("lat", "lon"), None),
        P(("lat", "lon"), None),
    )
    return jax.shard_map(shards, mesh=mesh, in_specs=in_specs, out_specs=out_specs, check_vma=False)
```

```python
import jax
import jax.numpy as jnp
import numpy as np
from jax import lax
from jax.experimental import pallas as pl
from jax.experimental.pallas import tpu as pltpu
from jax.sharding import PartitionSpec as P

CHUNKS = 4
MESH = pl.DeviceIdType.MESH
F32, BF16 = jnp.float32, jnp.bfloat16
epsilon = 1e-05
SCALE = 32 ** -0.5
MIB = 1024 * 1024
NT = (((1,), (1,)), ((), ()))
TN = (((0,), (0,)), ((), ()))


def dot(left, right, dims=(((1,), (0,)), ((), ()))):
    return lax.dot_general(left, right, dims, preferred_element_type=F32)


def picks(index):
    return (index[:, None] == np.arange(len(index))[None, :]).astype(np.float32)


def window_order():
    t = np.arange(128)
    quarter, level, a, b = t // 32, t // 16 % 2, t // 4 % 4, t % 4
    return picks((level * 8 + 2 * a + quarter % 2) * 8 + 2 * b + quarter // 2)


def orders():
    n = np.arange(128)
    level, i, j = n // 64, n // 8 % 8, n % 8
    to_natural = picks((((i // 4) * 2 + j // 4) * 2 + level) * 16 + (i % 4) * 4 + j % 4)
    to_quarters = window_order() @ to_natural
    n = np.arange(192)
    level, i, j = n // 96, n // 12 % 8, n % 12
    merged_natural = picks((((i // 2) * 6 + j // 2) * 2 + level) * 4 + (i % 2) * 2 + j % 2)
    window, level, a, b = n // 32, n // 16 % 2, n // 4 % 4, n % 4
    row, column = 2 * (window // 3) + a // 2, 2 * (window % 3) + b // 2
    merged_windows = picks(((row * 6 + column) * 2 + level) * 4 + (a % 2) * 2 + b % 2)
    return tuple(jnp.asarray(order, BF16) for order in (to_natural, to_quarters, merged_natural, merged_windows))


def statistics(values):
    center = jnp.mean(values, axis=-1, keepdims=True)
    shifted_values = values - center
    spread = jnp.mean(jnp.square(shifted_values), axis=-1, keepdims=True)
    return shifted_values, lax.rsqrt(spread + epsilon)


def place():
    lat, lon = lax.axis_index("lat"), lax.axis_index("lon")
    return (lat // 4) * 2 + (lon // 2) % 2, lon // 4, lat % 4, lon % 2


def device_at(x, y, z, core):
    return ((x // 2) * 4 + z, y * 4 + (x % 2) * 2 + core)


def neighbours(step):
    lat, lon = lax.axis_index("lat"), lax.axis_index("lon")
    lat_there, lon_there = (lat + step + 8) % 8, (lon + step + 16) % 16
    return (lat_there, lon), (lat, lon_there), (lat_there, lon_there)


def greet(receive_from, send_to):
    barrier = pltpu.get_barrier_semaphore()
    for device in receive_from:
        pl.semaphore_signal(barrier, inc=1, device_id=device, device_id_type=MESH)
    pl.semaphore_wait(barrier, len(send_to))


def remote(source, target, send, recv, device):
    return pltpu.make_async_remote_copy(src_ref=source, dst_ref=target, send_sem=send, recv_sem=recv,
                                        device_id=device, device_id_type=MESH)


def frame_copies(units, first, last, send, recv, base, devices):
    row, column, corner = devices
    return [remote(units.at[first[0], 1:6], units.at[last[0], 1:6], send.at[base], recv.at[base], row),
            remote(units.at[1:4, first[1]], units.at[1:4, last[1]], send.at[base + 1], recv.at[base + 1], column),
            remote(units.at[first[0], first[1]], units.at[last[0], last[1]], send.at[base + 2], recv.at[base + 2], corner)]


def wide_masks():
    lane = lax.broadcasted_iota(jnp.int32, (128, 256), 1)
    return [lane % 128 // 32 == head for head in range(4)], [lane // 128 == group for group in range(2)]


def stack(values, masks):
    zero = jnp.zeros_like(values)
    return jnp.concatenate([jnp.where(mask, values, zero) for mask in masks], axis=0)


def select(stacked, masks):
    rows = [stacked[128 * head:128 * head + 128] for head in range(4)]
    return jnp.where(masks[0], rows[0], jnp.where(masks[1], rows[1], jnp.where(masks[2], rows[2], rows[3])))


def other_region(rows, columns, edge):
    row = (lax.broadcasted_iota(jnp.int32, (rows, 1), 0) // 4 % 4 < 2) & edge
    column = (lax.broadcasted_iota(jnp.int32, (1, columns), 1) // 4 % 4 < 2) & edge
    return row.astype(jnp.int32) != column.astype(jnp.int32)


def back_kernel(q_hbm, k_hbm, v_hbm, mix_hbm, mix_grad_hbm, normed_hbm, mix_turned_hbm, grad_hbm, x_hbm, weight_hbm,
                merged_in, to_natural, to_quarters, merged_natural, merged_windows,
                qkv_out, out_out, tokens_out, merged_out,
                q, k, v, mix, mix_grad, normed_turned, mix_turned, grad, x_in, qkv_weight,
                dq, dk, dv, g, normed_grad, units, merged_units,
                from_core, acc_a, in_a, acc_b, in_b, acc_c, in_c, load, send, recv, strip_send, strip_recv):
    loads = {}

    def fetch(name, index, source, target):
        loads[name] = pltpu.make_async_copy(source, target, load.at[index])
        loads[name].start()

    fetch("mix", 21, mix_turned_hbm, mix_turned)
    fetch("grad", 22, grad_hbm, grad)
    fetch("normed", 20, normed_hbm, normed_turned)
    wide = ((q_hbm, q), (k_hbm, k), (v_hbm, v), (mix_hbm, mix), (mix_grad_hbm, mix_grad))
    for chunk in range(CHUNKS):
        columns = pl.ds(chunk * 256, 256)
        for i, (source, target) in enumerate(wide):
            fetch((chunk, i), chunk * 5 + i, source.at[:, columns], target.at[:, columns])
    fetch("weight", 23, weight_hbm, qkv_weight)
    fetch("x", 24, x_hbm, x_in)

    x, y, z, core = place()
    here = (x, y, z)

    def moved(axis, step):
        there = list(here)
        there[axis] = (here[axis] + step) % 4
        return device_at(there[0], there[1], there[2], core)

    sibling = device_at(x, y, z, 1 - core)
    ring = [sibling] + [moved(axis, step) for axis in range(3) for step in (1, 2, 3)]
    before, after = neighbours(-1), neighbours(1)
    greet(ring + list(after), ring + list(before))

    started = []
    first_send = {}

    def push(copy):
        copy.start()
        started.append(copy)
        return copy

    units_in = dot(merged_windows[...], merged_in[...], TN).reshape(4, 6, 8, 1024)
    for i in range(4):
        merged_units[i, 0:6] = units_in[i]
    merged_copies = frame_copies(merged_units, (0, 0), (4, 6), strip_send, strip_recv, 0, before)
    for copy in merged_copies:
        push(copy)

    def run(kind, chunk):
        stream = kind * CHUNKS + chunk
        slot = 6 + chunk if kind == 3 else chunk % 2 * 3 + kind
        order = [(kind + chunk + i) % 3 for i in range(3)]
        mine = [here[axis] for axis in order]
        copy = remote(g.at[slot, :, 1 - core], from_core.at[stream], send.at[stream, 0], recv.at[stream, 0], sibling)
        copy.start()
        first_send[(kind, chunk)] = copy
        yield
        copy.wait_recv()

        def add_block(index, carry):
            a, b = index // 4, index % 4
            for c in range(4):
                at = [None, None, None]
                for axis, value in zip(order, (a, b, c)):
                    at[axis] = value
                row = ((at[0] // 2) * 4 + at[2]) * 8 + at[1] * 2 + at[0] % 2
                total = g[slot, row, core].astype(F32) + from_core[stream, row].astype(F32)
                acc_a[stream, a, b * 4 + c] = total.astype(BF16)
            return carry

        lax.fori_loop(0, 16, add_block, 0)
        for level, (acc, arrived) in enumerate(((acc_a, in_a), (acc_b, in_b), (acc_c, in_c))):
            axis, p = order[level], mine[level]
            copies = [push(remote(acc.at[stream, (p + i + 1) % 4], arrived.at[stream, i],
                                  send.at[stream, 1 + level * 3 + i], recv.at[stream, 1 + level * 3 + i],
                                  moved(axis, i + 1))) for i in range(3)]
            yield
            for copy in copies:
                copy.wait_recv()
            total = acc[stream, p].astype(F32)
            for i in range(3):
                total = total + arrived[stream, i].astype(F32)
            if level == 0:
                for i in range(4):
                    acc_b[stream, i] = total[i * 4:i * 4 + 4].astype(BF16)
            elif level == 1:
                for i in range(4):
                    acc_c[stream, i] = total[i].astype(BF16)
        target, base = (out_out, chunk * 256) if kind == 3 else (qkv_out, kind * 1024 + chunk * 256)
        target[:, base:base + 128] = total[:8]
        target[:, base + 128:base + 256] = total[8:]

    running = []

    def advance():
        for job in list(running):
            try:
                next(job)
            except StopIteration:
                running.remove(job)

    head_mask, group_mask = wide_masks()
    row8 = lax.broadcasted_iota(jnp.int32, (8, 256), 0)
    lane8 = lax.broadcasted_iota(jnp.int32, (8, 256), 1) // 32
    own_head = jnp.where(lane8 == row8, 1.0, 0.0).astype(BF16)
    edge = lax.axis_index("lat") == 0
    def weight_terms(kinds, chunk):
        def weight_rows(i, carry):
            rows = pl.ds(pl.multiple_of(i * 256, 256), 256)
            pairs = pl.ds(i * 16, 16)
            for kind in kinds:
                left, right = ((normed_turned, dq), (normed_turned, dk), (normed_turned, dv), (mix_turned, grad))[kind]
                terms = dot(left[rows], right[:, chunk * 256:chunk * 256 + 256]).reshape(32, 8, 256)
                both = jnp.concatenate([terms[:, :, :128], terms[:, :, 128:]], axis=1)
                slot = 6 + chunk if kind == 3 else chunk % 2 * 3 + kind
                g[slot, pairs] = both.astype(BF16).reshape(16, 2, 16, 128)
            return carry

        lax.fori_loop(0, 4, weight_rows, 0)
        for kind in kinds:
            job = run(kind, chunk)
            next(job)
            running.append(job)

    for name in ("normed", "mix", "grad"):
        loads[name].wait()
    for chunk in range(CHUNKS):
        weight_terms((3,), chunk)
    for chunk in range(CHUNKS):
        columns = slice(chunk * 256, chunk * 256 + 256)
        for i in range(5):
            loads[(chunk, i)].wait()

        def window_back(wa):
            for wb in range(3):
                rows = pl.ds(pl.multiple_of(wa * 384 + wb * 128, 128), 128)
                queries, keys, values = q[rows, columns], k[rows, columns], v[rows, columns]
                out_grad = mix_grad[rows, columns]
                product = (out_grad.astype(F32) * mix[rows, columns].astype(F32)).astype(BF16)
                spread_queries, spread_grads = stack(queries, group_mask), stack(out_grad, group_mask)
                weights = jnp.exp(dot(stack(keys, head_mask), spread_queries, NT) * SCALE)
                weights = jnp.where(other_region(512, 256, edge & (wa == 0)), 0.0, weights)
                change = dot(stack(values, head_mask), spread_grads, NT)
                means = dot(own_head, product, NT)
                attention, scores_grad = [], []
                for head in range(4):
                    part = weights[128 * head:128 * head + 128]
                    part = part * (1.0 / jnp.sum(part, axis=0, keepdims=True))
                    mean = jnp.concatenate([means[head:head + 1], means[4 + head:5 + head]], axis=1)
                    attention.append(part.astype(BF16))
                    scores_grad.append((part * (change[128 * head:128 * head + 128] - mean)).astype(BF16))
                dv[rows, columns] = select(dot(jnp.concatenate(attention, axis=0), spread_grads), head_mask).astype(BF16)
                dk[rows, columns] = (select(dot(jnp.concatenate(scores_grad, axis=0), spread_queries), head_mask)
                                     * SCALE).astype(BF16)
                turned = keys.T
                pieces = []
                for group in range(2):
                    for head in range(4):
                        low = group * 128 + head * 32
                        pieces.append(dot(turned[low:low + 32], scores_grad[head][:, group * 128:group * 128 + 128]))
                dq[rows, columns] = (jnp.concatenate(pieces, axis=0).T * SCALE).astype(BF16)

        pl.loop(0, 2)(window_back)
        advance()
        if chunk >= 2:
            for kind in range(3):
                first_send.pop((kind, chunk - 2)).wait_send()
        weight_terms((0, 1, 2), chunk)
    loads["weight"].wait()
    loads["x"].wait()

    def finish_window(w):
        rows = pl.ds(w * 128, 128)
        change = normed_grad[rows].astype(BF16).astype(F32)
        centered, inverse = statistics(x_in[rows].astype(F32))
        normed = centered * inverse
        first = jnp.mean(change, axis=-1, keepdims=True)
        second = jnp.mean(change * normed, axis=-1, keepdims=True)
        value = (inverse * (change - first - normed * second)).astype(BF16).astype(F32) + grad[rows].astype(F32)
        quarters = dot(to_quarters[...], value.astype(BF16), TN).astype(BF16).reshape(4, 32, 1024)
        wa, wb = w // 3, w % 3
        for u in range(2):
            for side in range(2):
                units[2 * wa + u, 2 * wb + side] = quarters[2 * u + side]

    strips = frame_copies(units, (0, 0), (4, 6), strip_send, strip_recv, 3, before)
    for half in range(2):
        tokens = slice(half * 384, half * 384 + 384)
        for i in range(4):
            rows = slice(i * 256, i * 256 + 256)
            normed_grad[tokens, rows] = (dot(dq[tokens], qkv_weight[rows, 0:1024], NT)
                                         + dot(dk[tokens], qkv_weight[rows, 1024:2048], NT)
                                         + dot(dv[tokens], qkv_weight[rows, 2048:3072], NT))
            if (half, i) in ((0, 1), (1, 3)):
                advance()
        for wb in range(3):
            finish_window(half * 3 + wb)
            if half == 1 and wb == 0:
                push(strips[1])
        if half == 0:
            push(strips[0])
            push(strips[2])
        advance()
    for copy in merged_copies:
        copy.wait_recv()
    merged_natural_units = jnp.concatenate([merged_units[i, 1:7].reshape(48, 1024) for i in range(1, 5)], axis=0)
    natural = dot(merged_natural[...], merged_natural_units.astype(BF16))
    for i in range(16):
        merged_out[i // 8, i % 8] = natural[12 * i:12 * i + 12].astype(BF16)
    for copy in strips:
        copy.wait_recv()
    for m in range(2):
        blocks = []
        for n in range(3):
            parts = [units[2 * m + 1 + u, 2 * n + 1 + side] for u in range(2) for side in range(2)]
            natural = dot(to_natural[...], jnp.concatenate(parts, axis=0)).reshape(2, 8, 8, 1024)
            blocks.append(natural)
        tokens_out[:, 8 * m:8 * m + 8] = jnp.concatenate(blocks, axis=2).astype(BF16)
    while running:
        advance()
    for copy in list(first_send.values()) + started:
        copy.wait_send()


def back(q, k, v, mix, mix_grad, normed_turned, mix_turned, grad, x, qkv_weight, merged_groups):
    streams = 4 * CHUNKS
    vmem, anywhere = pl.BlockSpec(memory_space=pltpu.VMEM), pl.BlockSpec(memory_space=pl.ANY)
    tokens = pltpu.VMEM((768, 1024), BF16)
    turned = pltpu.VMEM((1024, 768), BF16)
    return pl.pallas_call(
        back_kernel,
        out_shape=(jax.ShapeDtypeStruct((8, 3072), F32), jax.ShapeDtypeStruct((8, 1024), F32),
                   jax.ShapeDtypeStruct((2, 16, 24, 1024), BF16), jax.ShapeDtypeStruct((2, 8, 12, 1024), BF16)),
        in_specs=[anywhere] * 10 + [vmem] * 5,
        out_specs=(vmem, vmem, vmem, vmem),
        scratch_shapes=[
            tokens, tokens, tokens, tokens, tokens, turned, turned, tokens, tokens, pltpu.VMEM((1024, 3072), BF16),
            tokens, tokens, tokens,
            pltpu.VMEM((10, 64, 2, 16, 128), BF16),
            pltpu.VMEM((768, 1024), F32),
            pltpu.VMEM((5, 7, 32, 1024), BF16),
            pltpu.VMEM((5, 7, 8, 1024), F32),
            pltpu.VMEM((streams, 64, 16, 128), BF16),
            pltpu.VMEM((streams, 4, 16, 16, 128), BF16),
            pltpu.VMEM((streams, 3, 16, 16, 128), BF16),
            pltpu.VMEM((streams, 4, 4, 16, 128), BF16),
            pltpu.VMEM((streams, 3, 4, 16, 128), BF16),
            pltpu.VMEM((streams, 4, 16, 128), BF16),
            pltpu.VMEM((streams, 3, 16, 128), BF16),
            pltpu.SemaphoreType.DMA((25,)),
            pltpu.SemaphoreType.DMA((streams, 10)),
            pltpu.SemaphoreType.DMA((streams, 10)),
            pltpu.SemaphoreType.DMA((6,)),
            pltpu.SemaphoreType.DMA((6,)),
        ],
        compiler_params=pltpu.CompilerParams(collective_id=0, has_side_effects=True, vmem_limit_bytes=62 * MIB),
        name="back",
    )(q, k, v, mix, mix_grad, normed_turned, mix_turned, grad, x, qkv_weight, merged_groups, *orders())


def front_kernel(tokens, merged_grad, weight_hbm, out_weight_hbm, merge_weight_hbm,
                 to_natural, to_quarters, merged_natural, merged_windows,
                 x_hbm, normed_hbm, q_hbm, k_hbm, v_hbm, mix_hbm, mix_turned_hbm, grad_hbm, mix_grad_hbm, merged_out,
                 x, normed, normed_turned, q, k, v, mix, mix_turned, grad, mix_grad,
                 qkv_weight, out_weight, merge_weight, scaled, change, inverses, groups, units, merged_units,
                 load, store, send, recv):
    loads = [pltpu.make_async_copy(source, target, load.at[i]) for i, (source, target) in enumerate(
        ((weight_hbm, qkv_weight), (out_weight_hbm, out_weight), (merge_weight_hbm, merge_weight)))]
    for copy in loads:
        copy.start()
    stores = []

    def keep(source, target):
        copy = pltpu.make_async_copy(source, target, store.at[len(stores)])
        copy.start()
        stores.append(copy)

    before, after = neighbours(-1), neighbours(1)
    greet(before, after)
    copies = (frame_copies(units, (4, 6), (0, 0), send, recv, 0, after)
              + frame_copies(merged_units, (4, 6), (0, 0), send, recv, 3, after))
    for m in (1, 0):
        rows = tokens[:, 8 * m:8 * m + 8].astype(F32)
        for n in range(3):
            natural = rows[:, :, 8 * n:8 * n + 8].reshape(128, 1024).astype(BF16)
            quarters = dot(to_natural[...], natural, TN).astype(BF16).reshape(4, 32, 1024)
            for u in range(2):
                for side in range(2):
                    units[2 * m + 1 + u, 2 * n + 1 + side] = quarters[2 * u + side]
        if m == 1:
            copies[0].start()
            copies[2].start()
        else:
            copies[1].start()
    merged_in = dot(merged_natural[...], merged_grad[...], TN).reshape(4, 6, 8, 1024)
    for i in range(4):
        merged_units[i + 1, 1:7] = merged_in[i]
    for copy in copies[3:]:
        copy.start()

    def window(w):
        wa, wb = w // 3, w % 3
        quarters = [units[2 * wa + u, 2 * wb + side] for u in range(2) for side in range(2)]
        values = dot(to_quarters[...], jnp.concatenate(quarters, axis=0))
        rows = pl.ds(w * 128, 128)
        x[rows] = values.astype(BF16)
        for i in range(4):
            centered, inverse = statistics(values[32 * i:32 * i + 32])
            normed[pl.ds(w * 128 + 32 * i, 32)] = (centered * inverse).astype(BF16)
        normed_turned[:, rows] = normed[rows].T

    lane = lax.broadcasted_iota(jnp.int32, (128, 128), 1)
    masks = [lane // 32 == head for head in range(4)]
    edge = lax.axis_index("lat") == 0

    def attend(half):
        tokens_here = pl.ds(half * 384, 384)

        def columns_of(chunk):
            low = pl.multiple_of(chunk * 256, 256)
            for third, target in enumerate((q, k, v)):
                weight = qkv_weight[:, pl.ds(pl.multiple_of(third * 1024 + chunk * 256, 256), 256)]
                target[tokens_here, pl.ds(low, 256)] = dot(normed[tokens_here], weight).astype(BF16)
            for w in range(3):
                rows = pl.ds(half * 384 + w * 128, 128)
                for group in range(2):
                    lanes = pl.ds(pl.multiple_of(low + group * 128, 128), 128)
                    scores = dot(q[rows, lanes], stack(k[rows, lanes], masks), NT)
                    weights = jnp.exp(scores * SCALE)
                    if half == 0:
                        weights = jnp.where(other_region(128, 512, edge), 0.0, weights)
                    pieces = []
                    for head in range(4):
                        piece = weights[:, head * 128:head * 128 + 128]
                        pieces.append((piece * (1.0 / jnp.sum(piece, axis=-1, keepdims=True))).astype(BF16))
                    mixture = select(dot(jnp.concatenate(pieces, axis=0), v[rows, lanes]), masks)
                    mix[rows, lanes] = mixture.astype(BF16)
                    mix_turned[lanes, rows] = mixture.T.astype(BF16)

        pl.loop(0, 4)(columns_of)

    window(4)
    window(5)
    copies[1].wait_recv()
    window(3)
    loads[0].wait()
    attend(1)
    copies[0].wait_recv()
    window(1)
    window(2)
    copies[2].wait_recv()
    window(0)
    keep(x, x_hbm)
    keep(normed_turned, normed_hbm)
    attend(0)
    for source, target in ((q, q_hbm), (k, k_hbm), (v, v_hbm), (mix, mix_hbm), (mix_turned, mix_turned_hbm)):
        keep(source, target)
    for copy in copies[3:]:
        copy.wait_recv()
    framed = jnp.concatenate([merged_units[i, 0:6].reshape(48, 1024) for i in range(4)], axis=0)
    groups[...] = dot(merged_windows[...], framed.astype(BF16)).astype(BF16)
    loads[1].wait()

    def add_branch(chunk):
        columns = pl.ds(pl.multiple_of(chunk * 256, 256), 256)
        scaled[:, columns] = x[:, columns].astype(F32) + dot(mix[...], out_weight[:, columns])

    pl.loop(0, 4)(add_branch)

    def quarter_rows(i):
        return [pl.ds(pl.multiple_of(i // 2 * 128 + j * 32 + i % 2 * 16, 16), 16) for j in range(4)]

    def group_rows(i):
        return [pl.ds(pl.multiple_of(j * 192 + i * 16, 16), 16) for j in range(4)]

    def normalize_groups(i):
        parts = [scaled[rows].astype(BF16).astype(F32) for rows in quarter_rows(i)]
        center = sum(jnp.sum(part, axis=-1, keepdims=True) for part in parts) * (1 / 4096)
        parts = [part - center for part in parts]
        spread = sum(jnp.sum(jnp.square(part), axis=-1, keepdims=True) for part in parts) * (1 / 4096)
        inverse = lax.rsqrt(spread + epsilon)
        inverses[pl.ds(pl.multiple_of(i * 16, 16), 16)] = jnp.broadcast_to(inverse, (16, 128))
        for part, rows in zip(parts, group_rows(i)):
            normed[rows] = (part * inverse).astype(BF16)
        for part, rows in zip(parts, quarter_rows(i)):
            scaled[rows] = part * inverse

    pl.loop(0, 12)(normalize_groups)
    loads[2].wait()

    def merge_columns(chunk):
        columns = pl.ds(pl.multiple_of(chunk * 256, 256), 256)
        total = dot(normed[0:192], merge_weight[0:1024, columns])
        for j in range(1, 4):
            total = total + dot(normed[192 * j:192 * j + 192], merge_weight[1024 * j:1024 * j + 1024, columns])
        merged_out[:, columns] = total.astype(BF16)
        for j in range(4):
            rows = pl.ds(pl.multiple_of(j * 1024 + chunk * 256, 256), 256)
            change[192 * j:192 * j + 192, columns] = dot(groups[...], merge_weight[rows], NT)

    pl.loop(0, 4)(merge_columns)

    def group_grads(i):
        changes = [change[rows].astype(BF16).astype(F32) for rows in group_rows(i)]
        values = [scaled[rows] for rows in quarter_rows(i)]
        first = sum(jnp.sum(part, axis=-1, keepdims=True) for part in changes) * (1 / 4096)
        second = sum(jnp.sum(part * value, axis=-1, keepdims=True) for part, value in zip(changes, values)) * (1 / 4096)
        inverse = inverses[pl.ds(pl.multiple_of(i * 16, 16), 16), 0:1]
        for part, value, rows in zip(changes, values, quarter_rows(i)):
            grad[rows] = (inverse * (part - first - value * second)).astype(BF16)

    pl.loop(0, 12)(group_grads)
    keep(grad, grad_hbm)

    def mixture_grads(chunk):
        rows = pl.ds(pl.multiple_of(chunk * 256, 256), 256)
        mix_grad[:, rows] = dot(grad[...], out_weight[rows], NT).astype(BF16)

    pl.loop(0, 4)(mixture_grads)
    keep(mix_grad, mix_grad_hbm)
    for copy in stores:
        copy.wait()
    for copy in copies:
        copy.wait_send()


def front(tokens, merged_grad, qkv_weight, out_weight, merge_weight):
    vmem, anywhere = pl.BlockSpec(memory_space=pltpu.VMEM), pl.BlockSpec(memory_space=pl.ANY)
    rows, turned = jax.ShapeDtypeStruct((768, 1024), BF16), jax.ShapeDtypeStruct((1024, 768), BF16)
    rows_vmem, turned_vmem = pltpu.VMEM((768, 1024), BF16), pltpu.VMEM((1024, 768), BF16)
    return pl.pallas_call(
        front_kernel,
        out_shape=(rows, turned, rows, rows, rows, rows, turned, rows, rows, jax.ShapeDtypeStruct((192, 1024), BF16)),
        in_specs=[vmem] * 2 + [anywhere] * 3 + [vmem] * 4,
        out_specs=(anywhere,) * 9 + (vmem,),
        scratch_shapes=[
            rows_vmem, rows_vmem, turned_vmem, rows_vmem, rows_vmem, rows_vmem, rows_vmem, turned_vmem, rows_vmem,
            rows_vmem,
            pltpu.VMEM((1024, 3072), BF16), pltpu.VMEM((1024, 1024), BF16), pltpu.VMEM((4096, 1024), BF16),
            pltpu.VMEM((768, 1024), F32), pltpu.VMEM((768, 1024), F32), pltpu.VMEM((192, 128), F32),
            pltpu.VMEM((192, 1024), BF16),
            pltpu.VMEM((5, 7, 32, 1024), BF16),
            pltpu.VMEM((5, 7, 8, 1024), F32),
            pltpu.SemaphoreType.DMA((3,)),
            pltpu.SemaphoreType.DMA((9,)),
            pltpu.SemaphoreType.DMA((6,)),
            pltpu.SemaphoreType.DMA((6,)),
        ],
        compiler_params=pltpu.CompilerParams(collective_id=1, has_side_effects=True, vmem_limit_bytes=62 * MIB),
        name="front",
    )(tokens, merged_grad, qkv_weight, out_weight, merge_weight, *orders())


def shards(tokens, qkv_weight, out_weight, merge_weight, merged_grad):
    x, normed_turned, q, k, v, mixture, mix_turned, grad, mixture_grad, merged_groups = front(
        tokens, merged_grad.reshape(192, 1024), qkv_weight, out_weight, merge_weight)
    qkv_weight_grad, out_weight_grad, tokens_grad, merged = back(
        q, k, v, mixture, mixture_grad, normed_turned, mix_turned, grad, x, qkv_weight, merged_groups)
    return (merged, tokens_grad, qkv_weight_grad, out_weight_grad)


def solution(mesh):
    in_specs = (P(None, "lat", "lon", None), P(), P(), P(), P(None, "lat", "lon", None))
    out_specs = (
        P(None, "lat", "lon", None),
        P(None, "lat", "lon", None),
        P(("lat", "lon"), None),
        P(("lat", "lon"), None),
    )
    return jax.shard_map(shards, mesh=mesh, in_specs=in_specs, out_specs=out_specs, check_vma=False)
```

```python
import jax
import jax.numpy as jnp
import numpy as np
from jax import lax
from jax.experimental import pallas as pl
from jax.experimental.pallas import tpu as pltpu
from jax.sharding import PartitionSpec as P

CHUNKS = 4
MESH = pl.DeviceIdType.MESH
F32, BF16 = jnp.float32, jnp.bfloat16
epsilon = 1e-05
SCALE = 32 ** -0.5
MIB = 1024 * 1024
NT = (((1,), (1,)), ((), ()))
TN = (((0,), (0,)), ((), ()))


def dot(left, right, dims=(((1,), (0,)), ((), ()))):
    return lax.dot_general(left, right, dims, preferred_element_type=F32)


def picks(index):
    return (index[:, None] == np.arange(len(index))[None, :]).astype(np.float32)


def window_order():
    t = np.arange(128)
    quarter, level, a, b = t // 32, t // 16 % 2, t // 4 % 4, t % 4
    return picks((level * 8 + 2 * a + quarter % 2) * 8 + 2 * b + quarter // 2)


def orders():
    n = np.arange(128)
    level, i, j = n // 64, n // 8 % 8, n % 8
    to_natural = picks((((i // 4) * 2 + j // 4) * 2 + level) * 16 + (i % 4) * 4 + j % 4)
    to_quarters = window_order() @ to_natural
    n = np.arange(192)
    level, j, i = n // 96, n // 8 % 12, n % 8
    merged_natural = picks((((i // 2) * 6 + j // 2) * 2 + level) * 4 + (i % 2) * 2 + j % 2)
    window, level, a, b = n // 32, n // 16 % 2, n // 4 % 4, n % 4
    row, column = 2 * (window // 3) + a // 2, 2 * (window % 3) + b // 2
    merged_windows = picks(((row * 6 + column) * 2 + level) * 4 + (a % 2) * 2 + b % 2)
    return tuple(jnp.asarray(order, BF16) for order in (to_natural, to_quarters, merged_natural, merged_windows))


def statistics(values):
    center = jnp.mean(values, axis=-1, keepdims=True)
    shifted_values = values - center
    spread = jnp.mean(jnp.square(shifted_values), axis=-1, keepdims=True)
    return shifted_values, lax.rsqrt(spread + epsilon)


def place():
    lat, lon = lax.axis_index("lat"), lax.axis_index("lon")
    return (lat // 4) * 2 + (lon // 2) % 2, lon // 4, lat % 4, lon % 2


def device_at(x, y, z, core):
    return ((x // 2) * 4 + z, y * 4 + (x % 2) * 2 + core)


def neighbours(step):
    lat, lon = lax.axis_index("lat"), lax.axis_index("lon")
    lat_there, lon_there = (lat + step + 8) % 8, (lon + step + 16) % 16
    return (lat_there, lon), (lat, lon_there), (lat_there, lon_there)


def greet(receive_from, send_to):
    barrier = pltpu.get_barrier_semaphore()
    for device in receive_from:
        pl.semaphore_signal(barrier, inc=1, device_id=device, device_id_type=MESH)
    pl.semaphore_wait(barrier, len(send_to))


def remote(source, target, send, recv, device):
    return pltpu.make_async_remote_copy(src_ref=source, dst_ref=target, send_sem=send, recv_sem=recv,
                                        device_id=device, device_id_type=MESH)


def frame_copies(units, first, last, send, recv, base, devices):
    row, column, corner = devices
    return [remote(units.at[first[0], 1:6], units.at[last[0], 1:6], send.at[base], recv.at[base], row),
            remote(units.at[1:4, first[1]], units.at[1:4, last[1]], send.at[base + 1], recv.at[base + 1], column),
            remote(units.at[first[0], first[1]], units.at[last[0], last[1]], send.at[base + 2], recv.at[base + 2], corner)]


def blocks_at(dims, axis, p):
    index = ({"h": p // 2, "l": p % 2}, {"y": p}, {"z": p})[axis]
    return tuple(index.get(dim, slice(None)) for dim in dims)


def left_over(dims, axis):
    return "".join(dim for dim in dims if dim not in ("hl", "y", "z")[axis])


def sizes(dims):
    return tuple({"h": 2, "z": 4, "y": 4, "l": 2}[dim] for dim in dims)


def wide_masks():
    lane = lax.broadcasted_iota(jnp.int32, (128, 256), 1)
    return [lane % 128 // 32 == head for head in range(4)], [lane // 128 == group for group in range(2)]


def stack(values, masks):
    zero = jnp.zeros_like(values)
    return jnp.concatenate([jnp.where(mask, values, zero) for mask in masks], axis=0)


def select(stacked, masks):
    rows = [stacked[128 * head:128 * head + 128] for head in range(4)]
    return jnp.where(masks[0], rows[0], jnp.where(masks[1], rows[1], jnp.where(masks[2], rows[2], rows[3])))


def other_region(rows, columns, edge):
    row = (lax.broadcasted_iota(jnp.int32, (rows, 1), 0) // 4 % 4 < 2) & edge
    column = (lax.broadcasted_iota(jnp.int32, (1, columns), 1) // 4 % 4 < 2) & edge
    return row.astype(jnp.int32) != column.astype(jnp.int32)


def back_kernel(q_hbm, k_hbm, v_hbm, mix_hbm, mix_grad_hbm, normed_hbm, mix_turned_hbm, grad_hbm, x_hbm, weight_hbm,
                merged_in, to_natural, to_quarters, merged_natural, merged_windows,
                qkv_out, out_out, tokens_out, merged_out,
                q, k, v, mix, mix_grad, normed_turned, mix_turned, grad, x_in, qkv_weight,
                dq, dk, dv, g, normed_grad, units, merged_units,
                from_core, acc_a, in_a_x, in_a_y, in_a_z, acc_b_x, acc_b_y, acc_b_z, in_b_x, in_b_y, in_b_z,
                acc_c_x, acc_c_y, acc_c_z, in_c, load, send, recv, strip_send, strip_recv):
    loads = {}

    def fetch(name, index, source, target):
        loads[name] = pltpu.make_async_copy(source, target, load.at[index])
        loads[name].start()

    fetch("mix", 21, mix_turned_hbm, mix_turned)
    fetch("grad", 22, grad_hbm, grad)
    wide = ((q_hbm, q), (k_hbm, k), (v_hbm, v), (mix_hbm, mix), (mix_grad_hbm, mix_grad))
    for chunk in range(CHUNKS):
        columns = pl.ds(chunk * 256, 256)
        for i, (source, target) in enumerate(wide):
            fetch((chunk, i), chunk * 5 + i, source.at[:, columns], target.at[:, columns])
        if chunk == 1:
            fetch("normed", 20, normed_hbm, normed_turned)
            fetch("weight", 23, weight_hbm, qkv_weight)
    fetch("x", 24, x_hbm, x_in)

    x, y, z, core = place()
    here = (x, y, z)

    def moved(axis, step):
        there = list(here)
        there[axis] = (here[axis] + step) % 4
        return device_at(there[0], there[1], there[2], core)

    sibling = device_at(x, y, z, 1 - core)
    ring = [sibling] + [moved(axis, step) for axis in range(3) for step in (1, 2, 3)]
    before, after = neighbours(-1), neighbours(1)
    greet(ring + list(after), ring + list(before))

    started = []
    first_send = {}

    def push(copy):
        copy.start()
        started.append(copy)
        return copy

    units_in = dot(merged_windows[...], merged_in[...], TN).reshape(4, 6, 8, 1024)
    for i in range(4):
        merged_units[i, 0:6] = units_in[i]
    merged_copies = frame_copies(merged_units, (0, 0), (4, 6), strip_send, strip_recv, 0, before)
    for copy in merged_copies:
        push(copy)

    by_axis = ((in_a_x, acc_b_x, in_b_x, acc_c_x), (in_a_y, acc_b_y, in_b_y, acc_c_y), (in_a_z, acc_b_z, in_b_z, acc_c_z))

    def run(kind, chunk):
        stream = kind * CHUNKS + chunk
        slot = 6 + chunk if kind == 3 else chunk % 2 * 3 + kind
        start = (kind + chunk) % 3
        local = sum((i // CHUNKS + i % CHUNKS) % 3 == start for i in range(stream))
        in_a, acc_b, in_b, acc_c = by_axis[start]
        copy = remote(g.at[slot, :, 1 - core], from_core.at[stream], send.at[stream, 0], recv.at[stream, 0], sibling)
        copy.start()
        first_send[(kind, chunk)] = copy
        yield
        copy.wait_recv()
        for i in range(8):
            total = (g[slot, i * 8:i * 8 + 8, core].astype(F32) + from_core[stream, i * 8:i * 8 + 8].astype(F32))
            acc_a[stream, i // 4, i % 4] = total.astype(BF16).reshape(4, 2, 16, 128)
        dims = "hzyl"
        levels = ((acc_a.at[stream], in_a.at[local], acc_b.at[local]), (acc_b.at[local], in_b.at[local], acc_c.at[local]),
                  (acc_c.at[local], in_c.at[stream], None))
        for level, (acc, arrived, following) in enumerate(levels):
            axis = (start + level) % 3
            p = here[axis]
            copies = [push(remote(acc.at[blocks_at(dims, axis, (p + i + 1) % 4)], arrived.at[i],
                                  send.at[stream, 1 + level * 3 + i], recv.at[stream, 1 + level * 3 + i],
                                  moved(axis, i + 1))) for i in range(3)]
            yield
            for copy in copies:
                copy.wait_recv()
            total = acc[blocks_at(dims, axis, p)].astype(F32)
            for i in range(3):
                total = total + arrived[i].astype(F32)
            if following is not None:
                following[...] = total.astype(BF16)
            dims = left_over(dims, axis)
        target, base = (out_out, chunk * 256) if kind == 3 else (qkv_out, kind * 1024 + chunk * 256)
        target[:, base:base + 128] = total[:8]
        target[:, base + 128:base + 256] = total[8:]

    jobs = {}

    def step(*names):
        for name in names:
            if name == "o":
                step("o0", "o1", "o2")
            elif name[0] == "c":
                for kind in range(3):
                    step("qkv"[kind] + name[1])
            elif name in jobs:
                next(jobs[name], None)
            else:
                jobs[name] = run("qkvo".index(name[0]), int(name[1]))
                next(jobs[name])

    head_mask, group_mask = wide_masks()
    row8 = lax.broadcasted_iota(jnp.int32, (8, 256), 0)
    lane8 = lax.broadcasted_iota(jnp.int32, (8, 256), 1) // 32
    own_head = jnp.where(lane8 == row8, 1.0, 0.0).astype(BF16)
    edge = lax.axis_index("lat") == 0
    def weight_terms(kinds, chunk, i):
        rows = pl.ds(i * 256, 256) if isinstance(i, int) else pl.ds(pl.multiple_of(i * 256, 256), 256)
        for kind in kinds:
            left, right = ((normed_turned, dq), (normed_turned, dk), (normed_turned, dv), (mix_turned, grad))[kind]
            terms = dot(left[rows], right[:, chunk * 256:chunk * 256 + 256]).reshape(32, 8, 256)
            both = jnp.concatenate([terms[:, :, :128], terms[:, :, 128:]], axis=1)
            slot = 6 + chunk if kind == 3 else chunk % 2 * 3 + kind
            g[slot, pl.ds(i * 16, 16)] = both.astype(BF16).reshape(16, 2, 16, 128)

    def add_normed_grad(chunk, half):
        tokens = slice(half * 384, half * 384 + 384)
        columns = slice(chunk * 256, chunk * 256 + 256)
        left = jnp.concatenate([part[tokens, columns] for part in (dq, dk, dv)], axis=1)
        for i in range(4):
            rows = slice(i * 256, i * 256 + 256)
            right = jnp.concatenate([qkv_weight[rows, third * 1024 + chunk * 256:third * 1024 + chunk * 256 + 256]
                                     for third in range(3)], axis=1)
            terms = dot(left, right, NT)
            normed_grad[tokens, rows] = terms if chunk == 0 else normed_grad[tokens, rows] + terms

    def window_back(chunk, w):
        columns = slice(chunk * 256, chunk * 256 + 256)
        rows = slice(w * 128, w * 128 + 128)
        queries, keys, values = q[rows, columns], k[rows, columns], v[rows, columns]
        out_grad = mix_grad[rows, columns]
        product = (out_grad.astype(F32) * mix[rows, columns].astype(F32)).astype(BF16)
        spread_queries, spread_grads = stack(queries, group_mask), stack(out_grad, group_mask)
        weights = jnp.exp(dot(stack(keys, head_mask), spread_queries, NT) * SCALE)
        if w < 3:
            weights = jnp.where(other_region(512, 256, edge), 0.0, weights)
        change = dot(stack(values, head_mask), spread_grads, NT)
        means = dot(own_head, product, NT)
        attention, scores_grad = [], []
        for head in range(4):
            part = weights[128 * head:128 * head + 128]
            part = part * (1.0 / jnp.sum(part, axis=0, keepdims=True))
            mean = jnp.concatenate([means[head:head + 1], means[4 + head:5 + head]], axis=1)
            attention.append(part.astype(BF16))
            scores_grad.append((part * (change[128 * head:128 * head + 128] - mean)).astype(BF16))
        dv[rows, columns] = select(dot(jnp.concatenate(attention, axis=0), spread_grads), head_mask).astype(BF16)
        dk[rows, columns] = (select(dot(jnp.concatenate(scores_grad, axis=0), spread_queries), head_mask)
                             * SCALE).astype(BF16)
        turned = keys.T
        pieces = []
        for group in range(2):
            for head in range(4):
                low = group * 128 + head * 32
                pieces.append(dot(turned[low:low + 32], scores_grad[head][:, group * 128:group * 128 + 128]))
        dq[rows, columns] = (jnp.concatenate(pieces, axis=0).T * SCALE).astype(BF16)

    for name in ("mix", "grad"):
        loads[name].wait()
    for chunk in range(CHUNKS):
        pl.loop(0, 4)(lambda i: weight_terms((3,), chunk, i))
        step("o" + str(chunk))
    schedule = (("o",), (), ("o3",), ("o", "c0"), (), ("c0", "o", "c1"), ("o3",), ("c1", "c2", "o"))
    for chunk in range(CHUNKS):
        for i in range(5):
            loads[(chunk, i)].wait()
        if chunk == 1:
            loads["normed"].wait()
            loads["weight"].wait()
        if chunk == 3:
            for kind in range(3):
                first_send.pop((kind, 0)).wait_send()
        for half in range(2):
            for wb in range(3):
                window_back(chunk, half * 3 + wb)
                if chunk > 0 and wb < 2:
                    weight_terms((0, 1, 2), chunk - 1, 2 * half + wb)
            if chunk > 0:
                add_normed_grad(chunk - 1, half)
            step(*schedule[2 * chunk + half])
    for kind in range(3):
        first_send.pop((kind, 1)).wait_send()
    for i in range(4):
        weight_terms((0, 1, 2), 3, i)
    step("c3", "c0", "o3")
    loads["x"].wait()

    def finish_window(w):
        pieces = []
        for i in range(4):
            rows = pl.ds(w * 128 + i * 32, 32)
            change = normed_grad[rows].astype(BF16).astype(F32)
            centered, inverse = statistics(x_in[rows].astype(F32))
            normed = centered * inverse
            first = jnp.mean(change, axis=-1, keepdims=True)
            second = jnp.mean(change * normed, axis=-1, keepdims=True)
            value = (inverse * (change - first - normed * second)).astype(BF16).astype(F32) + grad[rows].astype(F32)
            pieces.append(value.astype(BF16))
        quarters = dot(to_quarters[...], jnp.concatenate(pieces, axis=0), TN).astype(BF16).reshape(4, 32, 1024)
        wa, wb = w // 3, w % 3
        for u in range(2):
            for side in range(2):
                units[2 * wa + u, 2 * wb + side] = quarters[2 * u + side]

    strips = frame_copies(units, (0, 0), (4, 6), strip_send, strip_recv, 3, before)
    add_normed_grad(3, 0)
    step("c2")
    for w in range(3):
        finish_window(w)
        if w == 0:
            push(strips[2])
    push(strips[0])
    step("c3")
    add_normed_grad(3, 1)
    finish_window(3)
    push(strips[1])
    step("c1", "c0", "o3")
    for w in range(4, 6):
        finish_window(w)
    step("c2", "c1", "c0")
    for copy in merged_copies:
        copy.wait_recv()
    framed = jnp.concatenate([merged_units[i, 1:7].reshape(48, 1024) for i in range(1, 5)], axis=0)
    merged_out[...] = dot(merged_natural[...], framed.astype(BF16)).astype(BF16)

    def natural_rows(m):
        blocks = []
        for n in range(3):
            parts = [units[2 * m + 1 + u, 2 * n + 1 + side] for u in range(2) for side in range(2)]
            blocks.append(dot(to_natural[...], jnp.concatenate(parts, axis=0)).reshape(2, 8, 8, 1024))
        tokens_out[:, 8 * m:8 * m + 8] = jnp.concatenate(blocks, axis=2).astype(BF16)

    strips[1].wait_recv()
    natural_rows(0)
    step("c3", "c2", "c1")
    strips[0].wait_recv()
    strips[2].wait_recv()
    natural_rows(1)
    step("c3", "c2")
    step("c3")
    for copy in list(first_send.values()) + started:
        copy.wait_send()


def back(q, k, v, mix, mix_grad, normed_turned, mix_turned, grad, x, qkv_weight, merged_groups):
    streams = 4 * CHUNKS
    counts = [sum((i // CHUNKS + i % CHUNKS) % 3 == a for i in range(streams)) for a in range(3)]
    vmem, anywhere = pl.BlockSpec(memory_space=pltpu.VMEM), pl.BlockSpec(memory_space=pl.ANY)
    tokens = pltpu.VMEM((768, 1024), BF16)
    turned = pltpu.VMEM((1024, 768), BF16)
    return pl.pallas_call(
        back_kernel,
        out_shape=(jax.ShapeDtypeStruct((8, 3072), F32), jax.ShapeDtypeStruct((8, 1024), F32),
                   jax.ShapeDtypeStruct((2, 16, 24, 1024), BF16), jax.ShapeDtypeStruct((192, 1024), BF16)),
        in_specs=[anywhere] * 10 + [vmem] * 5,
        out_specs=(vmem, vmem, vmem, vmem),
        scratch_shapes=[
            tokens, tokens, tokens, tokens, tokens, turned, turned, tokens, tokens, pltpu.VMEM((1024, 3072), BF16),
            tokens, tokens, tokens,
            pltpu.VMEM((10, 64, 2, 16, 128), BF16),
            pltpu.VMEM((768, 1024), F32),
            pltpu.VMEM((5, 7, 32, 1024), BF16),
            pltpu.VMEM((5, 7, 8, 1024), F32),
            pltpu.VMEM((streams, 64, 16, 128), BF16),
            pltpu.VMEM((streams, 2, 4, 4, 2, 16, 128), BF16),
            *[pltpu.VMEM((counts[a], 3, *sizes(left_over("hzyl", a)), 16, 128), BF16) for a in range(3)],
            *[pltpu.VMEM((counts[a], *sizes(left_over("hzyl", a)), 16, 128), BF16) for a in range(3)],
            *[pltpu.VMEM((counts[a], 3, *sizes(left_over(left_over("hzyl", a), (a + 1) % 3)), 16, 128), BF16)
              for a in range(3)],
            *[pltpu.VMEM((counts[a], *sizes(left_over(left_over("hzyl", a), (a + 1) % 3)), 16, 128), BF16)
              for a in range(3)],
            pltpu.VMEM((streams, 3, 16, 128), BF16),
            pltpu.SemaphoreType.DMA((25,)),
            pltpu.SemaphoreType.DMA((streams, 10)),
            pltpu.SemaphoreType.DMA((streams, 10)),
            pltpu.SemaphoreType.DMA((6,)),
            pltpu.SemaphoreType.DMA((6,)),
        ],
        compiler_params=pltpu.CompilerParams(collective_id=0, has_side_effects=True, vmem_limit_bytes=62 * MIB),
        name="back",
    )(q, k, v, mix, mix_grad, normed_turned, mix_turned, grad, x, qkv_weight, merged_groups, *orders())


def front_kernel(tokens, merged_grad, weight_hbm, out_weight_hbm, merge_weight_hbm,
                 to_natural, to_quarters, merged_natural, merged_windows,
                 x_hbm, normed_hbm, q_hbm, k_hbm, v_hbm, mix_hbm, mix_turned_hbm, grad_hbm, mix_grad_hbm, merged_out,
                 x, normed, normed_turned, q, k, v, mix, mix_turned, grad, mix_grad,
                 qkv_weight, out_weight, merge_weight, scaled, change, inverses, groups, units, merged_units,
                 load, store, send, recv):
    loads = [pltpu.make_async_copy(source, target, load.at[i]) for i, (source, target) in enumerate(
        ((weight_hbm, qkv_weight), (out_weight_hbm, out_weight), (merge_weight_hbm, merge_weight)))]
    for copy in loads:
        copy.start()
    stores = []

    def keep(source, target):
        copy = pltpu.make_async_copy(source, target, store.at[len(stores)])
        copy.start()
        stores.append(copy)

    before, after = neighbours(-1), neighbours(1)
    greet(before, after)
    copies = (frame_copies(units, (4, 6), (0, 0), send, recv, 0, after)
              + frame_copies(merged_units, (4, 6), (0, 0), send, recv, 3, after))
    for m in (1, 0):
        rows = tokens[:, 8 * m:8 * m + 8].astype(F32)
        for n in range(3):
            natural = rows[:, :, 8 * n:8 * n + 8].reshape(128, 1024).astype(BF16)
            quarters = dot(to_natural[...], natural, TN).astype(BF16).reshape(4, 32, 1024)
            for u in range(2):
                for side in range(2):
                    units[2 * m + 1 + u, 2 * n + 1 + side] = quarters[2 * u + side]
        if m == 1:
            copies[0].start()
            copies[2].start()
        else:
            copies[1].start()
    merged_in = dot(merged_natural[...], merged_grad[...], TN).reshape(4, 6, 8, 1024)
    for i in range(4):
        merged_units[i + 1, 1:7] = merged_in[i]
    for copy in copies[3:]:
        copy.start()

    def window(w):
        wa, wb = w // 3, w % 3
        quarters = [units[2 * wa + u, 2 * wb + side] for u in range(2) for side in range(2)]
        values = dot(to_quarters[...], jnp.concatenate(quarters, axis=0))
        rows = pl.ds(w * 128, 128)
        x[rows] = values.astype(BF16)
        for i in range(4):
            centered, inverse = statistics(values[32 * i:32 * i + 32])
            normed[pl.ds(w * 128 + 32 * i, 32)] = (centered * inverse).astype(BF16)
        normed_turned[:, rows] = normed[rows].T

    head_mask, group_mask = wide_masks()
    edge = lax.axis_index("lat") == 0

    def project(half, chunk):
        rows = slice(half * 384, half * 384 + 384)
        for third, target in enumerate((q, k, v)):
            low = third * 1024 + chunk * 256
            target[rows, chunk * 256:chunk * 256 + 256] = dot(normed[rows], qkv_weight[:, low:low + 256]).astype(BF16)

    def attend(half, chunk):
        columns = slice(chunk * 256, chunk * 256 + 256)
        for w in range(half * 3, half * 3 + 3):
            rows = slice(w * 128, w * 128 + 128)
            scores = dot(stack(q[rows, columns], head_mask), stack(k[rows, columns], group_mask), NT)
            weights = jnp.exp(scores * SCALE)
            if half == 0:
                weights = jnp.where(other_region(512, 256, edge), 0.0, weights)
            pieces = []
            for group in range(2):
                piece = weights[:, group * 128:group * 128 + 128]
                pieces.append((piece * (1.0 / jnp.sum(piece, axis=-1, keepdims=True))).astype(BF16))
            mixture = select(dot(jnp.concatenate(pieces, axis=1), stack(v[rows, columns], group_mask)), head_mask)
            mixture = mixture.astype(BF16)
            mix[rows, columns] = mixture
            mix_turned[columns, rows] = mixture.T

    window(4)
    window(5)
    copies[1].wait_recv()
    window(3)
    loads[0].wait()
    project(1, 0)
    for chunk in range(3):
        project(1, chunk + 1)
        attend(1, chunk)
    copies[0].wait_recv()
    window(1)
    window(2)
    copies[2].wait_recv()
    window(0)
    keep(x, x_hbm)
    keep(normed_turned, normed_hbm)
    project(0, 0)
    attend(1, 3)
    for chunk in range(4):
        if chunk < 3:
            project(0, chunk + 1)
        attend(0, chunk)
    for source, target in ((q, q_hbm), (k, k_hbm), (v, v_hbm), (mix, mix_hbm), (mix_turned, mix_turned_hbm)):
        keep(source, target)
    for copy in copies[3:]:
        copy.wait_recv()
    framed = jnp.concatenate([merged_units[i, 0:6].reshape(48, 1024) for i in range(4)], axis=0)
    groups[...] = dot(merged_windows[...], framed.astype(BF16)).astype(BF16)
    loads[1].wait()

    def add_branch(chunk):
        columns = pl.ds(pl.multiple_of(chunk * 256, 256), 256)
        scaled[:, columns] = x[:, columns].astype(F32) + dot(mix[...], out_weight[:, columns])

    pl.loop(0, 4)(add_branch)

    def quarter_rows(i):
        return [pl.ds(pl.multiple_of(i // 2 * 128 + j * 32 + i % 2 * 16, 16), 16) for j in range(4)]

    def group_rows(i):
        return [pl.ds(pl.multiple_of(j * 192 + i * 16, 16), 16) for j in range(4)]

    def normalize_groups(i):
        parts = [scaled[rows].astype(BF16).astype(F32) for rows in quarter_rows(i)]
        center = sum(jnp.sum(part, axis=-1, keepdims=True) for part in parts) * (1 / 4096)
        parts = [part - center for part in parts]
        spread = sum(jnp.sum(jnp.square(part), axis=-1, keepdims=True) for part in parts) * (1 / 4096)
        inverse = lax.rsqrt(spread + epsilon)
        inverses[pl.ds(pl.multiple_of(i * 16, 16), 16)] = jnp.broadcast_to(inverse, (16, 128))
        for part, rows in zip(parts, group_rows(i)):
            normed[rows] = (part * inverse).astype(BF16)
        for part, rows in zip(parts, quarter_rows(i)):
            scaled[rows] = part * inverse

    pl.loop(0, 12)(normalize_groups)
    loads[2].wait()

    def merge_columns(chunk):
        columns = pl.ds(pl.multiple_of(chunk * 256, 256), 256)
        total = dot(normed[0:192], merge_weight[0:1024, columns])
        for j in range(1, 4):
            total = total + dot(normed[192 * j:192 * j + 192], merge_weight[1024 * j:1024 * j + 1024, columns])
        merged_out[:, columns] = total.astype(BF16)
        for j in range(4):
            rows = pl.ds(pl.multiple_of(j * 1024 + chunk * 256, 256), 256)
            change[192 * j:192 * j + 192, columns] = dot(groups[...], merge_weight[rows], NT)

    pl.loop(0, 4)(merge_columns)

    def group_grads(i):
        changes = [change[rows].astype(BF16).astype(F32) for rows in group_rows(i)]
        values = [scaled[rows] for rows in quarter_rows(i)]
        first = sum(jnp.sum(part, axis=-1, keepdims=True) for part in changes) * (1 / 4096)
        second = sum(jnp.sum(part * value, axis=-1, keepdims=True) for part, value in zip(changes, values)) * (1 / 4096)
        inverse = inverses[pl.ds(pl.multiple_of(i * 16, 16), 16), 0:1]
        for part, value, rows in zip(changes, values, quarter_rows(i)):
            grad[rows] = (inverse * (part - first - value * second)).astype(BF16)

    pl.loop(0, 12)(group_grads)
    keep(grad, grad_hbm)

    def mixture_grads(chunk):
        rows = pl.ds(pl.multiple_of(chunk * 256, 256), 256)
        mix_grad[:, rows] = dot(grad[...], out_weight[rows], NT).astype(BF16)

    pl.loop(0, 4)(mixture_grads)
    keep(mix_grad, mix_grad_hbm)
    for copy in stores:
        copy.wait()
    for copy in copies:
        copy.wait_send()


def front(tokens, merged_grad, qkv_weight, out_weight, merge_weight):
    vmem, anywhere = pl.BlockSpec(memory_space=pltpu.VMEM), pl.BlockSpec(memory_space=pl.ANY)
    rows, turned = jax.ShapeDtypeStruct((768, 1024), BF16), jax.ShapeDtypeStruct((1024, 768), BF16)
    rows_vmem, turned_vmem = pltpu.VMEM((768, 1024), BF16), pltpu.VMEM((1024, 768), BF16)
    return pl.pallas_call(
        front_kernel,
        out_shape=(rows, turned, rows, rows, rows, rows, turned, rows, rows, jax.ShapeDtypeStruct((192, 1024), BF16)),
        in_specs=[vmem] * 2 + [anywhere] * 3 + [vmem] * 4,
        out_specs=(anywhere,) * 9 + (vmem,),
        scratch_shapes=[
            rows_vmem, rows_vmem, turned_vmem, rows_vmem, rows_vmem, rows_vmem, rows_vmem, turned_vmem, rows_vmem,
            rows_vmem,
            pltpu.VMEM((1024, 3072), BF16), pltpu.VMEM((1024, 1024), BF16), pltpu.VMEM((4096, 1024), BF16),
            pltpu.VMEM((768, 1024), F32), pltpu.VMEM((768, 1024), F32), pltpu.VMEM((192, 128), F32),
            pltpu.VMEM((192, 1024), BF16),
            pltpu.VMEM((5, 7, 32, 1024), BF16),
            pltpu.VMEM((5, 7, 8, 1024), F32),
            pltpu.SemaphoreType.DMA((3,)),
            pltpu.SemaphoreType.DMA((9,)),
            pltpu.SemaphoreType.DMA((6,)),
            pltpu.SemaphoreType.DMA((6,)),
        ],
        compiler_params=pltpu.CompilerParams(collective_id=1, has_side_effects=True, vmem_limit_bytes=62 * MIB),
        name="front",
    )(tokens, merged_grad, qkv_weight, out_weight, merge_weight, *orders())


def shards(tokens, qkv_weight, out_weight, merge_weight, merged_grad):
    x, normed_turned, q, k, v, mixture, mix_turned, grad, mixture_grad, merged_groups = front(
        tokens, merged_grad.transpose(0, 2, 1, 3).reshape(192, 1024), qkv_weight, out_weight, merge_weight)
    qkv_weight_grad, out_weight_grad, tokens_grad, merged = back(
        q, k, v, mixture, mixture_grad, normed_turned, mix_turned, grad, x, qkv_weight, merged_groups)
    merged = merged.reshape(2, 12, 8, 1024).transpose(0, 2, 1, 3)
    return (merged, tokens_grad, qkv_weight_grad, out_weight_grad)


def solution(mesh):
    in_specs = (P(None, "lat", "lon", None), P(), P(), P(), P(None, "lat", "lon", None))
    out_specs = (
        P(None, "lat", "lon", None),
        P(None, "lat", "lon", None),
        P(("lat", "lon"), None),
        P(("lat", "lon"), None),
    )
    return jax.shard_map(shards, mesh=mesh, in_specs=in_specs, out_specs=out_specs, check_vma=False)
```

```python
import jax
import jax.numpy as jnp
import numpy as np
from jax import lax
from jax.experimental import pallas as pl
from jax.experimental.pallas import tpu as pltpu
from jax.sharding import PartitionSpec as P

CHUNKS = 4
MESH = pl.DeviceIdType.MESH
F32, BF16 = jnp.float32, jnp.bfloat16
epsilon = 1e-05
SCALE = 32 ** -0.5
MIB = 1024 * 1024
NT = (((1,), (1,)), ((), ()))
TN = (((0,), (0,)), ((), ()))


def dot(left, right, dims=(((1,), (0,)), ((), ()))):
    return lax.dot_general(left, right, dims, preferred_element_type=F32)


def picks(index):
    return (index[:, None] == np.arange(len(index))[None, :]).astype(np.float32)


def window_order():
    t = np.arange(128)
    quarter, level, a, b = t // 32, t // 16 % 2, t // 4 % 4, t % 4
    return picks((level * 8 + 2 * a + quarter % 2) * 8 + 2 * b + quarter // 2)


def orders():
    n = np.arange(128)
    level, i, j = n // 64, n // 8 % 8, n % 8
    to_natural = picks((((i // 4) * 2 + j // 4) * 2 + level) * 16 + (i % 4) * 4 + j % 4)
    to_quarters = window_order() @ to_natural
    n = np.arange(192)
    level, j, i = n // 96, n // 8 % 12, n % 8
    merged_natural = picks((((i // 2) * 6 + j // 2) * 2 + level) * 4 + (i % 2) * 2 + j % 2)
    window, level, a, b = n // 32, n // 16 % 2, n // 4 % 4, n % 4
    row, column = 2 * (window // 3) + a // 2, 2 * (window % 3) + b // 2
    merged_windows = picks(((row * 6 + column) * 2 + level) * 4 + (a % 2) * 2 + b % 2)
    return tuple(jnp.asarray(order, BF16) for order in (to_natural, to_quarters, merged_natural, merged_windows))


def statistics(values):
    center = jnp.mean(values, axis=-1, keepdims=True)
    shifted_values = values - center
    spread = jnp.mean(jnp.square(shifted_values), axis=-1, keepdims=True)
    return shifted_values, lax.rsqrt(spread + epsilon)


def place():
    lat, lon = lax.axis_index("lat"), lax.axis_index("lon")
    return (lat // 4) * 2 + (lon // 2) % 2, lon // 4, lat % 4, lon % 2


def device_at(x, y, z, core):
    return ((x // 2) * 4 + z, y * 4 + (x % 2) * 2 + core)


def neighbours(step):
    lat, lon = lax.axis_index("lat"), lax.axis_index("lon")
    lat_there, lon_there = (lat + step + 8) % 8, (lon + step + 16) % 16
    return (lat_there, lon), (lat, lon_there), (lat_there, lon_there)


def greet(receive_from, send_to):
    barrier = pltpu.get_barrier_semaphore()
    for device in receive_from:
        pl.semaphore_signal(barrier, inc=1, device_id=device, device_id_type=MESH)
    pl.semaphore_wait(barrier, len(send_to))


def remote(source, target, send, recv, device):
    return pltpu.make_async_remote_copy(src_ref=source, dst_ref=target, send_sem=send, recv_sem=recv,
                                        device_id=device, device_id_type=MESH)


def frame_copies(units, first, last, send, recv, base, devices):
    row, column, corner = devices
    return [remote(units.at[first[0], 1:6], units.at[last[0], 1:6], send.at[base], recv.at[base], row),
            remote(units.at[1:4, first[1]], units.at[1:4, last[1]], send.at[base + 1], recv.at[base + 1], column),
            remote(units.at[first[0], first[1]], units.at[last[0], last[1]], send.at[base + 2], recv.at[base + 2], corner)]


def blocks_at(dims, axis, p):
    index = ({"h": p // 2, "l": p % 2}, {"y": p}, {"z": p})[axis]
    return tuple(index.get(dim, slice(None)) for dim in dims)


def left_over(dims, axis):
    return "".join(dim for dim in dims if dim not in ("hl", "y", "z")[axis])


def sizes(dims):
    return tuple({"h": 2, "z": 4, "y": 4, "l": 2}[dim] for dim in dims)


def wide_masks():
    lane = lax.broadcasted_iota(jnp.int32, (128, 256), 1)
    return [lane % 128 // 32 == head for head in range(4)], [lane // 128 == group for group in range(2)]


def stack(values, masks):
    zero = jnp.zeros_like(values)
    return jnp.concatenate([jnp.where(mask, values, zero) for mask in masks], axis=0)


def select(stacked, masks):
    rows = [stacked[128 * head:128 * head + 128] for head in range(4)]
    return jnp.where(masks[0], rows[0], jnp.where(masks[1], rows[1], jnp.where(masks[2], rows[2], rows[3])))


def other_region(rows, columns, edge):
    row = (lax.broadcasted_iota(jnp.int32, (rows, 1), 0) // 4 % 4 < 2) & edge
    column = (lax.broadcasted_iota(jnp.int32, (1, columns), 1) // 4 % 4 < 2) & edge
    return row.astype(jnp.int32) != column.astype(jnp.int32)


def back_kernel(q_hbm, k_hbm, v_hbm, mix_hbm, mix_grad_hbm, normed_hbm, mix_turned_hbm, grad_hbm, x_hbm, weight_hbm,
                merged_in, to_natural, to_quarters, merged_natural, merged_windows,
                qkv_out, out_out, tokens_out, merged_out,
                q, k, v, mix, mix_grad, normed_turned, mix_turned, grad, x_in, qkv_weight,
                dq, dk, dv, g_x, g_y, g_z, g_p, g_r, normed_grad, units, merged_units, *rest):
    stream_buffers, (load, send, recv, strip_send, strip_recv) = rest[:-5], rest[-5:]

    def fetch(index, source, target):
        return pltpu.make_async_copy(source, target, load.at[index])

    def chunk_loads(chunk):
        columns = pl.ds(pl.multiple_of(chunk * 256, 256), 256)
        return [fetch(chunk * 5 + i, source.at[:, columns], target.at[:, columns]) for i, (source, target) in enumerate(
            ((q_hbm, q), (k_hbm, k), (v_hbm, v), (mix_hbm, mix), (mix_grad_hbm, mix_grad)))]

    normed_load, mix_load = fetch(20, normed_hbm, normed_turned), fetch(21, mix_turned_hbm, mix_turned)
    grad_load, weight_load, x_load = fetch(22, grad_hbm, grad), fetch(23, weight_hbm, qkv_weight), fetch(24, x_hbm, x_in)
    mix_load.start()
    grad_load.start()
    for copy in chunk_loads(0):
        copy.start()
    normed_load.start()

    @pl.loop(1, CHUNKS)
    def _(chunk):
        for copy in chunk_loads(chunk):
            copy.start()

    weight_load.start()
    x_load.start()

    x, y, z, core = place()
    here = (x, y, z)

    def moved(axis, step):
        there = list(here)
        there[axis] = (here[axis] + step) % 4
        return device_at(there[0], there[1], there[2], core)

    sibling = device_at(x, y, z, 1 - core)
    ring = [sibling] + [moved(axis, step) for axis in range(3) for step in (1, 2, 3)]
    before, after = neighbours(-1), neighbours(1)
    greet(ring + list(after), ring + list(before))

    units_in = dot(merged_windows[...], merged_in[...], TN).reshape(4, 6, 8, 1024)
    for i in range(4):
        merged_units[i, 0:6] = units_in[i]
    merged_copies = frame_copies(merged_units, (0, 0), (4, 6), strip_send, strip_recv, 0, before)
    for copy in merged_copies:
        copy.start()

    streams = ((g_x, 0), (g_y, 1), (g_z, 2), (g_p, 1), (g_r, 2))
    buffers = tuple(stream_buffers[7 * i:7 * i + 7] for i in range(5))

    def slot_of(kind, chunk):
        return chunk % 2 if kind < 3 else 0

    def core_copy(kind, chunk):
        return remote(streams[kind][0].at[slot_of(kind, chunk), :, 1 - core], buffers[kind][0].at[chunk],
                      send.at[kind, chunk, 0], recv.at[kind, chunk, 0], sibling)

    def level_refs(kind, chunk, level):
        acc = buffers[kind][1 + 2 * level].at[chunk]
        into = buffers[kind][2 + 2 * level].at[chunk]
        dims = "hzyl"
        for i in range(level):
            dims = left_over(dims, (streams[kind][1] + i) % 3)
        return acc, into, dims, (streams[kind][1] + level) % 3

    def level_copies(kind, chunk, level):
        acc, into, dims, axis = level_refs(kind, chunk, level)
        return [remote(acc.at[blocks_at(dims, axis, (here[axis] + i + 1) % 4)], into.at[i],
                       send.at[kind, chunk, 1 + level * 3 + i], recv.at[kind, chunk, 1 + level * 3 + i],
                       moved(axis, i + 1)) for i in range(3)]

    def core_to_first(kind, chunk):
        core_copy(kind, chunk).wait_recv()
        g, (from_core, acc) = streams[kind][0], buffers[kind][:2]
        width = g.shape[-1]

        @pl.loop(0, 8)
        def _(i):
            blocks = pl.ds(i * 8, 8)
            total = g[slot_of(kind, chunk), blocks, core].astype(F32) + from_core[chunk, blocks].astype(F32)
            acc[chunk, i // 4, i % 4] = total.astype(BF16).reshape(4, 2, 16, width)

        for copy in level_copies(kind, chunk, 0):
            copy.start()

    def level_to_next(kind, chunk, level):
        for copy in level_copies(kind, chunk, level):
            copy.wait_recv()
        acc, into, dims, axis = level_refs(kind, chunk, level)
        total = acc[blocks_at(dims, axis, here[axis])].astype(F32)
        for i in range(3):
            total = total + into[i].astype(F32)
        if level < 2:
            buffers[kind][3 + 2 * level][chunk] = total.astype(BF16)
            for copy in level_copies(kind, chunk, level + 1):
                copy.start()
            return
        width = total.shape[-1]
        if kind < 3:
            low = pl.multiple_of(kind * 1024 + chunk * 256, 256)
            qkv_out[:, pl.ds(low, width)] = total[:8]
            qkv_out[:, pl.ds(pl.multiple_of(low + width, 128), width)] = total[8:]
        else:
            low = (kind - 3) * 512
            out_out[:, low:low + width] = total[:8]
            out_out[:, low + width:low + 2 * width] = total[8:]

    head_mask, group_mask = wide_masks()
    row8 = lax.broadcasted_iota(jnp.int32, (8, 256), 0)
    lane8 = lax.broadcasted_iota(jnp.int32, (8, 256), 1) // 32
    own_head = jnp.where(lane8 == row8, 1.0, 0.0).astype(BF16)
    edge = lax.axis_index("lat") == 0
    def put_terms(kind, chunk, i, terms):
        g = streams[kind][0]
        width = g.shape[-1]
        both = jnp.concatenate([terms[:, :, :width], terms[:, :, width:]], axis=1)
        g[slot_of(kind, chunk), pl.ds(i * 16, 16)] = both.astype(BF16).reshape(16, 2, 16, width)

    def window_back(chunk, w):
        columns = pl.ds(pl.multiple_of(chunk * 256, 256), 256)
        rows = pl.ds(pl.multiple_of(w * 128, 128), 128)
        queries, keys, values = q[rows, columns], k[rows, columns], v[rows, columns]
        out_grad = mix_grad[rows, columns]
        product = (out_grad.astype(F32) * mix[rows, columns].astype(F32)).astype(BF16)
        spread_queries, spread_grads = stack(queries, group_mask), stack(out_grad, group_mask)
        weights = jnp.exp(dot(stack(keys, head_mask), spread_queries, NT) * SCALE)
        weights = jnp.where(other_region(512, 256, edge & (w < 3)), 0.0, weights)
        change = dot(stack(values, head_mask), spread_grads, NT)
        means = dot(own_head, product, NT)
        attention, scores_grad = [], []
        for head in range(4):
            part = weights[128 * head:128 * head + 128]
            part = part * (1.0 / jnp.sum(part, axis=0, keepdims=True))
            mean = jnp.concatenate([means[head:head + 1], means[4 + head:5 + head]], axis=1)
            attention.append(part.astype(BF16))
            scores_grad.append((part * (change[128 * head:128 * head + 128] - mean)).astype(BF16))
        dv[rows, columns] = select(dot(jnp.concatenate(attention, axis=0), spread_grads), head_mask).astype(BF16)
        dk[rows, columns] = (select(dot(jnp.concatenate(scores_grad, axis=0), spread_queries), head_mask)
                             * SCALE).astype(BF16)
        turned = keys.T
        pieces = []
        for group in range(2):
            for head in range(4):
                low = group * 128 + head * 32
                pieces.append(dot(turned[low:low + 32], scores_grad[head][:, group * 128:group * 128 + 128]))
        dq[rows, columns] = (jnp.concatenate(pieces, axis=0).T * SCALE).astype(BF16)

    mix_load.wait()
    grad_load.wait()

    @pl.loop(0, 4)
    def _(i):
        rows = pl.ds(pl.multiple_of(i * 256, 256), 256)
        for kind in (3, 4):
            low = (kind - 3) * 512
            put_terms(kind, 0, i, dot(mix_turned[rows], grad[:, low:low + 512]).reshape(32, 8, 512))

    for kind in (3, 4):
        core_copy(kind, 0).start()

    def finish_window(w):
        pieces = []
        for i in range(4):
            rows = pl.ds(pl.multiple_of(w * 128 + i * 32, 32), 32)
            change = normed_grad[rows].astype(BF16).astype(F32)
            centered, inverse = statistics(x_in[rows].astype(F32))
            normed = centered * inverse
            first = jnp.mean(change, axis=-1, keepdims=True)
            second = jnp.mean(change * normed, axis=-1, keepdims=True)
            value = (inverse * (change - first - normed * second)).astype(BF16).astype(F32) + grad[rows].astype(F32)
            pieces.append(value.astype(BF16))
        quarters = dot(to_quarters[...], jnp.concatenate(pieces, axis=0), TN).astype(BF16).reshape(4, 32, 1024)
        wa, wb = w // 3, w % 3
        for u in range(2):
            for side in range(2):
                units[2 * wa + u, 2 * wb + side] = quarters[2 * u + side]

    strips = frame_copies(units, (0, 0), (4, 6), strip_send, strip_recv, 3, before)

    @pl.loop(0, 8)
    def _(t):
        @pl.when(t < CHUNKS)
        def _():
            for copy in chunk_loads(t):
                copy.wait()

            @pl.loop(0, 2)
            def _(wa):
                for wb in range(3):
                    window_back(t, wa * 3 + wb)

        @pl.when((t == 4) | (t == 5))
        def _():
            @pl.when(t == 4)
            def _():
                weight_load.wait()
                x_load.wait()

            tokens = pl.ds(pl.multiple_of((t - 4) * 384, 384), 384)

            @pl.loop(0, 4)
            def _(i):
                rows = pl.ds(pl.multiple_of(i * 256, 256), 256)
                normed_grad[tokens, rows] = (dot(dq[tokens], qkv_weight[rows, 0:1024], NT)
                                             + dot(dk[tokens], qkv_weight[rows, 1024:2048], NT)
                                             + dot(dv[tokens], qkv_weight[rows, 2048:3072], NT))

            @pl.loop(0, 3)
            def _(wb):
                finish_window((t - 4) * 3 + wb)

                @pl.when((t == 5) & (wb == 0))
                def _():
                    strips[1].start()

            @pl.when(t == 4)
            def _():
                strips[0].start()
                strips[2].start()

        @pl.when(t == 6)
        def _():
            for copy in merged_copies:
                copy.wait_recv()
            framed = jnp.concatenate([merged_units[i, 1:7].reshape(48, 1024) for i in range(1, 5)], axis=0)
            merged_out[...] = dot(merged_natural[...], framed.astype(BF16)).astype(BF16)
            strips[1].wait_recv()

        @pl.when(t == 7)
        def _():
            strips[0].wait_recv()
            strips[2].wait_recv()

        @pl.when(t >= 6)
        def _():
            m = t - 6
            blocks = []
            for n in range(3):
                parts = [units[2 * m + 1 + u, 2 * n + 1 + side] for u in range(2) for side in range(2)]
                blocks.append(dot(to_natural[...], jnp.concatenate(parts, axis=0)).reshape(2, 8, 8, 1024))
            tokens_out[:, pl.ds(8 * m, 8)] = jnp.concatenate(blocks, axis=2).astype(BF16)

        for level in (2, 1, 0):
            chunk = t - 2 - level

            @pl.when((chunk >= 0) & (chunk < CHUNKS))
            def _():
                for kind in range(3):
                    level_to_next(kind, chunk, level)

        @pl.when((t >= 1) & (t <= CHUNKS))
        def _():
            for kind in range(3):
                core_to_first(kind, t - 1)

        @pl.when(t == 0)
        def _():
            for kind in (3, 4):
                core_to_first(kind, 0)

            normed_load.wait()

        for level in range(3):
            @pl.when(t == level + 1)
            def _():
                for kind in (3, 4):
                    level_to_next(kind, 0, level)

        @pl.when(t < CHUNKS)
        def _():
            @pl.when(t >= 2)
            def _():
                for kind in range(3):
                    core_copy(kind, t - 2).wait_send()

            columns = pl.ds(pl.multiple_of(t * 256, 256), 256)

            @pl.loop(0, 4)
            def _(i):
                rows = pl.ds(pl.multiple_of(i * 256, 256), 256)
                for kind, right in enumerate((dq, dk, dv)):
                    put_terms(kind, t, i, dot(normed_turned[rows], right[:, columns]).reshape(32, 8, 256))

            for kind in range(3):
                core_copy(kind, t).start()

    for kind in range(3):
        core_copy(kind, 2).wait_send()
        core_copy(kind, 3).wait_send()

    @pl.loop(0, CHUNKS)
    def _(chunk):
        for kind in range(3):
            for level in range(3):
                for copy in level_copies(kind, chunk, level):
                    copy.wait_send()

    for kind in (3, 4):
        core_copy(kind, 0).wait_send()
        for level in range(3):
            for copy in level_copies(kind, 0, level):
                copy.wait_send()
    for copy in merged_copies + strips:
        copy.wait_send()


def back(q, k, v, mix, mix_grad, normed_turned, mix_turned, grad, x, qkv_weight, merged_groups):
    buffers = []
    for axis, count, width in ((0, CHUNKS, 128), (1, CHUNKS, 128), (2, CHUNKS, 128), (1, 1, 256), (2, 1, 256)):
        first = left_over("hzyl", axis)
        second = left_over(first, (axis + 1) % 3)
        for shape in ((64,), (2, 4, 4, 2), (3, *sizes(first)), sizes(first), (3, *sizes(second)), sizes(second), (3,)):
            buffers.append(pltpu.VMEM((count, *shape, 16, width), BF16))
    vmem, anywhere = pl.BlockSpec(memory_space=pltpu.VMEM), pl.BlockSpec(memory_space=pl.ANY)
    tokens = pltpu.VMEM((768, 1024), BF16)
    turned = pltpu.VMEM((1024, 768), BF16)
    return pl.pallas_call(
        back_kernel,
        out_shape=(jax.ShapeDtypeStruct((8, 3072), F32), jax.ShapeDtypeStruct((8, 1024), F32),
                   jax.ShapeDtypeStruct((2, 16, 24, 1024), BF16), jax.ShapeDtypeStruct((192, 1024), BF16)),
        in_specs=[anywhere] * 10 + [vmem] * 5,
        out_specs=(vmem, vmem, vmem, vmem),
        scratch_shapes=[
            tokens, tokens, tokens, tokens, tokens, turned, turned, tokens, tokens, pltpu.VMEM((1024, 3072), BF16),
            tokens, tokens, tokens,
            *[pltpu.VMEM((2, 64, 2, 16, 128), BF16)] * 3, *[pltpu.VMEM((1, 64, 2, 16, 256), BF16)] * 2,
            pltpu.VMEM((768, 1024), F32),
            pltpu.VMEM((5, 7, 32, 1024), BF16),
            pltpu.VMEM((5, 7, 8, 1024), F32),
            *buffers,
            pltpu.SemaphoreType.DMA((25,)),
            pltpu.SemaphoreType.DMA((5, CHUNKS, 10)),
            pltpu.SemaphoreType.DMA((5, CHUNKS, 10)),
            pltpu.SemaphoreType.DMA((6,)),
            pltpu.SemaphoreType.DMA((6,)),
        ],
        compiler_params=pltpu.CompilerParams(collective_id=0, has_side_effects=True, vmem_limit_bytes=62 * MIB),
        name="back",
    )(q, k, v, mix, mix_grad, normed_turned, mix_turned, grad, x, qkv_weight, merged_groups, *orders())


def front_kernel(tokens, merged_grad, weight_hbm, out_weight_hbm, merge_weight_hbm,
                 to_natural, to_quarters, merged_natural, merged_windows,
                 x_hbm, normed_hbm, q_hbm, k_hbm, v_hbm, mix_hbm, mix_turned_hbm, grad_hbm, mix_grad_hbm, merged_out,
                 x, normed, normed_turned, q, k, v, mix, mix_turned, grad, mix_grad,
                 qkv_weight, out_weight, merge_weight, scaled, change, inverses, groups, units, merged_units,
                 load, store, send, recv):
    loads = [pltpu.make_async_copy(source, target, load.at[i]) for i, (source, target) in enumerate(
        ((weight_hbm, qkv_weight), (out_weight_hbm, out_weight), (merge_weight_hbm, merge_weight)))]
    for copy in loads:
        copy.start()
    before, after = neighbours(-1), neighbours(1)
    greet(before, after)
    copies = (frame_copies(units, (4, 6), (0, 0), send, recv, 0, after)
              + frame_copies(merged_units, (4, 6), (0, 0), send, recv, 3, after))

    @pl.loop(0, 32)
    def _(i):
        change[pl.ds(pl.multiple_of(i * 24, 8), 24)] = tokens[i // 16, i % 16].astype(F32)

    @pl.loop(0, 6)
    def _(i):
        m, n = 1 - i // 3, i % 3
        natural = [change[pl.ds(pl.multiple_of((level * 16 + 8 * m + row) * 24 + 8 * n, 8), 8)]
                   for level in range(2) for row in range(8)]
        quarters = dot(to_natural[...], jnp.concatenate(natural, axis=0).astype(BF16), TN)
        quarters = quarters.astype(BF16).reshape(4, 32, 1024)
        for u in range(2):
            for side in range(2):
                units[2 * m + 1 + u, 2 * n + 1 + side] = quarters[2 * u + side]

        @pl.when(i == 2)
        def _():
            copies[0].start()
            copies[2].start()

        @pl.when(i == 5)
        def _():
            copies[1].start()

    merged_in = dot(merged_natural[...], merged_grad[...], TN).reshape(4, 6, 8, 1024)
    for i in range(4):
        merged_units[i + 1, 1:7] = merged_in[i]
    for copy in copies[3:]:
        copy.start()

    def window(w):
        wa, wb = w // 3, w % 3
        quarters = [units[2 * wa + u, 2 * wb + side] for u in range(2) for side in range(2)]
        values = dot(to_quarters[...], jnp.concatenate(quarters, axis=0))
        rows = pl.ds(pl.multiple_of(w * 128, 128), 128)
        x[rows] = values.astype(BF16)
        for i in range(4):
            centered, inverse = statistics(values[32 * i:32 * i + 32])
            normed[pl.ds(pl.multiple_of(w * 128 + 32 * i, 32), 32)] = (centered * inverse).astype(BF16)
        normed_turned[:, rows] = normed[rows].T

    head_mask, group_mask = wide_masks()
    edge = lax.axis_index("lat") == 0

    def project(half, chunk):
        rows = pl.ds(pl.multiple_of(half * 384, 384), 384)
        columns = pl.ds(pl.multiple_of(chunk * 256, 256), 256)
        for third, target in enumerate((q, k, v)):
            low = pl.multiple_of(third * 1024 + chunk * 256, 256)
            target[rows, columns] = dot(normed[rows], qkv_weight[:, pl.ds(low, 256)]).astype(BF16)

    def attend(half, chunk):
        columns = pl.ds(pl.multiple_of(chunk * 256, 256), 256)
        for wb in range(3):
            rows = pl.ds(pl.multiple_of(half * 384 + wb * 128, 128), 128)
            scores = dot(stack(q[rows, columns], head_mask), stack(k[rows, columns], group_mask), NT)
            weights = jnp.exp(scores * SCALE)
            weights = jnp.where(other_region(512, 256, edge & (half == 0)), 0.0, weights)
            pieces = []
            for group in range(2):
                piece = weights[:, group * 128:group * 128 + 128]
                pieces.append((piece * (1.0 / jnp.sum(piece, axis=-1, keepdims=True))).astype(BF16))
            mixture = select(dot(jnp.concatenate(pieces, axis=1), stack(v[rows, columns], group_mask)), head_mask)
            mixture = mixture.astype(BF16)
            mix[rows, columns] = mixture
            mix_turned[columns, rows] = mixture.T

    keeps = [(x, x_hbm), (normed_turned, normed_hbm), (q, q_hbm), (k, k_hbm), (v, v_hbm), (mix, mix_hbm),
             (mix_turned, mix_turned_hbm), (grad, grad_hbm), (mix_grad, mix_grad_hbm)]
    stores = [pltpu.make_async_copy(source, target, store.at[i]) for i, (source, target) in enumerate(keeps)]

    @pl.loop(0, 2)
    def _(phase):
        half = 1 - phase

        @pl.loop(0, 3)
        def _(i):
            @pl.when((phase == 0) & (i == 2))
            def _():
                copies[1].wait_recv()

            @pl.when((phase == 1) & (i == 0))
            def _():
                copies[0].wait_recv()

            @pl.when((phase == 1) & (i == 2))
            def _():
                copies[2].wait_recv()

            window(half * 3 + (i + 1) % 3)

        @pl.when(phase == 0)
        def _():
            loads[0].wait()

        @pl.when(phase == 1)
        def _():
            stores[0].start()
            stores[1].start()

        project(half, 0)

        @pl.loop(0, 3)
        def _(chunk):
            project(half, chunk + 1)
            attend(half, chunk)

        attend(half, 3)

    for copy in stores[2:7]:
        copy.start()
    for copy in copies[3:]:
        copy.wait_recv()
    framed = jnp.concatenate([merged_units[i, 0:6].reshape(48, 1024) for i in range(4)], axis=0)
    groups[...] = dot(merged_windows[...], framed.astype(BF16)).astype(BF16)
    loads[1].wait()

    def add_branch(chunk):
        columns = pl.ds(pl.multiple_of(chunk * 256, 256), 256)
        scaled[:, columns] = x[:, columns].astype(F32) + dot(mix[...], out_weight[:, columns])

    pl.loop(0, 4)(add_branch)

    def quarter_rows(i):
        return [pl.ds(pl.multiple_of(i // 2 * 128 + j * 32 + i % 2 * 16, 16), 16) for j in range(4)]

    def group_rows(i):
        return [pl.ds(pl.multiple_of(j * 192 + i * 16, 16), 16) for j in range(4)]

    def normalize_groups(i):
        parts = [scaled[rows].astype(BF16).astype(F32) for rows in quarter_rows(i)]
        center = sum(jnp.sum(part, axis=-1, keepdims=True) for part in parts) * (1 / 4096)
        parts = [part - center for part in parts]
        spread = sum(jnp.sum(jnp.square(part), axis=-1, keepdims=True) for part in parts) * (1 / 4096)
        inverse = lax.rsqrt(spread + epsilon)
        inverses[pl.ds(pl.multiple_of(i * 16, 16), 16)] = jnp.broadcast_to(inverse, (16, 128))
        for part, rows in zip(parts, group_rows(i)):
            normed[rows] = (part * inverse).astype(BF16)
        for part, rows in zip(parts, quarter_rows(i)):
            scaled[rows] = part * inverse

    pl.loop(0, 12)(normalize_groups)
    loads[2].wait()

    def merge_columns(chunk):
        columns = pl.ds(pl.multiple_of(chunk * 256, 256), 256)
        total = dot(normed[0:192], merge_weight[0:1024, columns])
        for j in range(1, 4):
            total = total + dot(normed[192 * j:192 * j + 192], merge_weight[1024 * j:1024 * j + 1024, columns])
        merged_out[:, columns] = total.astype(BF16)
        for j in range(4):
            rows = pl.ds(pl.multiple_of(j * 1024 + chunk * 256, 256), 256)
            change[192 * j:192 * j + 192, columns] = dot(groups[...], merge_weight[rows], NT)

    pl.loop(0, 4)(merge_columns)

    def group_grads(i):
        changes = [change[rows].astype(BF16).astype(F32) for rows in group_rows(i)]
        values = [scaled[rows] for rows in quarter_rows(i)]
        first = sum(jnp.sum(part, axis=-1, keepdims=True) for part in changes) * (1 / 4096)
        second = sum(jnp.sum(part * value, axis=-1, keepdims=True) for part, value in zip(changes, values)) * (1 / 4096)
        inverse = inverses[pl.ds(pl.multiple_of(i * 16, 16), 16), 0:1]
        for part, value, rows in zip(changes, values, quarter_rows(i)):
            grad[rows] = (inverse * (part - first - value * second)).astype(BF16)

    pl.loop(0, 12)(group_grads)
    stores[7].start()

    def mixture_grads(chunk):
        rows = pl.ds(pl.multiple_of(chunk * 256, 256), 256)
        mix_grad[:, rows] = dot(grad[...], out_weight[rows], NT).astype(BF16)

    pl.loop(0, 4)(mixture_grads)
    stores[8].start()
    for copy in stores:
        copy.wait()
    for copy in copies:
        copy.wait_send()


def front(tokens, merged_grad, qkv_weight, out_weight, merge_weight):
    vmem, anywhere = pl.BlockSpec(memory_space=pltpu.VMEM), pl.BlockSpec(memory_space=pl.ANY)
    rows, turned = jax.ShapeDtypeStruct((768, 1024), BF16), jax.ShapeDtypeStruct((1024, 768), BF16)
    rows_vmem, turned_vmem = pltpu.VMEM((768, 1024), BF16), pltpu.VMEM((1024, 768), BF16)
    return pl.pallas_call(
        front_kernel,
        out_shape=(rows, turned, rows, rows, rows, rows, turned, rows, rows, jax.ShapeDtypeStruct((192, 1024), BF16)),
        in_specs=[vmem] * 2 + [anywhere] * 3 + [vmem] * 4,
        out_specs=(anywhere,) * 9 + (vmem,),
        scratch_shapes=[
            rows_vmem, rows_vmem, turned_vmem, rows_vmem, rows_vmem, rows_vmem, rows_vmem, turned_vmem, rows_vmem,
            rows_vmem,
            pltpu.VMEM((1024, 3072), BF16), pltpu.VMEM((1024, 1024), BF16), pltpu.VMEM((4096, 1024), BF16),
            pltpu.VMEM((768, 1024), F32), pltpu.VMEM((768, 1024), F32), pltpu.VMEM((192, 128), F32),
            pltpu.VMEM((192, 1024), BF16),
            pltpu.VMEM((5, 7, 32, 1024), BF16),
            pltpu.VMEM((5, 7, 8, 1024), F32),
            pltpu.SemaphoreType.DMA((3,)),
            pltpu.SemaphoreType.DMA((9,)),
            pltpu.SemaphoreType.DMA((6,)),
            pltpu.SemaphoreType.DMA((6,)),
        ],
        compiler_params=pltpu.CompilerParams(collective_id=1, has_side_effects=True, vmem_limit_bytes=62 * MIB),
        name="front",
    )(tokens, merged_grad, qkv_weight, out_weight, merge_weight, *orders())


def shards(tokens, qkv_weight, out_weight, merge_weight, merged_grad):
    x, normed_turned, q, k, v, mixture, mix_turned, grad, mixture_grad, merged_groups = front(
        tokens, merged_grad.transpose(0, 2, 1, 3).reshape(192, 1024), qkv_weight, out_weight, merge_weight)
    qkv_weight_grad, out_weight_grad, tokens_grad, merged = back(
        q, k, v, mixture, mixture_grad, normed_turned, mix_turned, grad, x, qkv_weight, merged_groups)
    merged = merged.reshape(2, 12, 8, 1024).transpose(0, 2, 1, 3)
    return (merged, tokens_grad, qkv_weight_grad, out_weight_grad)


def solution(mesh):
    in_specs = (P(None, "lat", "lon", None), P(), P(), P(), P(None, "lat", "lon", None))
    out_specs = (
        P(None, "lat", "lon", None),
        P(None, "lat", "lon", None),
        P(("lat", "lon"), None),
        P(("lat", "lon"), None),
    )
    return jax.shard_map(shards, mesh=mesh, in_specs=in_specs, out_specs=out_specs, check_vma=False)
```

```python
import jax
import jax.numpy as jnp
import numpy as np
from jax import lax
from jax.experimental import pallas as pl
from jax.experimental.pallas import tpu as pltpu
from jax.sharding import PartitionSpec as P

CHUNKS = 4
ROUTES = ((0, 1, 2), (1, 0, 2), (2, 1, 0), (0, 1, 2), (1, 0, 2))
MESH = pl.DeviceIdType.MESH
F32, BF16 = jnp.float32, jnp.bfloat16
epsilon = 1e-05
SCALE = 32 ** -0.5
MIB = 1024 * 1024
NT = (((1,), (1,)), ((), ()))
TN = (((0,), (0,)), ((), ()))


def dot(left, right, dims=(((1,), (0,)), ((), ()))):
    return lax.dot_general(left, right, dims, preferred_element_type=F32)


def picks(index):
    return (index[:, None] == np.arange(len(index))[None, :]).astype(np.float32)


def window_order():
    t = np.arange(128)
    quarter, level, a, b = t // 32, t // 16 % 2, t // 4 % 4, t % 4
    return picks((level * 8 + 2 * a + quarter % 2) * 8 + 2 * b + quarter // 2)


def orders():
    n = np.arange(128)
    level, i, j = n // 64, n // 8 % 8, n % 8
    to_natural = picks((((i // 4) * 2 + j // 4) * 2 + level) * 16 + (i % 4) * 4 + j % 4)
    to_quarters = window_order() @ to_natural
    n = np.arange(192)
    level, j, i = n // 96, n // 8 % 12, n % 8
    merged_natural = picks((((i // 2) * 6 + j // 2) * 2 + level) * 4 + (i % 2) * 2 + j % 2)
    window, level, a, b = n // 32, n // 16 % 2, n // 4 % 4, n % 4
    row, column = 2 * (window // 3) + a // 2, 2 * (window % 3) + b // 2
    merged_windows = picks(((row * 6 + column) * 2 + level) * 4 + (a % 2) * 2 + b % 2)
    return tuple(jnp.asarray(order, BF16) for order in (to_natural, to_quarters, merged_natural, merged_windows))


def statistics(values):
    center = jnp.mean(values, axis=-1, keepdims=True)
    shifted_values = values - center
    spread = jnp.mean(jnp.square(shifted_values), axis=-1, keepdims=True)
    return shifted_values, lax.rsqrt(spread + epsilon)


def place():
    lat, lon = lax.axis_index("lat"), lax.axis_index("lon")
    return (lat // 4) * 2 + (lon // 2) % 2, lon // 4, lat % 4, lon % 2


def device_at(x, y, z, core):
    return ((x // 2) * 4 + z, y * 4 + (x % 2) * 2 + core)


def neighbours(step):
    lat, lon = lax.axis_index("lat"), lax.axis_index("lon")
    lat_there, lon_there = (lat + step + 8) % 8, (lon + step + 16) % 16
    return (lat_there, lon), (lat, lon_there), (lat_there, lon_there)


def greet(receive_from, send_to):
    barrier = pltpu.get_barrier_semaphore()
    for device in receive_from:
        pl.semaphore_signal(barrier, inc=1, device_id=device, device_id_type=MESH)
    pl.semaphore_wait(barrier, len(send_to))


def remote(source, target, send, recv, device):
    return pltpu.make_async_remote_copy(src_ref=source, dst_ref=target, send_sem=send, recv_sem=recv,
                                        device_id=device, device_id_type=MESH)


def frame_copies(units, first, last, send, recv, base, devices):
    row, column, corner = devices
    return [remote(units.at[first[0], 1:6], units.at[last[0], 1:6], send.at[base], recv.at[base], row),
            remote(units.at[1:4, first[1]], units.at[1:4, last[1]], send.at[base + 1], recv.at[base + 1], column),
            remote(units.at[first[0], first[1]], units.at[last[0], last[1]], send.at[base + 2], recv.at[base + 2], corner)]


def blocks_at(dims, axis, p):
    index = ({"h": p // 2, "l": p % 2}, {"y": p}, {"z": p})[axis]
    return tuple(index.get(dim, slice(None)) for dim in dims)


def left_over(dims, axis):
    return "".join(dim for dim in dims if dim not in ("hl", "y", "z")[axis])


def sizes(dims):
    return tuple({"h": 2, "z": 4, "y": 4, "l": 2}[dim] for dim in dims)


def wide_masks():
    lane = lax.broadcasted_iota(jnp.int32, (128, 256), 1)
    return [lane % 128 // 32 == head for head in range(4)], [lane // 128 == group for group in range(2)]


def stack(values, masks):
    zero = jnp.zeros_like(values)
    return jnp.concatenate([jnp.where(mask, values, zero) for mask in masks], axis=0)


def select(stacked, masks):
    rows = [stacked[128 * head:128 * head + 128] for head in range(4)]
    return jnp.where(masks[0], rows[0], jnp.where(masks[1], rows[1], jnp.where(masks[2], rows[2], rows[3])))


def other_region(rows, columns, edge):
    row = (lax.broadcasted_iota(jnp.int32, (rows, 1), 0) // 4 % 4 < 2) & edge
    column = (lax.broadcasted_iota(jnp.int32, (1, columns), 1) // 4 % 4 < 2) & edge
    return row.astype(jnp.int32) != column.astype(jnp.int32)


def back_kernel(q_hbm, k_hbm, v_hbm, mix_hbm, mix_grad_hbm, normed_hbm, mix_turned_hbm, grad_hbm, x_hbm, weight_hbm,
                merged_in, to_natural, to_quarters, merged_natural, merged_windows,
                qkv_out, out_out, tokens_out, merged_out,
                q, k, v, mix, mix_grad, normed_turned, mix_turned, grad, x_in, qkv_weight,
                dq, dk, dv, g_x, g_y, g_z, g_p, g_r, normed_grad, units, merged_units, *rest):
    stream_buffers, (load, send, recv, strip_send, strip_recv) = rest[:-5], rest[-5:]

    def fetch(index, source, target):
        return pltpu.make_async_copy(source, target, load.at[index])

    def chunk_loads(chunk):
        columns = pl.ds(pl.multiple_of(chunk * 256, 256), 256)
        return [fetch(chunk * 5 + i, source.at[:, columns], target.at[:, columns]) for i, (source, target) in enumerate(
            ((q_hbm, q), (k_hbm, k), (v_hbm, v), (mix_hbm, mix), (mix_grad_hbm, mix_grad)))]

    normed_load, mix_load = fetch(20, normed_hbm, normed_turned), fetch(21, mix_turned_hbm, mix_turned)
    grad_load, weight_load, x_load = fetch(22, grad_hbm, grad), fetch(23, weight_hbm, qkv_weight), fetch(24, x_hbm, x_in)
    mix_load.start()
    grad_load.start()
    for copy in chunk_loads(0):
        copy.start()
    normed_load.start()

    @pl.loop(1, CHUNKS)
    def _(chunk):
        for copy in chunk_loads(chunk):
            copy.start()

    weight_load.start()
    x_load.start()

    x, y, z, core = place()
    here = (x, y, z)

    def moved(axis, step):
        there = list(here)
        there[axis] = (here[axis] + step) % 4
        return device_at(there[0], there[1], there[2], core)

    sibling = device_at(x, y, z, 1 - core)
    ring = [sibling] + [moved(axis, step) for axis in range(3) for step in (1, 2, 3)]
    before, after = neighbours(-1), neighbours(1)
    greet(ring + list(after), ring + list(before))

    units_in = dot(merged_windows[...], merged_in[...], TN).reshape(4, 6, 8, 1024)
    for i in range(4):
        merged_units[i, 0:6] = units_in[i]
    merged_copies = frame_copies(merged_units, (0, 0), (4, 6), strip_send, strip_recv, 0, before)
    for copy in merged_copies:
        copy.start()

    streams = ((g_x, ROUTES[0]), (g_y, ROUTES[1]), (g_z, ROUTES[2]), (g_p, ROUTES[3]), (g_r, ROUTES[4]))
    buffers = tuple(stream_buffers[7 * i:7 * i + 7] for i in range(5))

    def slot_of(kind, chunk):
        return chunk % 2 if kind < 3 else 0

    def core_copy(kind, chunk):
        return remote(streams[kind][0].at[slot_of(kind, chunk), :, 1 - core], buffers[kind][0].at[chunk],
                      send.at[kind, chunk, 0], recv.at[kind, chunk, 0], sibling)

    def level_refs(kind, chunk, level):
        acc = buffers[kind][1 + 2 * level].at[chunk]
        into = buffers[kind][2 + 2 * level].at[chunk]
        dims = "hzyl"
        for i in range(level):
            dims = left_over(dims, streams[kind][1][i])
        return acc, into, dims, streams[kind][1][level]

    def level_copies(kind, chunk, level):
        acc, into, dims, axis = level_refs(kind, chunk, level)
        return [remote(acc.at[blocks_at(dims, axis, (here[axis] + i + 1) % 4)], into.at[i],
                       send.at[kind, chunk, 1 + level * 3 + i], recv.at[kind, chunk, 1 + level * 3 + i],
                       moved(axis, i + 1)) for i in range(3)]

    def core_to_first(kind, chunk):
        core_copy(kind, chunk).wait_recv()
        g, (from_core, acc) = streams[kind][0], buffers[kind][:2]
        width = g.shape[-1]

        @pl.loop(0, 8)
        def _(i):
            blocks = pl.ds(i * 8, 8)
            total = g[slot_of(kind, chunk), blocks, core].astype(F32) + from_core[chunk, blocks].astype(F32)
            acc[chunk, i // 4, i % 4] = total.astype(BF16).reshape(4, 2, 16, width)

        for copy in level_copies(kind, chunk, 0):
            copy.start()

    def level_to_next(kind, chunk, level):
        for copy in level_copies(kind, chunk, level):
            copy.wait_recv()
        acc, into, dims, axis = level_refs(kind, chunk, level)
        total = acc[blocks_at(dims, axis, here[axis])].astype(F32)
        for i in range(3):
            total = total + into[i].astype(F32)
        if level < 2:
            buffers[kind][3 + 2 * level][chunk] = total.astype(BF16)
            for copy in level_copies(kind, chunk, level + 1):
                copy.start()
            return
        width = total.shape[-1]
        if kind < 3:
            low = pl.multiple_of(kind * 1024 + chunk * 256, 256)
            qkv_out[:, pl.ds(low, width)] = total[:8]
            qkv_out[:, pl.ds(pl.multiple_of(low + width, 128), width)] = total[8:]
        else:
            low = (kind - 3) * 512
            out_out[:, low:low + width] = total[:8]
            out_out[:, low + width:low + 2 * width] = total[8:]

    head_mask, group_mask = wide_masks()
    row8 = lax.broadcasted_iota(jnp.int32, (8, 256), 0)
    lane8 = lax.broadcasted_iota(jnp.int32, (8, 256), 1) // 32
    own_head = jnp.where(lane8 == row8, 1.0, 0.0).astype(BF16)
    edge = lax.axis_index("lat") == 0
    def put_terms(kind, chunk, i, terms):
        g = streams[kind][0]
        width = g.shape[-1]
        both = jnp.concatenate([terms[:, :, :width], terms[:, :, width:]], axis=1)
        pairs = terms.shape[0] // 2
        g[slot_of(kind, chunk), pl.ds(i * pairs, pairs)] = both.astype(BF16).reshape(pairs, 2, 16, width)

    def window_back(chunk, w):
        columns = pl.ds(pl.multiple_of(chunk * 256, 256), 256)
        rows = pl.ds(pl.multiple_of(w * 128, 128), 128)
        queries, keys, values = q[rows, columns], k[rows, columns], v[rows, columns]
        out_grad = mix_grad[rows, columns]
        product = (out_grad.astype(F32) * mix[rows, columns].astype(F32)).astype(BF16)
        spread_queries, spread_grads = stack(queries, group_mask), stack(out_grad, group_mask)
        weights = jnp.exp(dot(stack(keys, head_mask), spread_queries, NT) * SCALE)
        weights = jnp.where(other_region(512, 256, edge & (w < 3)), 0.0, weights)
        change = dot(stack(values, head_mask), spread_grads, NT)
        means = dot(own_head, product, NT)
        attention, scores_grad = [], []
        for head in range(4):
            part = weights[128 * head:128 * head + 128]
            part = part * (1.0 / jnp.sum(part, axis=0, keepdims=True))
            mean = jnp.concatenate([means[head:head + 1], means[4 + head:5 + head]], axis=1)
            attention.append(part.astype(BF16))
            scores_grad.append((part * (change[128 * head:128 * head + 128] - mean)).astype(BF16))
        dv[rows, columns] = select(dot(jnp.concatenate(attention, axis=0), spread_grads), head_mask).astype(BF16)
        dk[rows, columns] = (select(dot(jnp.concatenate(scores_grad, axis=0), spread_queries), head_mask)
                             * SCALE).astype(BF16)
        turned = keys.T
        pieces = []
        for group in range(2):
            for head in range(4):
                low = group * 128 + head * 32
                pieces.append(dot(turned[low:low + 32], scores_grad[head][:, group * 128:group * 128 + 128]))
        dq[rows, columns] = (jnp.concatenate(pieces, axis=0).T * SCALE).astype(BF16)

    mix_load.wait()
    grad_load.wait()

    @pl.loop(0, 4)
    def _(i):
        rows = pl.ds(pl.multiple_of(i * 256, 256), 256)
        for kind in (3, 4):
            low = (kind - 3) * 512
            put_terms(kind, 0, i, dot(mix_turned[rows], grad[:, low:low + 512]).reshape(32, 8, 512))

    for kind in (3, 4):
        core_copy(kind, 0).start()

    def finish_window(w):
        pieces = []
        for i in range(4):
            rows = pl.ds(pl.multiple_of(w * 128 + i * 32, 32), 32)
            change = normed_grad[rows].astype(BF16).astype(F32)
            centered, inverse = statistics(x_in[rows].astype(F32))
            normed = centered * inverse
            first = jnp.mean(change, axis=-1, keepdims=True)
            second = jnp.mean(change * normed, axis=-1, keepdims=True)
            value = (inverse * (change - first - normed * second)).astype(BF16).astype(F32) + grad[rows].astype(F32)
            pieces.append(value.astype(BF16))
        quarters = dot(to_quarters[...], jnp.concatenate(pieces, axis=0), TN).astype(BF16).reshape(4, 32, 1024)
        wa, wb = w // 3, w % 3
        for u in range(2):
            for side in range(2):
                units[2 * wa + u, 2 * wb + side] = quarters[2 * u + side]

    strips = frame_copies(units, (0, 0), (4, 6), strip_send, strip_recv, 3, before)

    @pl.loop(0, 8)
    def _(t):
        @pl.when(t < CHUNKS)
        def _():
            for copy in chunk_loads(t):
                copy.wait()

            @pl.loop(0, 2)
            def _(wa):
                for wb in range(3):
                    window_back(t, wa * 3 + wb)

        @pl.when((t == 4) | (t == 5))
        def _():
            @pl.when(t == 4)
            def _():
                weight_load.wait()
                x_load.wait()

            tokens = pl.ds(pl.multiple_of((t - 4) * 384, 384), 384)

            @pl.loop(0, 4)
            def _(i):
                rows = pl.ds(pl.multiple_of(i * 256, 256), 256)
                normed_grad[tokens, rows] = (dot(dq[tokens], qkv_weight[rows, 0:1024], NT)
                                             + dot(dk[tokens], qkv_weight[rows, 1024:2048], NT)
                                             + dot(dv[tokens], qkv_weight[rows, 2048:3072], NT))

            @pl.loop(0, 3)
            def _(wb):
                finish_window((t - 4) * 3 + wb)

                @pl.when((t == 5) & (wb == 0))
                def _():
                    strips[1].start()

            @pl.when(t == 4)
            def _():
                strips[0].start()
                strips[2].start()

        @pl.when(t == 6)
        def _():
            for copy in merged_copies:
                copy.wait_recv()
            framed = jnp.concatenate([merged_units[i, 1:7].reshape(48, 1024) for i in range(1, 5)], axis=0)
            merged_out[...] = dot(merged_natural[...], framed.astype(BF16)).astype(BF16)
            strips[1].wait_recv()

        @pl.when(t == 7)
        def _():
            strips[0].wait_recv()
            strips[2].wait_recv()

        @pl.when(t >= 6)
        def _():
            m = t - 6
            blocks = []
            for n in range(3):
                parts = [units[2 * m + 1 + u, 2 * n + 1 + side] for u in range(2) for side in range(2)]
                blocks.append(dot(to_natural[...], jnp.concatenate(parts, axis=0)).reshape(2, 8, 8, 1024))
            tokens_out[:, pl.ds(8 * m, 8)] = jnp.concatenate(blocks, axis=2).astype(BF16)

        for level in (2, 1, 0):
            chunk = t - 2 - level

            @pl.when((chunk >= 0) & (chunk < CHUNKS))
            def _():
                for kind in range(3):
                    level_to_next(kind, chunk, level)

        @pl.when((t >= 1) & (t <= CHUNKS))
        def _():
            for kind in range(3):
                core_to_first(kind, t - 1)

        @pl.when(t == 0)
        def _():
            for kind in (3, 4):
                core_to_first(kind, 0)

            normed_load.wait()

        for level in range(3):
            @pl.when(t == level + 2)
            def _():
                for kind in (3, 4):
                    level_to_next(kind, 0, level)

        @pl.when(t < CHUNKS)
        def _():
            @pl.when(t >= 2)
            def _():
                for kind in range(3):
                    core_copy(kind, t - 2).wait_send()

            columns = pl.ds(pl.multiple_of(t * 256, 256), 256)

            @pl.loop(0, 2)
            def _(i):
                rows = pl.ds(pl.multiple_of(i * 512, 512), 512)
                for kind, right in enumerate((dq, dk, dv)):
                    put_terms(kind, t, i, dot(normed_turned[rows], right[:, columns]).reshape(64, 8, 256))

            for kind in range(3):
                core_copy(kind, t).start()

    for kind in range(3):
        core_copy(kind, 2).wait_send()
        core_copy(kind, 3).wait_send()

    @pl.loop(0, CHUNKS)
    def _(chunk):
        for kind in range(3):
            for level in range(3):
                for copy in level_copies(kind, chunk, level):
                    copy.wait_send()

    for kind in (3, 4):
        core_copy(kind, 0).wait_send()
        for level in range(3):
            for copy in level_copies(kind, 0, level):
                copy.wait_send()
    for copy in merged_copies + strips:
        copy.wait_send()


def back(q, k, v, mix, mix_grad, normed_turned, mix_turned, grad, x, qkv_weight, merged_groups):
    buffers = []
    for route, count, width in zip(ROUTES, (CHUNKS,) * 3 + (1,) * 2, (128,) * 3 + (256,) * 2):
        first = left_over("hzyl", route[0])
        second = left_over(first, route[1])
        for shape in ((64,), (2, 4, 4, 2), (3, *sizes(first)), sizes(first), (3, *sizes(second)), sizes(second), (3,)):
            buffers.append(pltpu.VMEM((count, *shape, 16, width), BF16))
    vmem, anywhere = pl.BlockSpec(memory_space=pltpu.VMEM), pl.BlockSpec(memory_space=pl.ANY)
    tokens = pltpu.VMEM((768, 1024), BF16)
    turned = pltpu.VMEM((1024, 768), BF16)
    return pl.pallas_call(
        back_kernel,
        out_shape=(jax.ShapeDtypeStruct((8, 3072), F32), jax.ShapeDtypeStruct((8, 1024), F32),
                   jax.ShapeDtypeStruct((2, 16, 24, 1024), BF16), jax.ShapeDtypeStruct((192, 1024), BF16)),
        in_specs=[anywhere] * 10 + [vmem] * 5,
        out_specs=(vmem, vmem, vmem, vmem),
        scratch_shapes=[
            tokens, tokens, tokens, tokens, tokens, turned, turned, tokens, tokens, pltpu.VMEM((1024, 3072), BF16),
            tokens, tokens, tokens,
            *[pltpu.VMEM((2, 64, 2, 16, 128), BF16)] * 3, *[pltpu.VMEM((1, 64, 2, 16, 256), BF16)] * 2,
            pltpu.VMEM((768, 1024), F32),
            pltpu.VMEM((5, 7, 32, 1024), BF16),
            pltpu.VMEM((5, 7, 8, 1024), F32),
            *buffers,
            pltpu.SemaphoreType.DMA((25,)),
            pltpu.SemaphoreType.DMA((5, CHUNKS, 10)),
            pltpu.SemaphoreType.DMA((5, CHUNKS, 10)),
            pltpu.SemaphoreType.DMA((6,)),
            pltpu.SemaphoreType.DMA((6,)),
        ],
        compiler_params=pltpu.CompilerParams(collective_id=0, has_side_effects=True, vmem_limit_bytes=62 * MIB),
        name="back",
    )(q, k, v, mix, mix_grad, normed_turned, mix_turned, grad, x, qkv_weight, merged_groups, *orders())


def front_kernel(tokens, merged_grad, weight_hbm, out_weight_hbm, merge_weight_hbm,
                 to_natural, to_quarters, merged_natural, merged_windows,
                 x_hbm, normed_hbm, q_hbm, k_hbm, v_hbm, mix_hbm, mix_turned_hbm, grad_hbm, mix_grad_hbm, merged_out,
                 x, normed, normed_turned, q, k, v, mix, mix_turned, grad, mix_grad,
                 qkv_weight, out_weight, merge_weight, scaled, change, inverses, groups, units, merged_units,
                 load, store, send, recv):
    loads = [pltpu.make_async_copy(source, target, load.at[i]) for i, (source, target) in enumerate(
        ((weight_hbm, qkv_weight), (out_weight_hbm, out_weight), (merge_weight_hbm, merge_weight)))]
    for copy in loads:
        copy.start()
    before, after = neighbours(-1), neighbours(1)
    greet(before, after)
    copies = (frame_copies(units, (4, 6), (0, 0), send, recv, 0, after)
              + frame_copies(merged_units, (4, 6), (0, 0), send, recv, 3, after))

    @pl.loop(0, 32)
    def _(i):
        change[pl.ds(pl.multiple_of(i * 24, 8), 24)] = tokens[i // 16, i % 16].astype(F32)

    @pl.loop(0, 6)
    def _(i):
        m = jnp.where((i >= 1) & (i <= 3), 1, 0)
        n = jnp.where(i < 2, 2, 1 - i % 2)
        natural = [change[pl.ds(pl.multiple_of((level * 16 + 8 * m + row) * 24 + 8 * n, 8), 8)]
                   for level in range(2) for row in range(8)]
        quarters = dot(to_natural[...], jnp.concatenate(natural, axis=0).astype(BF16), TN)
        quarters = quarters.astype(BF16).reshape(4, 32, 1024)
        for u in range(2):
            for side in range(2):
                units[2 * m + 1 + u, 2 * n + 1 + side] = quarters[2 * u + side]

        @pl.when(i == 1)
        def _():
            copies[1].start()

        @pl.when(i == 3)
        def _():
            copies[0].start()
            copies[2].start()

    merged_in = dot(merged_natural[...], merged_grad[...], TN).reshape(4, 6, 8, 1024)
    for i in range(4):
        merged_units[i + 1, 1:7] = merged_in[i]
    for copy in copies[3:]:
        copy.start()

    def window(w):
        wa, wb = w // 3, w % 3
        quarters = [units[2 * wa + u, 2 * wb + side] for u in range(2) for side in range(2)]
        values = dot(to_quarters[...], jnp.concatenate(quarters, axis=0))
        rows = pl.ds(pl.multiple_of(w * 128, 128), 128)
        x[rows] = values.astype(BF16)
        for i in range(4):
            centered, inverse = statistics(values[32 * i:32 * i + 32])
            normed[pl.ds(pl.multiple_of(w * 128 + 32 * i, 32), 32)] = (centered * inverse).astype(BF16)
        normed_turned[:, rows] = normed[rows].T

    head_mask, group_mask = wide_masks()
    edge = lax.axis_index("lat") == 0

    def project(half, chunk):
        rows = pl.ds(pl.multiple_of(half * 384, 384), 384)
        columns = pl.ds(pl.multiple_of(chunk * 256, 256), 256)
        for third, target in enumerate((q, k, v)):
            low = pl.multiple_of(third * 1024 + chunk * 256, 256)
            target[rows, columns] = dot(normed[rows], qkv_weight[:, pl.ds(low, 256)]).astype(BF16)

    def attend(half, chunk):
        columns = pl.ds(pl.multiple_of(chunk * 256, 256), 256)
        for wb in range(3):
            rows = pl.ds(pl.multiple_of(half * 384 + wb * 128, 128), 128)
            scores = dot(stack(q[rows, columns], head_mask), stack(k[rows, columns], group_mask), NT)
            weights = jnp.exp(scores * SCALE)
            weights = jnp.where(other_region(512, 256, edge & (half == 0)), 0.0, weights)
            pieces = []
            for group in range(2):
                piece = weights[:, group * 128:group * 128 + 128]
                pieces.append((piece * (1.0 / jnp.sum(piece, axis=-1, keepdims=True))).astype(BF16))
            mixture = select(dot(jnp.concatenate(pieces, axis=1), stack(v[rows, columns], group_mask)), head_mask)
            mixture = mixture.astype(BF16)
            mix[rows, columns] = mixture
            mix_turned[columns, rows] = mixture.T

    keeps = [(x, x_hbm), (normed_turned, normed_hbm), (q, q_hbm), (k, k_hbm), (v, v_hbm), (mix, mix_hbm),
             (mix_turned, mix_turned_hbm), (grad, grad_hbm), (mix_grad, mix_grad_hbm)]
    stores = [pltpu.make_async_copy(source, target, store.at[i]) for i, (source, target) in enumerate(keeps)]

    @pl.loop(0, 2)
    def _(phase):
        half = 1 - phase

        @pl.loop(0, 3)
        def _(i):
            @pl.when((phase == 0) & (i == 2))
            def _():
                copies[1].wait_recv()

            @pl.when((phase == 1) & (i == 0))
            def _():
                copies[0].wait_recv()

            @pl.when((phase == 1) & (i == 2))
            def _():
                copies[2].wait_recv()

            window(half * 3 + (i + 1) % 3)

        @pl.when(phase == 0)
        def _():
            loads[0].wait()

        @pl.when(phase == 1)
        def _():
            stores[0].start()
            stores[1].start()

        project(half, 0)

        @pl.loop(0, 3)
        def _(chunk):
            project(half, chunk + 1)
            attend(half, chunk)

        attend(half, 3)

    for copy in stores[2:7]:
        copy.start()
    for copy in copies[3:]:
        copy.wait_recv()
    framed = jnp.concatenate([merged_units[i, 0:6].reshape(48, 1024) for i in range(4)], axis=0)
    groups[...] = dot(merged_windows[...], framed.astype(BF16)).astype(BF16)
    loads[1].wait()

    def add_branch(chunk):
        columns = pl.ds(pl.multiple_of(chunk * 256, 256), 256)
        scaled[:, columns] = x[:, columns].astype(F32) + dot(mix[...], out_weight[:, columns])

    pl.loop(0, 4)(add_branch)

    def quarter_rows(i):
        return [pl.ds(pl.multiple_of(i // 2 * 128 + j * 32 + i % 2 * 16, 16), 16) for j in range(4)]

    def group_rows(i):
        return [pl.ds(pl.multiple_of(j * 192 + i * 16, 16), 16) for j in range(4)]

    def normalize_groups(i):
        parts = [scaled[rows].astype(BF16).astype(F32) for rows in quarter_rows(i)]
        center = sum(jnp.sum(part, axis=-1, keepdims=True) for part in parts) * (1 / 4096)
        parts = [part - center for part in parts]
        spread = sum(jnp.sum(jnp.square(part), axis=-1, keepdims=True) for part in parts) * (1 / 4096)
        inverse = lax.rsqrt(spread + epsilon)
        inverses[pl.ds(pl.multiple_of(i * 16, 16), 16)] = jnp.broadcast_to(inverse, (16, 128))
        for part, rows in zip(parts, group_rows(i)):
            normed[rows] = (part * inverse).astype(BF16)
        for part, rows in zip(parts, quarter_rows(i)):
            scaled[rows] = part * inverse

    pl.loop(0, 12)(normalize_groups)
    loads[2].wait()

    def merge_columns(chunk):
        columns = pl.ds(pl.multiple_of(chunk * 256, 256), 256)
        total = dot(normed[0:192], merge_weight[0:1024, columns])
        for j in range(1, 4):
            total = total + dot(normed[192 * j:192 * j + 192], merge_weight[1024 * j:1024 * j + 1024, columns])
        merged_out[:, columns] = total.astype(BF16)
        for j in range(4):
            rows = pl.ds(pl.multiple_of(j * 1024 + chunk * 256, 256), 256)
            change[192 * j:192 * j + 192, columns] = dot(groups[...], merge_weight[rows], NT)

    pl.loop(0, 4)(merge_columns)

    def group_grads(i):
        changes = [change[rows].astype(BF16).astype(F32) for rows in group_rows(i)]
        values = [scaled[rows] for rows in quarter_rows(i)]
        first = sum(jnp.sum(part, axis=-1, keepdims=True) for part in changes) * (1 / 4096)
        second = sum(jnp.sum(part * value, axis=-1, keepdims=True) for part, value in zip(changes, values)) * (1 / 4096)
        inverse = inverses[pl.ds(pl.multiple_of(i * 16, 16), 16), 0:1]
        for part, value, rows in zip(changes, values, quarter_rows(i)):
            grad[rows] = (inverse * (part - first - value * second)).astype(BF16)

    pl.loop(0, 12)(group_grads)
    stores[7].start()

    def mixture_grads(chunk):
        rows = pl.ds(pl.multiple_of(chunk * 256, 256), 256)
        mix_grad[:, rows] = dot(grad[...], out_weight[rows], NT).astype(BF16)

    pl.loop(0, 4)(mixture_grads)
    stores[8].start()
    for copy in stores:
        copy.wait()
    for copy in copies:
        copy.wait_send()


def front(tokens, merged_grad, qkv_weight, out_weight, merge_weight):
    vmem, anywhere = pl.BlockSpec(memory_space=pltpu.VMEM), pl.BlockSpec(memory_space=pl.ANY)
    rows, turned = jax.ShapeDtypeStruct((768, 1024), BF16), jax.ShapeDtypeStruct((1024, 768), BF16)
    rows_vmem, turned_vmem = pltpu.VMEM((768, 1024), BF16), pltpu.VMEM((1024, 768), BF16)
    return pl.pallas_call(
        front_kernel,
        out_shape=(rows, turned, rows, rows, rows, rows, turned, rows, rows, jax.ShapeDtypeStruct((192, 1024), BF16)),
        in_specs=[vmem] * 2 + [anywhere] * 3 + [vmem] * 4,
        out_specs=(anywhere,) * 9 + (vmem,),
        scratch_shapes=[
            rows_vmem, rows_vmem, turned_vmem, rows_vmem, rows_vmem, rows_vmem, rows_vmem, turned_vmem, rows_vmem,
            rows_vmem,
            pltpu.VMEM((1024, 3072), BF16), pltpu.VMEM((1024, 1024), BF16), pltpu.VMEM((4096, 1024), BF16),
            pltpu.VMEM((768, 1024), F32), pltpu.VMEM((768, 1024), F32), pltpu.VMEM((192, 128), F32),
            pltpu.VMEM((192, 1024), BF16),
            pltpu.VMEM((5, 7, 32, 1024), BF16),
            pltpu.VMEM((5, 7, 8, 1024), F32),
            pltpu.SemaphoreType.DMA((3,)),
            pltpu.SemaphoreType.DMA((9,)),
            pltpu.SemaphoreType.DMA((6,)),
            pltpu.SemaphoreType.DMA((6,)),
        ],
        compiler_params=pltpu.CompilerParams(collective_id=1, has_side_effects=True, vmem_limit_bytes=62 * MIB),
        name="front",
    )(tokens, merged_grad, qkv_weight, out_weight, merge_weight, *orders())


def shards(tokens, qkv_weight, out_weight, merge_weight, merged_grad):
    x, normed_turned, q, k, v, mixture, mix_turned, grad, mixture_grad, merged_groups = front(
        tokens, merged_grad.transpose(0, 2, 1, 3).reshape(192, 1024), qkv_weight, out_weight, merge_weight)
    qkv_weight_grad, out_weight_grad, tokens_grad, merged = back(
        q, k, v, mixture, mixture_grad, normed_turned, mix_turned, grad, x, qkv_weight, merged_groups)
    merged = merged.reshape(2, 12, 8, 1024).transpose(0, 2, 1, 3)
    return (merged, tokens_grad, qkv_weight_grad, out_weight_grad)


def solution(mesh):
    in_specs = (P(None, "lat", "lon", None), P(), P(), P(), P(None, "lat", "lon", None))
    out_specs = (
        P(None, "lat", "lon", None),
        P(None, "lat", "lon", None),
        P(("lat", "lon"), None),
        P(("lat", "lon"), None),
    )
    return jax.shard_map(shards, mesh=mesh, in_specs=in_specs, out_specs=out_specs, check_vma=False)
```

```python
import jax
import jax.numpy as jnp
import numpy as np
from jax import lax
from jax.experimental import pallas as pl
from jax.experimental.pallas import tpu as pltpu
from jax.sharding import PartitionSpec as P

CHUNKS = 4
ROUTES = ((0, 1, 2), (1, 0, 2), (2, 1, 0), (0, 1, 2), (1, 0, 2))
MESH = pl.DeviceIdType.MESH
F32, BF16 = jnp.float32, jnp.bfloat16
epsilon = 1e-05
SCALE = 32 ** -0.5
MIB = 1024 * 1024
NT = (((1,), (1,)), ((), ()))
TN = (((0,), (0,)), ((), ()))


def dot(left, right, dims=(((1,), (0,)), ((), ()))):
    return lax.dot_general(left, right, dims, preferred_element_type=F32)


def picks(index):
    return (index[:, None] == np.arange(len(index))[None, :]).astype(np.float32)


def window_order():
    t = np.arange(128)
    quarter, level, a, b = t // 32, t // 16 % 2, t // 4 % 4, t % 4
    return picks((level * 8 + 2 * a + quarter % 2) * 8 + 2 * b + quarter // 2)


def orders():
    n = np.arange(128)
    level, i, j = n // 64, n // 8 % 8, n % 8
    to_natural = picks((((i // 4) * 2 + j // 4) * 2 + level) * 16 + (i % 4) * 4 + j % 4)
    to_quarters = window_order() @ to_natural
    n = np.arange(192)
    level, j, i = n // 96, n // 8 % 12, n % 8
    merged_natural = picks((((i // 2) * 6 + j // 2) * 2 + level) * 4 + (i % 2) * 2 + j % 2)
    window, level, a, b = n // 32, n // 16 % 2, n // 4 % 4, n % 4
    row, column = 2 * (window // 3) + a // 2, 2 * (window % 3) + b // 2
    merged_windows = picks(((row * 6 + column) * 2 + level) * 4 + (a % 2) * 2 + b % 2)
    return tuple(jnp.asarray(order, BF16) for order in (to_natural, to_quarters, merged_natural, merged_windows))


def statistics(values):
    center = jnp.mean(values, axis=-1, keepdims=True)
    shifted_values = values - center
    spread = jnp.mean(jnp.square(shifted_values), axis=-1, keepdims=True)
    return shifted_values, lax.rsqrt(spread + epsilon)


def place():
    lat, lon = lax.axis_index("lat"), lax.axis_index("lon")
    return (lat // 4) * 2 + (lon // 2) % 2, lon // 4, lat % 4, lon % 2


def device_at(x, y, z, core):
    return ((x // 2) * 4 + z, y * 4 + (x % 2) * 2 + core)


def neighbours(step):
    lat, lon = lax.axis_index("lat"), lax.axis_index("lon")
    lat_there, lon_there = (lat + step + 8) % 8, (lon + step + 16) % 16
    return (lat_there, lon), (lat, lon_there), (lat_there, lon_there)


def greet(receive_from, send_to):
    barrier = pltpu.get_barrier_semaphore()
    for device in receive_from:
        pl.semaphore_signal(barrier, inc=1, device_id=device, device_id_type=MESH)
    pl.semaphore_wait(barrier, len(send_to))


def remote(source, target, send, recv, device):
    return pltpu.make_async_remote_copy(src_ref=source, dst_ref=target, send_sem=send, recv_sem=recv,
                                        device_id=device, device_id_type=MESH)


def frame_copies(units, first, last, send, recv, base, devices):
    row, column, corner = devices
    return [remote(units.at[first[0], 1:6], units.at[last[0], 1:6], send.at[base], recv.at[base], row),
            remote(units.at[1:4, first[1]], units.at[1:4, last[1]], send.at[base + 1], recv.at[base + 1], column),
            remote(units.at[first[0], first[1]], units.at[last[0], last[1]], send.at[base + 2], recv.at[base + 2], corner)]


def blocks_at(dims, axis, p):
    index = ({"h": p // 2, "l": p % 2}, {"y": p}, {"z": p})[axis]
    return tuple(index.get(dim, slice(None)) for dim in dims)


def left_over(dims, axis):
    return "".join(dim for dim in dims if dim not in ("hl", "y", "z")[axis])


def sizes(dims):
    return tuple({"h": 2, "z": 4, "y": 4, "l": 2}[dim] for dim in dims)


def wide_masks():
    lane = lax.broadcasted_iota(jnp.int32, (128, 256), 1)
    return [lane % 128 // 32 == head for head in range(4)], [lane // 128 == group for group in range(2)]


def stack(values, masks):
    zero = jnp.zeros_like(values)
    return jnp.concatenate([jnp.where(mask, values, zero) for mask in masks], axis=0)


def select(stacked, masks):
    rows = [stacked[128 * head:128 * head + 128] for head in range(4)]
    return jnp.where(masks[0], rows[0], jnp.where(masks[1], rows[1], jnp.where(masks[2], rows[2], rows[3])))


def other_region(rows, columns, edge):
    row = (lax.broadcasted_iota(jnp.int32, (rows, 1), 0) // 4 % 4 < 2) & edge
    column = (lax.broadcasted_iota(jnp.int32, (1, columns), 1) // 4 % 4 < 2) & edge
    return row.astype(jnp.int32) != column.astype(jnp.int32)


def back_kernel(q_hbm, k_hbm, v_hbm, mix_hbm, mix_grad_hbm, normed_hbm, mix_turned_hbm, grad_hbm, x_hbm, weight_hbm,
                merged_in, to_natural, to_quarters, merged_natural, merged_windows,
                qkv_out, out_out, tokens_out, merged_out,
                q, k, v, mix, mix_grad, normed_turned, mix_turned, grad, x_in, qkv_weight,
                dq, dk, dv, g_x, g_y, g_z, g_p, g_r, normed_grad, units, merged_units, *rest):
    stream_buffers, (load, send, recv, strip_send, strip_recv) = rest[:-5], rest[-5:]

    def fetch(index, source, target):
        return pltpu.make_async_copy(source, target, load.at[index])

    def chunk_loads(chunk):
        columns = pl.ds(pl.multiple_of(chunk * 256, 256), 256)
        return [fetch(chunk * 5 + i, source.at[:, columns], target.at[:, columns]) for i, (source, target) in enumerate(
            ((q_hbm, q), (k_hbm, k), (v_hbm, v), (mix_hbm, mix), (mix_grad_hbm, mix_grad)))]

    normed_load, mix_load = fetch(20, normed_hbm, normed_turned), fetch(21, mix_turned_hbm, mix_turned)
    grad_load, weight_load, x_load = fetch(22, grad_hbm, grad), fetch(23, weight_hbm, qkv_weight), fetch(24, x_hbm, x_in)
    mix_load.start()
    grad_load.start()
    for copy in chunk_loads(0):
        copy.start()
    normed_load.start()

    @pl.loop(1, CHUNKS)
    def _(chunk):
        for copy in chunk_loads(chunk):
            copy.start()

    weight_load.start()
    x_load.start()

    x, y, z, core = place()
    here = (x, y, z)

    def moved(axis, step):
        there = list(here)
        there[axis] = (here[axis] + step) % 4
        return device_at(there[0], there[1], there[2], core)

    sibling = device_at(x, y, z, 1 - core)
    ring = [sibling] + [moved(axis, step) for axis in range(3) for step in (1, 2, 3)]
    before, after = neighbours(-1), neighbours(1)
    greet(ring + list(after), ring + list(before))

    units_in = dot(merged_windows[...], merged_in[...], TN).reshape(4, 6, 8, 1024)
    for i in range(4):
        merged_units[i, 0:6] = units_in[i]
    merged_copies = frame_copies(merged_units, (0, 0), (4, 6), strip_send, strip_recv, 0, before)
    for copy in merged_copies:
        copy.start()

    streams = ((g_x, ROUTES[0]), (g_y, ROUTES[1]), (g_z, ROUTES[2]), (g_p, ROUTES[3]), (g_r, ROUTES[4]))
    buffers = tuple(stream_buffers[7 * i:7 * i + 7] for i in range(5))

    def slot_of(kind, chunk):
        return chunk % 2 if kind < 3 else 0

    def core_copy(kind, chunk):
        return remote(streams[kind][0].at[slot_of(kind, chunk), :, 1 - core], buffers[kind][0].at[chunk],
                      send.at[kind, chunk, 0], recv.at[kind, chunk, 0], sibling)

    def level_refs(kind, chunk, level):
        acc = buffers[kind][1 + 2 * level].at[chunk]
        into = buffers[kind][2 + 2 * level].at[chunk]
        dims = "hzyl"
        for i in range(level):
            dims = left_over(dims, streams[kind][1][i])
        return acc, into, dims, streams[kind][1][level]

    def level_copies(kind, chunk, level):
        acc, into, dims, axis = level_refs(kind, chunk, level)
        return [remote(acc.at[blocks_at(dims, axis, (here[axis] + i + 1) % 4)], into.at[i],
                       send.at[kind, chunk, 1 + level * 3 + i], recv.at[kind, chunk, 1 + level * 3 + i],
                       moved(axis, i + 1)) for i in range(3)]

    def core_to_first(kind, chunk):
        core_copy(kind, chunk).wait_recv()
        g, (from_core, acc) = streams[kind][0], buffers[kind][:2]
        width = g.shape[-1]

        @pl.loop(0, 8)
        def _(i):
            blocks = pl.ds(i * 8, 8)
            total = g[slot_of(kind, chunk), blocks, core].astype(F32) + from_core[chunk, blocks].astype(F32)
            acc[chunk, i // 4, i % 4] = total.astype(BF16).reshape(4, 2, 16, width)

        for copy in level_copies(kind, chunk, 0):
            copy.start()

    def level_to_next(kind, chunk, level):
        for copy in level_copies(kind, chunk, level):
            copy.wait_recv()
        acc, into, dims, axis = level_refs(kind, chunk, level)
        total = acc[blocks_at(dims, axis, here[axis])].astype(F32)
        for i in range(3):
            total = total + into[i].astype(F32)
        if level < 2:
            buffers[kind][3 + 2 * level][chunk] = total.astype(BF16)
            for copy in level_copies(kind, chunk, level + 1):
                copy.start()
            return
        width = total.shape[-1]
        if kind < 3:
            low = pl.multiple_of(kind * 1024 + chunk * 256, 256)
            qkv_out[:, pl.ds(low, width)] = total[:8]
            qkv_out[:, pl.ds(pl.multiple_of(low + width, 128), width)] = total[8:]
        else:
            low = (kind - 3) * 512
            out_out[:, low:low + width] = total[:8]
            out_out[:, low + width:low + 2 * width] = total[8:]

    head_mask, group_mask = wide_masks()
    row8 = lax.broadcasted_iota(jnp.int32, (8, 256), 0)
    lane8 = lax.broadcasted_iota(jnp.int32, (8, 256), 1) // 32
    own_head = jnp.where(lane8 == row8, 1.0, 0.0).astype(BF16)
    edge = lax.axis_index("lat") == 0
    def put_terms(kind, chunk, i, terms):
        g = streams[kind][0]
        width = g.shape[-1]
        both = jnp.concatenate([terms[:, :, :width], terms[:, :, width:]], axis=1)
        pairs = terms.shape[0] // 2
        g[slot_of(kind, chunk), pl.ds(i * pairs, pairs)] = both.astype(BF16).reshape(pairs, 2, 16, width)

    def window_back(chunk, w):
        columns = pl.ds(pl.multiple_of(chunk * 256, 256), 256)
        rows = pl.ds(pl.multiple_of(w * 128, 128), 128)
        queries, keys, values = q[rows, columns], k[rows, columns], v[rows, columns]
        out_grad = mix_grad[rows, columns]
        product = (out_grad.astype(F32) * mix[rows, columns].astype(F32)).astype(BF16)
        spread_queries, spread_grads = stack(queries, group_mask), stack(out_grad, group_mask)
        weights = jnp.exp(dot(stack(keys, head_mask), spread_queries, NT) * SCALE)
        weights = jnp.where(other_region(512, 256, edge & (w < 3)), 0.0, weights)
        change = dot(stack(values, head_mask), spread_grads, NT)
        means = dot(own_head, product, NT)
        attention, scores_grad = [], []
        for head in range(4):
            part = weights[128 * head:128 * head + 128]
            part = part * (1.0 / jnp.sum(part, axis=0, keepdims=True))
            mean = jnp.concatenate([means[head:head + 1], means[4 + head:5 + head]], axis=1)
            attention.append(part.astype(BF16))
            scores_grad.append((part * (change[128 * head:128 * head + 128] - mean)).astype(BF16))
        dv[rows, columns] = select(dot(jnp.concatenate(attention, axis=0), spread_grads), head_mask).astype(BF16)
        dk[rows, columns] = (select(dot(jnp.concatenate(scores_grad, axis=0), spread_queries), head_mask)
                             * SCALE).astype(BF16)
        turned = keys.T
        pieces = []
        for group in range(2):
            for head in range(4):
                low = group * 128 + head * 32
                pieces.append(dot(turned[low:low + 32], scores_grad[head][:, group * 128:group * 128 + 128]))
        dq[rows, columns] = (jnp.concatenate(pieces, axis=0).T * SCALE).astype(BF16)

    mix_load.wait()
    grad_load.wait()

    @pl.loop(0, 4)
    def _(i):
        rows = pl.ds(pl.multiple_of(i * 256, 256), 256)
        for kind in (3, 4):
            low = (kind - 3) * 512
            put_terms(kind, 0, i, dot(mix_turned[rows], grad[:, low:low + 512]).reshape(32, 8, 512))

    for kind in (3, 4):
        core_copy(kind, 0).start()

    def finish_window(w):
        pieces = []
        for i in range(4):
            rows = pl.ds(pl.multiple_of(w * 128 + i * 32, 32), 32)
            change = normed_grad[rows].astype(BF16).astype(F32)
            centered, inverse = statistics(x_in[rows].astype(F32))
            normed = centered * inverse
            first = jnp.mean(change, axis=-1, keepdims=True)
            second = jnp.mean(change * normed, axis=-1, keepdims=True)
            value = (inverse * (change - first - normed * second)).astype(BF16).astype(F32) + grad[rows].astype(F32)
            pieces.append(value.astype(BF16))
        quarters = dot(to_quarters[...], jnp.concatenate(pieces, axis=0), TN).astype(BF16).reshape(4, 32, 1024)
        wa, wb = w // 3, w % 3
        for u in range(2):
            for side in range(2):
                units[2 * wa + u, 2 * wb + side] = quarters[2 * u + side]

    strips = frame_copies(units, (0, 0), (4, 6), strip_send, strip_recv, 3, before)

    @pl.loop(0, 8)
    def _(t):
        @pl.when(t < CHUNKS)
        def _():
            for copy in chunk_loads(t):
                copy.wait()

            @pl.loop(0, 2)
            def _(wa):
                for wb in range(3):
                    window_back(t, wa * 3 + wb)

        @pl.when((t == 4) | (t == 5))
        def _():
            @pl.when(t == 4)
            def _():
                weight_load.wait()
                x_load.wait()

            tokens = pl.ds(pl.multiple_of((t - 4) * 384, 384), 384)

            @pl.loop(0, 4)
            def _(i):
                rows = pl.ds(pl.multiple_of(i * 256, 256), 256)
                normed_grad[tokens, rows] = (dot(dq[tokens], qkv_weight[rows, 0:1024], NT)
                                             + dot(dk[tokens], qkv_weight[rows, 1024:2048], NT)
                                             + dot(dv[tokens], qkv_weight[rows, 2048:3072], NT))

            @pl.when(t == 4)
            def _():
                for kind in range(3):
                    core_to_first(kind, 3)

            @pl.when(t == 5)
            def _():
                for kind in range(3):
                    level_to_next(kind, 3, 0)

            @pl.loop(0, 3)
            def _(wb):
                finish_window((t - 4) * 3 + wb)

                @pl.when((t == 5) & (wb == 0))
                def _():
                    strips[1].start()

            @pl.when(t == 4)
            def _():
                strips[0].start()
                strips[2].start()

        @pl.when(t == 6)
        def _():
            for copy in merged_copies:
                copy.wait_recv()
            framed = jnp.concatenate([merged_units[i, 1:7].reshape(48, 1024) for i in range(1, 5)], axis=0)
            merged_out[...] = dot(merged_natural[...], framed.astype(BF16)).astype(BF16)
            for kind in range(3):
                level_to_next(kind, 3, 1)
            strips[1].wait_recv()

        @pl.when(t == 7)
        def _():
            strips[0].wait_recv()
            strips[2].wait_recv()

        @pl.when(t >= 6)
        def _():
            m = t - 6
            blocks = []
            for n in range(3):
                parts = [units[2 * m + 1 + u, 2 * n + 1 + side] for u in range(2) for side in range(2)]
                blocks.append(dot(to_natural[...], jnp.concatenate(parts, axis=0)).reshape(2, 8, 8, 1024))
            tokens_out[:, pl.ds(8 * m, 8)] = jnp.concatenate(blocks, axis=2).astype(BF16)

        for level in (2, 1, 0):
            chunk = t - 2 - level

            @pl.when((chunk >= 0) & (chunk < CHUNKS - (level < 2)))
            def _():
                for kind in range(3):
                    level_to_next(kind, chunk, level)

        @pl.when((t >= 1) & (t < CHUNKS))
        def _():
            for kind in range(3):
                core_to_first(kind, t - 1)

        @pl.when(t == 0)
        def _():
            for kind in (3, 4):
                core_to_first(kind, 0)

            normed_load.wait()

        for level in range(3):
            @pl.when(t == level + 2)
            def _():
                for kind in (3, 4):
                    level_to_next(kind, 0, level)

        @pl.when(t < CHUNKS)
        def _():
            @pl.when(t >= 2)
            def _():
                for kind in range(3):
                    core_copy(kind, t - 2).wait_send()

            columns = pl.ds(pl.multiple_of(t * 256, 256), 256)

            @pl.loop(0, 2)
            def _(i):
                rows = pl.ds(pl.multiple_of(i * 512, 512), 512)
                for kind, right in enumerate((dq, dk, dv)):
                    put_terms(kind, t, i, dot(normed_turned[rows], right[:, columns]).reshape(64, 8, 256))

            for kind in range(3):
                core_copy(kind, t).start()

    for kind in range(3):
        core_copy(kind, 2).wait_send()
        core_copy(kind, 3).wait_send()

    @pl.loop(0, CHUNKS)
    def _(chunk):
        for kind in range(3):
            for level in range(3):
                for copy in level_copies(kind, chunk, level):
                    copy.wait_send()

    for kind in (3, 4):
        core_copy(kind, 0).wait_send()
        for level in range(3):
            for copy in level_copies(kind, 0, level):
                copy.wait_send()
    for copy in merged_copies + strips:
        copy.wait_send()


def back(q, k, v, mix, mix_grad, normed_turned, mix_turned, grad, x, qkv_weight, merged_groups):
    buffers = []
    for route, count, width in zip(ROUTES, (CHUNKS,) * 3 + (1,) * 2, (128,) * 3 + (256,) * 2):
        first = left_over("hzyl", route[0])
        second = left_over(first, route[1])
        for shape in ((64,), (2, 4, 4, 2), (3, *sizes(first)), sizes(first), (3, *sizes(second)), sizes(second), (3,)):
            buffers.append(pltpu.VMEM((count, *shape, 16, width), BF16))
    vmem, anywhere = pl.BlockSpec(memory_space=pltpu.VMEM), pl.BlockSpec(memory_space=pl.ANY)
    tokens = pltpu.VMEM((768, 1024), BF16)
    turned = pltpu.VMEM((1024, 768), BF16)
    return pl.pallas_call(
        back_kernel,
        out_shape=(jax.ShapeDtypeStruct((8, 3072), F32), jax.ShapeDtypeStruct((8, 1024), F32),
                   jax.ShapeDtypeStruct((2, 16, 24, 1024), BF16), jax.ShapeDtypeStruct((192, 1024), BF16)),
        in_specs=[anywhere] * 10 + [vmem] * 5,
        out_specs=(vmem, vmem, vmem, vmem),
        scratch_shapes=[
            tokens, tokens, tokens, tokens, tokens, turned, turned, tokens, tokens, pltpu.VMEM((1024, 3072), BF16),
            tokens, tokens, tokens,
            *[pltpu.VMEM((2, 64, 2, 16, 128), BF16)] * 3, *[pltpu.VMEM((1, 64, 2, 16, 256), BF16)] * 2,
            pltpu.VMEM((768, 1024), F32),
            pltpu.VMEM((5, 7, 32, 1024), BF16),
            pltpu.VMEM((5, 7, 8, 1024), F32),
            *buffers,
            pltpu.SemaphoreType.DMA((25,)),
            pltpu.SemaphoreType.DMA((5, CHUNKS, 10)),
            pltpu.SemaphoreType.DMA((5, CHUNKS, 10)),
            pltpu.SemaphoreType.DMA((6,)),
            pltpu.SemaphoreType.DMA((6,)),
        ],
        compiler_params=pltpu.CompilerParams(collective_id=0, has_side_effects=True, vmem_limit_bytes=62 * MIB),
        name="back",
    )(q, k, v, mix, mix_grad, normed_turned, mix_turned, grad, x, qkv_weight, merged_groups, *orders())


def front_kernel(tokens, merged_grad, weight_hbm, out_weight_hbm, merge_weight_hbm,
                 to_natural, to_quarters, merged_natural, merged_windows,
                 x_hbm, normed_hbm, q_hbm, k_hbm, v_hbm, mix_hbm, mix_turned_hbm, grad_hbm, mix_grad_hbm, merged_out,
                 x, normed, normed_turned, q, k, v, mix, mix_turned, grad, mix_grad,
                 qkv_weight, out_weight, merge_weight, merge_normed, scaled, change, inverses, groups, units, merged_units,
                 load, store, send, recv):
    loads = [pltpu.make_async_copy(source, target, load.at[i]) for i, (source, target) in enumerate(
        ((weight_hbm, qkv_weight), (out_weight_hbm, out_weight), (merge_weight_hbm, merge_weight)))]
    for copy in loads:
        copy.start()
    before, after = neighbours(-1), neighbours(1)
    greet(before, after)
    copies = (frame_copies(units, (4, 6), (0, 0), send, recv, 0, after)
              + frame_copies(merged_units, (4, 6), (0, 0), send, recv, 3, after))

    @pl.loop(0, 32)
    def _(i):
        change[pl.ds(pl.multiple_of(i * 24, 8), 24)] = tokens[i // 16, i % 16].astype(F32)

    @pl.loop(0, 6)
    def _(i):
        m = jnp.where((i >= 1) & (i <= 3), 1, 0)
        n = jnp.where(i < 2, 2, 1 - i % 2)
        natural = [change[pl.ds(pl.multiple_of((level * 16 + 8 * m + row) * 24 + 8 * n, 8), 8)]
                   for level in range(2) for row in range(8)]
        quarters = dot(to_natural[...], jnp.concatenate(natural, axis=0).astype(BF16), TN)
        quarters = quarters.astype(BF16).reshape(4, 32, 1024)
        for u in range(2):
            for side in range(2):
                units[2 * m + 1 + u, 2 * n + 1 + side] = quarters[2 * u + side]

        @pl.when(i == 1)
        def _():
            copies[1].start()

        @pl.when(i == 3)
        def _():
            copies[0].start()
            copies[2].start()

    merged_in = dot(merged_natural[...], merged_grad[...], TN).reshape(4, 6, 8, 1024)
    for i in range(4):
        merged_units[i + 1, 1:7] = merged_in[i]
    for copy in copies[3:]:
        copy.start()

    def window(w):
        wa, wb = w // 3, w % 3
        quarters = [units[2 * wa + u, 2 * wb + side] for u in range(2) for side in range(2)]
        values = dot(to_quarters[...], jnp.concatenate(quarters, axis=0))
        rows = pl.ds(pl.multiple_of(w * 128, 128), 128)
        x[rows] = values.astype(BF16)
        for i in range(4):
            centered, inverse = statistics(values[32 * i:32 * i + 32])
            normed[pl.ds(pl.multiple_of(w * 128 + 32 * i, 32), 32)] = (centered * inverse).astype(BF16)
        normed_turned[:, rows] = normed[rows].T

    head_mask, group_mask = wide_masks()
    edge = lax.axis_index("lat") == 0

    def project(half, chunk):
        rows = pl.ds(pl.multiple_of(half * 384, 384), 384)
        columns = pl.ds(pl.multiple_of(chunk * 256, 256), 256)
        for third, target in enumerate((q, k, v)):
            low = pl.multiple_of(third * 1024 + chunk * 256, 256)
            target[rows, columns] = dot(normed[rows], qkv_weight[:, pl.ds(low, 256)]).astype(BF16)

    def attend(half, chunk):
        columns = pl.ds(pl.multiple_of(chunk * 256, 256), 256)
        for wb in range(3):
            rows = pl.ds(pl.multiple_of(half * 384 + wb * 128, 128), 128)
            scores = dot(stack(q[rows, columns], head_mask), stack(k[rows, columns], group_mask), NT)
            weights = jnp.exp(scores * SCALE)
            weights = jnp.where(other_region(512, 256, edge & (half == 0)), 0.0, weights)
            pieces = []
            for group in range(2):
                piece = weights[:, group * 128:group * 128 + 128]
                pieces.append((piece * (1.0 / jnp.sum(piece, axis=-1, keepdims=True))).astype(BF16))
            mixture = select(dot(jnp.concatenate(pieces, axis=1), stack(v[rows, columns], group_mask)), head_mask)
            mixture = mixture.astype(BF16)
            mix[rows, columns] = mixture
            mix_turned[columns, rows] = mixture.T

    keeps = [(x, x_hbm), (normed_turned, normed_hbm), (q, q_hbm), (k, k_hbm), (v, v_hbm), (mix, mix_hbm),
             (mix_turned, mix_turned_hbm), (grad, grad_hbm), (mix_grad, mix_grad_hbm)]
    stores = [pltpu.make_async_copy(source, target, store.at[i]) for i, (source, target) in enumerate(keeps)]

    def add_branch(half, chunk):
        rows = pl.ds(pl.multiple_of(half * 384, 384), 384)
        columns = pl.ds(pl.multiple_of(chunk * 256, 256), 256)
        scaled[rows, columns] = x[rows, columns].astype(F32) + dot(mix[rows], out_weight[:, columns])

    def quarter_rows(i):
        return [pl.ds(pl.multiple_of(i // 2 * 128 + j * 32 + i % 2 * 16, 16), 16) for j in range(4)]

    def group_rows(i):
        return [pl.ds(pl.multiple_of(j * 192 + i * 16, 16), 16) for j in range(4)]

    def normalize_groups(i):
        parts = [scaled[rows].astype(BF16).astype(F32) for rows in quarter_rows(i)]
        center = sum(jnp.sum(part, axis=-1, keepdims=True) for part in parts) * (1 / 4096)
        parts = [part - center for part in parts]
        spread = sum(jnp.sum(jnp.square(part), axis=-1, keepdims=True) for part in parts) * (1 / 4096)
        inverse = lax.rsqrt(spread + epsilon)
        inverses[pl.ds(pl.multiple_of(i * 16, 16), 16)] = jnp.broadcast_to(inverse, (16, 128))
        for part, rows in zip(parts, group_rows(i)):
            merge_normed[rows] = (part * inverse).astype(BF16)
        for part, rows in zip(parts, quarter_rows(i)):
            scaled[rows] = part * inverse

    @pl.loop(0, 2)
    def _(phase):
        half = 1 - phase

        @pl.loop(0, 3)
        def _(i):
            @pl.when((phase == 0) & (i == 2))
            def _():
                copies[1].wait_recv()

            @pl.when((phase == 1) & (i == 0))
            def _():
                copies[0].wait_recv()

            @pl.when((phase == 1) & (i == 2))
            def _():
                copies[2].wait_recv()

            window(half * 3 + (i + 1) % 3)

        @pl.when(phase == 0)
        def _():
            loads[0].wait()

        @pl.when(phase == 1)
        def _():
            stores[0].start()
            stores[1].start()

        project(half, 0)

        @pl.loop(0, 3)
        def _(chunk):
            project(half, chunk + 1)
            attend(half, chunk)

        attend(half, 3)

        @pl.when(phase == 0)
        def _():
            loads[1].wait()

        @pl.loop(0, 4)
        def _(chunk):
            add_branch(half, chunk)

        @pl.loop(0, 6)
        def _(i):
            normalize_groups(half * 6 + i)

    for copy in stores[2:7]:
        copy.start()
    for copy in copies[3:]:
        copy.wait_recv()
    framed = jnp.concatenate([merged_units[i, 0:6].reshape(48, 1024) for i in range(4)], axis=0)
    groups[...] = dot(merged_windows[...], framed.astype(BF16)).astype(BF16)
    loads[2].wait()

    def merge_columns(chunk):
        columns = pl.ds(pl.multiple_of(chunk * 256, 256), 256)
        total = dot(merge_normed[0:192], merge_weight[0:1024, columns])
        for j in range(1, 4):
            total = total + dot(merge_normed[192 * j:192 * j + 192], merge_weight[1024 * j:1024 * j + 1024, columns])
        merged_out[:, columns] = total.astype(BF16)
        for j in range(4):
            rows = pl.ds(pl.multiple_of(j * 1024 + chunk * 256, 256), 256)
            change[192 * j:192 * j + 192, columns] = dot(groups[...], merge_weight[rows], NT)

    pl.loop(0, 4)(merge_columns)

    def group_grads(i):
        changes = [change[rows].astype(BF16).astype(F32) for rows in group_rows(i)]
        values = [scaled[rows] for rows in quarter_rows(i)]
        first = sum(jnp.sum(part, axis=-1, keepdims=True) for part in changes) * (1 / 4096)
        second = sum(jnp.sum(part * value, axis=-1, keepdims=True) for part, value in zip(changes, values)) * (1 / 4096)
        inverse = inverses[pl.ds(pl.multiple_of(i * 16, 16), 16), 0:1]
        for part, value, rows in zip(changes, values, quarter_rows(i)):
            grad[rows] = (inverse * (part - first - value * second)).astype(BF16)

    pl.loop(0, 12)(group_grads)
    stores[7].start()

    def mixture_grads(chunk):
        rows = pl.ds(pl.multiple_of(chunk * 256, 256), 256)
        mix_grad[:, rows] = dot(grad[...], out_weight[rows], NT).astype(BF16)

    pl.loop(0, 4)(mixture_grads)
    stores[8].start()
    for copy in stores:
        copy.wait()
    for copy in copies:
        copy.wait_send()


def front(tokens, merged_grad, qkv_weight, out_weight, merge_weight):
    vmem, anywhere = pl.BlockSpec(memory_space=pltpu.VMEM), pl.BlockSpec(memory_space=pl.ANY)
    rows, turned = jax.ShapeDtypeStruct((768, 1024), BF16), jax.ShapeDtypeStruct((1024, 768), BF16)
    rows_vmem, turned_vmem = pltpu.VMEM((768, 1024), BF16), pltpu.VMEM((1024, 768), BF16)
    return pl.pallas_call(
        front_kernel,
        out_shape=(rows, turned, rows, rows, rows, rows, turned, rows, rows, jax.ShapeDtypeStruct((192, 1024), BF16)),
        in_specs=[vmem] * 2 + [anywhere] * 3 + [vmem] * 4,
        out_specs=(anywhere,) * 9 + (vmem,),
        scratch_shapes=[
            rows_vmem, rows_vmem, turned_vmem, rows_vmem, rows_vmem, rows_vmem, rows_vmem, turned_vmem, rows_vmem,
            rows_vmem,
            pltpu.VMEM((1024, 3072), BF16), pltpu.VMEM((1024, 1024), BF16), pltpu.VMEM((4096, 1024), BF16), rows_vmem,
            pltpu.VMEM((768, 1024), F32), pltpu.VMEM((768, 1024), F32), pltpu.VMEM((192, 128), F32),
            pltpu.VMEM((192, 1024), BF16),
            pltpu.VMEM((5, 7, 32, 1024), BF16),
            pltpu.VMEM((5, 7, 8, 1024), F32),
            pltpu.SemaphoreType.DMA((3,)),
            pltpu.SemaphoreType.DMA((9,)),
            pltpu.SemaphoreType.DMA((6,)),
            pltpu.SemaphoreType.DMA((6,)),
        ],
        compiler_params=pltpu.CompilerParams(collective_id=1, has_side_effects=True, vmem_limit_bytes=62 * MIB),
        name="front",
    )(tokens, merged_grad, qkv_weight, out_weight, merge_weight, *orders())


def shards(tokens, qkv_weight, out_weight, merge_weight, merged_grad):
    x, normed_turned, q, k, v, mixture, mix_turned, grad, mixture_grad, merged_groups = front(
        tokens, merged_grad.transpose(0, 2, 1, 3).reshape(192, 1024), qkv_weight, out_weight, merge_weight)
    qkv_weight_grad, out_weight_grad, tokens_grad, merged = back(
        q, k, v, mixture, mixture_grad, normed_turned, mix_turned, grad, x, qkv_weight, merged_groups)
    merged = merged.reshape(2, 12, 8, 1024).transpose(0, 2, 1, 3)
    return (merged, tokens_grad, qkv_weight_grad, out_weight_grad)


def solution(mesh):
    in_specs = (P(None, "lat", "lon", None), P(), P(), P(), P(None, "lat", "lon", None))
    out_specs = (
        P(None, "lat", "lon", None),
        P(None, "lat", "lon", None),
        P(("lat", "lon"), None),
        P(("lat", "lon"), None),
    )
    return jax.shard_map(shards, mesh=mesh, in_specs=in_specs, out_specs=out_specs, check_vma=False)
```

```python
import jax
import jax.numpy as jnp
import numpy as np
from jax import lax
from jax.experimental import pallas as pl
from jax.experimental.pallas import tpu as pltpu
from jax.sharding import PartitionSpec as P

CHUNKS = 4
ROUTES = ((0, 1, 2), (1, 0, 2), (2, 1, 0), (0, 1, 2), (1, 0, 2))
MESH = pl.DeviceIdType.MESH
F32, BF16 = jnp.float32, jnp.bfloat16
epsilon = 1e-05
SCALE = 32 ** -0.5
MIB = 1024 * 1024
NT = (((1,), (1,)), ((), ()))
TN = (((0,), (0,)), ((), ()))


def dot(left, right, dims=(((1,), (0,)), ((), ()))):
    return lax.dot_general(left, right, dims, preferred_element_type=F32)


def picks(index):
    return (index[:, None] == np.arange(len(index))[None, :]).astype(np.float32)


def window_order():
    t = np.arange(128)
    quarter, level, a, b = t // 32, t // 16 % 2, t // 4 % 4, t % 4
    return picks((level * 8 + 2 * a + quarter % 2) * 8 + 2 * b + quarter // 2)


def orders():
    n = np.arange(128)
    level, i, j = n // 64, n // 8 % 8, n % 8
    to_natural = picks((((i // 4) * 2 + j // 4) * 2 + level) * 16 + (i % 4) * 4 + j % 4)
    to_quarters = window_order() @ to_natural
    n = np.arange(192)
    level, j, i = n // 96, n // 8 % 12, n % 8
    merged_natural = picks((((i // 2) * 6 + j // 2) * 2 + level) * 4 + (i % 2) * 2 + j % 2)
    window, level, a, b = n // 32, n // 16 % 2, n // 4 % 4, n % 4
    row, column = 2 * (window // 3) + a // 2, 2 * (window % 3) + b // 2
    merged_windows = picks(((row * 6 + column) * 2 + level) * 4 + (a % 2) * 2 + b % 2)
    return tuple(jnp.asarray(order, BF16) for order in (to_natural, to_quarters, merged_natural, merged_windows))


def statistics(values):
    center = jnp.mean(values, axis=-1, keepdims=True)
    shifted_values = values - center
    spread = jnp.mean(jnp.square(shifted_values), axis=-1, keepdims=True)
    return shifted_values, lax.rsqrt(spread + epsilon)


def place():
    lat, lon = lax.axis_index("lat"), lax.axis_index("lon")
    return (lat // 4) * 2 + (lon // 2) % 2, lon // 4, lat % 4, lon % 2


def device_at(x, y, z, core):
    return ((x // 2) * 4 + z, y * 4 + (x % 2) * 2 + core)


def neighbours(step):
    lat, lon = lax.axis_index("lat"), lax.axis_index("lon")
    lat_there, lon_there = (lat + step + 8) % 8, (lon + step + 16) % 16
    return (lat_there, lon), (lat, lon_there), (lat_there, lon_there)


def greet(receive_from):
    barrier = pltpu.get_barrier_semaphore()
    for device in receive_from:
        pl.semaphore_signal(barrier, inc=1, device_id=device, device_id_type=MESH)


def await_greetings(send_to):
    pl.semaphore_wait(pltpu.get_barrier_semaphore(), len(send_to))


def remote(source, target, send, recv, device):
    return pltpu.make_async_remote_copy(src_ref=source, dst_ref=target, send_sem=send, recv_sem=recv,
                                        device_id=device, device_id_type=MESH)


def frame_copies(units, first, last, send, recv, base, devices):
    row, column, corner = devices
    return [remote(units.at[first[0], 1:6], units.at[last[0], 1:6], send.at[base], recv.at[base], row),
            remote(units.at[1:4, first[1]], units.at[1:4, last[1]], send.at[base + 1], recv.at[base + 1], column),
            remote(units.at[first[0], first[1]], units.at[last[0], last[1]], send.at[base + 2], recv.at[base + 2], corner)]


def blocks_at(dims, axis, p):
    index = ({"h": p // 2, "l": p % 2}, {"y": p}, {"z": p})[axis]
    return tuple(index.get(dim, slice(None)) for dim in dims)


def left_over(dims, axis):
    return "".join(dim for dim in dims if dim not in ("hl", "y", "z")[axis])


def sizes(dims):
    return tuple({"h": 2, "z": 4, "y": 4, "l": 2}[dim] for dim in dims)


def wide_masks():
    lane = lax.broadcasted_iota(jnp.int32, (128, 256), 1)
    return [lane % 128 // 32 == head for head in range(4)], [lane // 128 == group for group in range(2)]


def stack(values, masks):
    zero = jnp.zeros_like(values)
    return jnp.concatenate([jnp.where(mask, values, zero) for mask in masks], axis=0)


def select(stacked, masks):
    rows = [stacked[128 * head:128 * head + 128] for head in range(4)]
    return jnp.where(masks[0], rows[0], jnp.where(masks[1], rows[1], jnp.where(masks[2], rows[2], rows[3])))


def other_region(rows, columns, edge):
    row = (lax.broadcasted_iota(jnp.int32, (rows, 1), 0) // 4 % 4 < 2) & edge
    column = (lax.broadcasted_iota(jnp.int32, (1, columns), 1) // 4 % 4 < 2) & edge
    return row.astype(jnp.int32) != column.astype(jnp.int32)


def back_kernel(q_hbm, k_hbm, v_hbm, mix_hbm, mix_grad_hbm, normed_hbm, mix_turned_hbm, grad_hbm, x_hbm, weight_hbm,
                merged_in, to_natural, to_quarters, merged_natural, merged_windows,
                qkv_out, out_out, tokens_out, merged_out,
                q, k, v, mix, mix_grad, normed_turned, mix_turned, grad, x_in, qkv_weight,
                dq, dk, dv, g_x, g_y, g_z, g_p, g_r, normed_grad, units, merged_units, *rest):
    stream_buffers, (load, send, recv, strip_send, strip_recv) = rest[:-5], rest[-5:]

    def fetch(index, source, target):
        return pltpu.make_async_copy(source, target, load.at[index])

    def chunk_loads(chunk):
        columns = pl.ds(pl.multiple_of(chunk * 256, 256), 256)
        return [fetch(chunk * 5 + i, source.at[:, columns], target.at[:, columns]) for i, (source, target) in enumerate(
            ((q_hbm, q), (k_hbm, k), (v_hbm, v), (mix_hbm, mix), (mix_grad_hbm, mix_grad)))]

    normed_load, mix_load = fetch(20, normed_hbm, normed_turned), fetch(21, mix_turned_hbm, mix_turned)
    grad_load, weight_load, x_load = fetch(22, grad_hbm, grad), fetch(23, weight_hbm, qkv_weight), fetch(24, x_hbm, x_in)
    for copy in chunk_loads(0):
        copy.start()
    mix_load.start()
    grad_load.start()
    normed_load.start()

    @pl.loop(1, CHUNKS)
    def _(chunk):
        for copy in chunk_loads(chunk):
            copy.start()

    weight_load.start()
    x_load.start()

    x, y, z, core = place()
    here = (x, y, z)

    def moved(axis, step):
        there = list(here)
        there[axis] = (here[axis] + step) % 4
        return device_at(there[0], there[1], there[2], core)

    sibling = device_at(x, y, z, 1 - core)
    ring = [sibling] + [moved(axis, step) for axis in range(3) for step in (1, 2, 3)]
    before, after = neighbours(-1), neighbours(1)
    greet(ring + list(after))

    units_in = dot(merged_windows[...], merged_in[...], TN).reshape(4, 6, 8, 1024)
    for i in range(4):
        merged_units[i, 0:6] = units_in[i]
    merged_copies = frame_copies(merged_units, (0, 0), (4, 6), strip_send, strip_recv, 0, before)
    streams = ((g_x, ROUTES[0]), (g_y, ROUTES[1]), (g_z, ROUTES[2]), (g_p, ROUTES[3]), (g_r, ROUTES[4]))
    buffers = tuple(stream_buffers[7 * i:7 * i + 7] for i in range(5))

    def slot_of(kind, chunk):
        return chunk % 2 if kind < 3 else 0

    def core_copy(kind, chunk):
        return remote(streams[kind][0].at[slot_of(kind, chunk), :, 1 - core], buffers[kind][0].at[chunk],
                      send.at[kind, chunk, 0], recv.at[kind, chunk, 0], sibling)

    def level_refs(kind, chunk, level):
        acc = buffers[kind][1 + 2 * level].at[chunk]
        into = buffers[kind][2 + 2 * level].at[chunk]
        dims = "hzyl"
        for i in range(level):
            dims = left_over(dims, streams[kind][1][i])
        return acc, into, dims, streams[kind][1][level]

    def level_copies(kind, chunk, level):
        acc, into, dims, axis = level_refs(kind, chunk, level)
        return [remote(acc.at[blocks_at(dims, axis, (here[axis] + i + 1) % 4)], into.at[i],
                       send.at[kind, chunk, 1 + level * 3 + i], recv.at[kind, chunk, 1 + level * 3 + i],
                       moved(axis, i + 1)) for i in range(3)]

    def core_to_first(kind, chunk):
        core_copy(kind, chunk).wait_recv()
        g, (from_core, acc) = streams[kind][0], buffers[kind][:2]
        width = g.shape[-1]

        @pl.loop(0, 8)
        def _(i):
            blocks = pl.ds(i * 8, 8)
            total = g[slot_of(kind, chunk), blocks, core].astype(F32) + from_core[chunk, blocks].astype(F32)
            acc[chunk, i // 4, i % 4] = total.astype(BF16).reshape(4, 2, 16, width)

        for copy in level_copies(kind, chunk, 0):
            copy.start()

    def level_to_next(kind, chunk, level):
        for copy in level_copies(kind, chunk, level):
            copy.wait_recv()
        acc, into, dims, axis = level_refs(kind, chunk, level)
        total = acc[blocks_at(dims, axis, here[axis])].astype(F32)
        for i in range(3):
            total = total + into[i].astype(F32)
        if level < 2:
            buffers[kind][3 + 2 * level][chunk] = total.astype(BF16)
            for copy in level_copies(kind, chunk, level + 1):
                copy.start()
            return
        width = total.shape[-1]
        if kind < 3:
            low = pl.multiple_of(kind * 1024 + chunk * 256, 256)
            qkv_out[:, pl.ds(low, width)] = total[:8]
            qkv_out[:, pl.ds(pl.multiple_of(low + width, 128), width)] = total[8:]
        else:
            low = (kind - 3) * 512
            out_out[:, low:low + width] = total[:8]
            out_out[:, low + width:low + 2 * width] = total[8:]

    head_mask, group_mask = wide_masks()
    row8 = lax.broadcasted_iota(jnp.int32, (8, 256), 0)
    lane8 = lax.broadcasted_iota(jnp.int32, (8, 256), 1) // 32
    own_head = jnp.where(lane8 == row8, 1.0, 0.0).astype(BF16)
    edge = lax.axis_index("lat") == 0
    def put_terms(kind, chunk, i, terms):
        g = streams[kind][0]
        width = g.shape[-1]
        both = jnp.concatenate([terms[:, :, :width], terms[:, :, width:]], axis=1)
        pairs = terms.shape[0] // 2
        g[slot_of(kind, chunk), pl.ds(i * pairs, pairs)] = both.astype(BF16).reshape(pairs, 2, 16, width)

    def window_back(chunk, w):
        columns = pl.ds(pl.multiple_of(chunk * 256, 256), 256)
        rows = pl.ds(pl.multiple_of(w * 128, 128), 128)
        queries, keys, values = q[rows, columns], k[rows, columns], v[rows, columns]
        out_grad = mix_grad[rows, columns]
        product = (out_grad.astype(F32) * mix[rows, columns].astype(F32)).astype(BF16)
        spread_queries, spread_grads = stack(queries, group_mask), stack(out_grad, group_mask)
        weights = jnp.exp(dot(stack(keys, head_mask), spread_queries, NT) * SCALE)
        weights = jnp.where(other_region(512, 256, edge & (w < 3)), 0.0, weights)
        change = dot(stack(values, head_mask), spread_grads, NT)
        means = dot(own_head, product, NT)
        attention, scores_grad = [], []
        for head in range(4):
            part = weights[128 * head:128 * head + 128]
            part = part * (1.0 / jnp.sum(part, axis=0, keepdims=True))
            mean = jnp.concatenate([means[head:head + 1], means[4 + head:5 + head]], axis=1)
            attention.append(part.astype(BF16))
            scores_grad.append((part * (change[128 * head:128 * head + 128] - mean)).astype(BF16))
        dv[rows, columns] = select(dot(jnp.concatenate(attention, axis=0), spread_grads), head_mask).astype(BF16)
        dk[rows, columns] = (select(dot(jnp.concatenate(scores_grad, axis=0), spread_queries), head_mask)
                             * SCALE).astype(BF16)
        turned = keys.T
        pieces = []
        for group in range(2):
            for head in range(4):
                low = group * 128 + head * 32
                pieces.append(dot(turned[low:low + 32], scores_grad[head][:, group * 128:group * 128 + 128]))
        dq[rows, columns] = (jnp.concatenate(pieces, axis=0).T * SCALE).astype(BF16)

    def finish_window(w):
        pieces = []
        for i in range(4):
            rows = pl.ds(pl.multiple_of(w * 128 + i * 32, 32), 32)
            change = normed_grad[rows].astype(BF16).astype(F32)
            centered, inverse = statistics(x_in[rows].astype(F32))
            normed = centered * inverse
            first = jnp.mean(change, axis=-1, keepdims=True)
            second = jnp.mean(change * normed, axis=-1, keepdims=True)
            value = (inverse * (change - first - normed * second)).astype(BF16).astype(F32) + grad[rows].astype(F32)
            pieces.append(value.astype(BF16))
        quarters = dot(to_quarters[...], jnp.concatenate(pieces, axis=0), TN).astype(BF16).reshape(4, 32, 1024)
        wa, wb = w // 3, w % 3
        for u in range(2):
            for side in range(2):
                units[2 * wa + u, 2 * wb + side] = quarters[2 * u + side]

    strips = frame_copies(units, (0, 0), (4, 6), strip_send, strip_recv, 3, before)

    @pl.loop(0, 8)
    def _(t):
        @pl.when(t < CHUNKS)
        def _():
            for copy in chunk_loads(t):
                copy.wait()

            @pl.loop(0, 2)
            def _(wa):
                for wb in range(3):
                    window_back(t, wa * 3 + wb)

        @pl.when(t == 0)
        def _():
            await_greetings(ring + list(before))
            for copy in merged_copies:
                copy.start()
            mix_load.wait()
            grad_load.wait()

            @pl.loop(0, 4)
            def _(i):
                rows = pl.ds(pl.multiple_of(i * 256, 256), 256)
                for kind in (3, 4):
                    low = (kind - 3) * 512
                    put_terms(kind, 0, i, dot(mix_turned[rows], grad[:, low:low + 512]).reshape(32, 8, 512))

            for kind in (3, 4):
                core_copy(kind, 0).start()

            normed_load.wait()

        @pl.when((t == 4) | (t == 5))
        def _():
            @pl.when(t == 4)
            def _():
                weight_load.wait()
                x_load.wait()

            tokens = pl.ds(pl.multiple_of((t - 4) * 384, 384), 384)

            @pl.loop(0, 4)
            def _(i):
                rows = pl.ds(pl.multiple_of(i * 256, 256), 256)
                normed_grad[tokens, rows] = (dot(dq[tokens], qkv_weight[rows, 0:1024], NT)
                                             + dot(dk[tokens], qkv_weight[rows, 1024:2048], NT)
                                             + dot(dv[tokens], qkv_weight[rows, 2048:3072], NT))

            @pl.when(t == 4)
            def _():
                for kind in range(3):
                    core_to_first(kind, 3)

            @pl.when(t == 5)
            def _():
                for kind in range(3):
                    level_to_next(kind, 3, 0)

            @pl.loop(0, 3)
            def _(wb):
                finish_window((t - 4) * 3 + wb)

                @pl.when((t == 5) & (wb == 0))
                def _():
                    strips[1].start()

            @pl.when(t == 4)
            def _():
                strips[0].start()
                strips[2].start()

        @pl.when(t == 6)
        def _():
            for copy in merged_copies:
                copy.wait_recv()
            framed = jnp.concatenate([merged_units[i, 1:7].reshape(48, 1024) for i in range(1, 5)], axis=0)
            merged_out[...] = dot(merged_natural[...], framed.astype(BF16)).astype(BF16)
            for kind in range(3):
                level_to_next(kind, 3, 1)
            strips[1].wait_recv()

        @pl.when(t == 7)
        def _():
            strips[0].wait_recv()
            strips[2].wait_recv()

        @pl.when(t >= 6)
        def _():
            m = t - 6
            blocks = []
            for n in range(3):
                parts = [units[2 * m + 1 + u, 2 * n + 1 + side] for u in range(2) for side in range(2)]
                blocks.append(dot(to_natural[...], jnp.concatenate(parts, axis=0)).reshape(2, 8, 8, 1024))
            tokens_out[:, pl.ds(8 * m, 8)] = jnp.concatenate(blocks, axis=2).astype(BF16)

        for level in (2, 1, 0):
            chunk = t - 2 - level

            @pl.when((chunk >= 0) & (chunk < CHUNKS - (level < 2)))
            def _():
                for kind in range(3):
                    level_to_next(kind, chunk, level)

        @pl.when((t >= 1) & (t < CHUNKS))
        def _():
            for kind in range(3):
                core_to_first(kind, t - 1)

        @pl.when(t == 1)
        def _():
            for kind in (3, 4):
                core_to_first(kind, 0)

        for level in range(3):
            @pl.when(t == level + 3)
            def _():
                for kind in (3, 4):
                    level_to_next(kind, 0, level)

        @pl.when(t < CHUNKS)
        def _():
            @pl.when(t >= 2)
            def _():
                for kind in range(3):
                    core_copy(kind, t - 2).wait_send()

            columns = pl.ds(pl.multiple_of(t * 256, 256), 256)

            @pl.loop(0, 2)
            def _(i):
                rows = pl.ds(pl.multiple_of(i * 512, 512), 512)
                for kind, right in enumerate((dq, dk, dv)):
                    put_terms(kind, t, i, dot(normed_turned[rows], right[:, columns]).reshape(64, 8, 256))

            for kind in range(3):
                core_copy(kind, t).start()

    for kind in range(3):
        core_copy(kind, 2).wait_send()
        core_copy(kind, 3).wait_send()

    @pl.loop(0, CHUNKS)
    def _(chunk):
        for kind in range(3):
            for level in range(3):
                for copy in level_copies(kind, chunk, level):
                    copy.wait_send()

    for kind in (3, 4):
        core_copy(kind, 0).wait_send()
        for level in range(3):
            for copy in level_copies(kind, 0, level):
                copy.wait_send()
    for copy in merged_copies + strips:
        copy.wait_send()


def back(q, k, v, mix, mix_grad, normed_turned, mix_turned, grad, x, qkv_weight, merged_groups):
    buffers = []
    for route, count, width in zip(ROUTES, (CHUNKS,) * 3 + (1,) * 2, (128,) * 3 + (256,) * 2):
        first = left_over("hzyl", route[0])
        second = left_over(first, route[1])
        for shape in ((64,), (2, 4, 4, 2), (3, *sizes(first)), sizes(first), (3, *sizes(second)), sizes(second), (3,)):
            buffers.append(pltpu.VMEM((count, *shape, 16, width), BF16))
    vmem, anywhere = pl.BlockSpec(memory_space=pltpu.VMEM), pl.BlockSpec(memory_space=pl.ANY)
    tokens = pltpu.VMEM((768, 1024), BF16)
    turned = pltpu.VMEM((1024, 768), BF16)
    return pl.pallas_call(
        back_kernel,
        out_shape=(jax.ShapeDtypeStruct((8, 3072), F32), jax.ShapeDtypeStruct((8, 1024), F32),
                   jax.ShapeDtypeStruct((2, 16, 24, 1024), BF16), jax.ShapeDtypeStruct((192, 1024), BF16)),
        in_specs=[anywhere] * 10 + [vmem] * 5,
        out_specs=(vmem, vmem, vmem, vmem),
        scratch_shapes=[
            tokens, tokens, tokens, tokens, tokens, turned, turned, tokens, tokens, pltpu.VMEM((1024, 3072), BF16),
            tokens, tokens, tokens,
            *[pltpu.VMEM((2, 64, 2, 16, 128), BF16)] * 3, *[pltpu.VMEM((1, 64, 2, 16, 256), BF16)] * 2,
            pltpu.VMEM((768, 1024), F32),
            pltpu.VMEM((5, 7, 32, 1024), BF16),
            pltpu.VMEM((5, 7, 8, 1024), F32),
            *buffers,
            pltpu.SemaphoreType.DMA((25,)),
            pltpu.SemaphoreType.DMA((5, CHUNKS, 10)),
            pltpu.SemaphoreType.DMA((5, CHUNKS, 10)),
            pltpu.SemaphoreType.DMA((6,)),
            pltpu.SemaphoreType.DMA((6,)),
        ],
        compiler_params=pltpu.CompilerParams(collective_id=0, has_side_effects=True, vmem_limit_bytes=62 * MIB),
        name="back",
    )(q, k, v, mix, mix_grad, normed_turned, mix_turned, grad, x, qkv_weight, merged_groups, *orders())


def place_kernel(tokens, merged, qkv, out, tokens_out, merged_out, qkv_out, out_out, done):
    copies = [pltpu.make_async_copy(tokens.at[i // 2, pl.ds(i % 2 * 8, 8)], tokens_out.at[i // 2, pl.ds(i % 2 * 8, 8)],
                                    done.at[i]) for i in range(4)]
    copies += [pltpu.make_async_copy(merged, merged_out, done.at[4]), pltpu.make_async_copy(qkv, qkv_out, done.at[5]),
               pltpu.make_async_copy(out, out_out, done.at[6])]
    for copy in copies:
        copy.start()
    for copy in copies:
        copy.wait()


def place_results(*results):
    anywhere = pl.BlockSpec(memory_space=pl.ANY)
    return pl.pallas_call(
        place_kernel,
        out_shape=tuple(jax.ShapeDtypeStruct(result.shape, result.dtype) for result in results),
        in_specs=[anywhere] * 4,
        out_specs=(anywhere,) * 4,
        scratch_shapes=[pltpu.SemaphoreType.DMA((7,))],
        compiler_params=pltpu.CompilerParams(vmem_limit_bytes=62 * MIB),
        name="place_results",
    )(*results)


def front_kernel(tokens, merged_grad, weight_hbm, out_weight_hbm, merge_weight_hbm,
                 to_natural, to_quarters, merged_natural, merged_windows,
                 x_hbm, normed_hbm, q_hbm, k_hbm, v_hbm, mix_hbm, mix_turned_hbm, grad_hbm, mix_grad_hbm, merged_out,
                 x, normed, normed_turned, q, k, v, mix, mix_turned, grad, mix_grad,
                 qkv_weight, out_weight, merge_weight, merge_normed, scaled, change, inverses, groups, units, merged_units,
                 load, store, send, recv):
    loads = [pltpu.make_async_copy(source, target, load.at[i]) for i, (source, target) in enumerate(
        ((weight_hbm, qkv_weight), (out_weight_hbm, out_weight), (merge_weight_hbm, merge_weight)))]
    for copy in loads:
        copy.start()
    before, after = neighbours(-1), neighbours(1)
    greet(before)
    copies = (frame_copies(units, (4, 6), (0, 0), send, recv, 0, after)
              + frame_copies(merged_units, (4, 6), (0, 0), send, recv, 3, after))

    @pl.loop(0, 32)
    def _(i):
        change[pl.ds(pl.multiple_of(i * 24, 8), 24)] = tokens[i // 16, i % 16].astype(F32)

    await_greetings(after)

    @pl.loop(0, 6)
    def _(i):
        m = jnp.where((i >= 1) & (i <= 3), 1, 0)
        n = jnp.where(i < 2, 2, 1 - i % 2)
        natural = [change[pl.ds(pl.multiple_of((level * 16 + 8 * m + row) * 24 + 8 * n, 8), 8)]
                   for level in range(2) for row in range(8)]
        quarters = dot(to_natural[...], jnp.concatenate(natural, axis=0).astype(BF16), TN)
        quarters = quarters.astype(BF16).reshape(4, 32, 1024)
        for u in range(2):
            for side in range(2):
                units[2 * m + 1 + u, 2 * n + 1 + side] = quarters[2 * u + side]

        @pl.when(i == 1)
        def _():
            copies[1].start()

        @pl.when(i == 3)
        def _():
            copies[0].start()
            copies[2].start()

    merged_in = dot(merged_natural[...], merged_grad[...], TN).reshape(4, 6, 8, 1024)
    for i in range(4):
        merged_units[i + 1, 1:7] = merged_in[i]
    for copy in copies[3:]:
        copy.start()

    def window(w):
        wa, wb = w // 3, w % 3
        quarters = [units[2 * wa + u, 2 * wb + side] for u in range(2) for side in range(2)]
        values = dot(to_quarters[...], jnp.concatenate(quarters, axis=0))
        rows = pl.ds(pl.multiple_of(w * 128, 128), 128)
        x[rows] = values.astype(BF16)
        for i in range(4):
            centered, inverse = statistics(values[32 * i:32 * i + 32])
            normed[pl.ds(pl.multiple_of(w * 128 + 32 * i, 32), 32)] = (centered * inverse).astype(BF16)
        normed_turned[:, rows] = normed[rows].T

    head_mask, group_mask = wide_masks()
    edge = lax.axis_index("lat") == 0

    def project(half, chunk):
        rows = pl.ds(pl.multiple_of(half * 384, 384), 384)
        columns = pl.ds(pl.multiple_of(chunk * 256, 256), 256)
        for third, target in enumerate((q, k, v)):
            low = pl.multiple_of(third * 1024 + chunk * 256, 256)
            target[rows, columns] = dot(normed[rows], qkv_weight[:, pl.ds(low, 256)]).astype(BF16)

    def attend(half, chunk):
        columns = pl.ds(pl.multiple_of(chunk * 256, 256), 256)
        for wb in range(3):
            rows = pl.ds(pl.multiple_of(half * 384 + wb * 128, 128), 128)
            scores = dot(stack(q[rows, columns], head_mask), stack(k[rows, columns], group_mask), NT)
            weights = jnp.exp(scores * SCALE)
            weights = jnp.where(other_region(512, 256, edge & (half == 0)), 0.0, weights)
            pieces = []
            for group in range(2):
                piece = weights[:, group * 128:group * 128 + 128]
                pieces.append((piece * (1.0 / jnp.sum(piece, axis=-1, keepdims=True))).astype(BF16))
            mixture = select(dot(jnp.concatenate(pieces, axis=1), stack(v[rows, columns], group_mask)), head_mask)
            mixture = mixture.astype(BF16)
            mix[rows, columns] = mixture
            mix_turned[columns, rows] = mixture.T

    keeps = [(x, x_hbm), (normed_turned, normed_hbm), (q, q_hbm), (k, k_hbm), (v, v_hbm), (mix, mix_hbm),
             (mix_turned, mix_turned_hbm), (grad, grad_hbm), (mix_grad, mix_grad_hbm)]
    stores = [pltpu.make_async_copy(source, target, store.at[i]) for i, (source, target) in enumerate(keeps)]

    def add_branch(half, chunk):
        rows = pl.ds(pl.multiple_of(half * 384, 384), 384)
        columns = pl.ds(pl.multiple_of(chunk * 256, 256), 256)
        scaled[rows, columns] = x[rows, columns].astype(F32) + dot(mix[rows], out_weight[:, columns])

    def quarter_rows(i):
        return [pl.ds(pl.multiple_of(i // 2 * 128 + j * 32 + i % 2 * 16, 16), 16) for j in range(4)]

    def group_rows(i):
        return [pl.ds(pl.multiple_of(j * 192 + i * 16, 16), 16) for j in range(4)]

    def normalize_groups(i):
        parts = [scaled[rows].astype(BF16).astype(F32) for rows in quarter_rows(i)]
        center = sum(jnp.sum(part, axis=-1, keepdims=True) for part in parts) * (1 / 4096)
        parts = [part - center for part in parts]
        spread = sum(jnp.sum(jnp.square(part), axis=-1, keepdims=True) for part in parts) * (1 / 4096)
        inverse = lax.rsqrt(spread + epsilon)
        inverses[pl.ds(pl.multiple_of(i * 16, 16), 16)] = jnp.broadcast_to(inverse, (16, 128))
        for part, rows in zip(parts, group_rows(i)):
            merge_normed[rows] = (part * inverse).astype(BF16)
        for part, rows in zip(parts, quarter_rows(i)):
            scaled[rows] = part * inverse

    @pl.loop(0, 2)
    def _(phase):
        half = 1 - phase

        @pl.loop(0, 3)
        def _(i):
            @pl.when((phase == 0) & (i == 2))
            def _():
                copies[1].wait_recv()

            @pl.when((phase == 1) & (i == 0))
            def _():
                copies[0].wait_recv()

            @pl.when((phase == 1) & (i == 2))
            def _():
                copies[2].wait_recv()

            window(half * 3 + (i + 1) % 3)

        @pl.when(phase == 0)
        def _():
            loads[0].wait()

        @pl.when(phase == 1)
        def _():
            stores[0].start()
            stores[1].start()

        project(half, 0)

        @pl.loop(0, 3)
        def _(chunk):
            project(half, chunk + 1)
            attend(half, chunk)

        attend(half, 3)

        @pl.when(phase == 0)
        def _():
            loads[1].wait()

        @pl.loop(0, 4)
        def _(chunk):
            add_branch(half, chunk)

        @pl.loop(0, 6)
        def _(i):
            normalize_groups(half * 6 + i)

    for copy in stores[2:7]:
        copy.start()
    for copy in copies[3:]:
        copy.wait_recv()
    framed = jnp.concatenate([merged_units[i, 0:6].reshape(48, 1024) for i in range(4)], axis=0)
    groups[...] = dot(merged_windows[...], framed.astype(BF16)).astype(BF16)
    loads[2].wait()

    def merge_columns(chunk):
        columns = pl.ds(pl.multiple_of(chunk * 256, 256), 256)
        total = dot(merge_normed[0:192], merge_weight[0:1024, columns])
        for j in range(1, 4):
            total = total + dot(merge_normed[192 * j:192 * j + 192], merge_weight[1024 * j:1024 * j + 1024, columns])
        merged_out[:, columns] = total.astype(BF16)
        for j in range(4):
            rows = pl.ds(pl.multiple_of(j * 1024 + chunk * 256, 256), 256)
            change[192 * j:192 * j + 192, columns] = dot(groups[...], merge_weight[rows], NT)

    pl.loop(0, 4)(merge_columns)

    def group_grads(i):
        changes = [change[rows].astype(BF16).astype(F32) for rows in group_rows(i)]
        values = [scaled[rows] for rows in quarter_rows(i)]
        first = sum(jnp.sum(part, axis=-1, keepdims=True) for part in changes) * (1 / 4096)
        second = sum(jnp.sum(part * value, axis=-1, keepdims=True) for part, value in zip(changes, values)) * (1 / 4096)
        inverse = inverses[pl.ds(pl.multiple_of(i * 16, 16), 16), 0:1]
        for part, value, rows in zip(changes, values, quarter_rows(i)):
            grad[rows] = (inverse * (part - first - value * second)).astype(BF16)

    pl.loop(0, 12)(group_grads)
    stores[7].start()

    def mixture_grads(chunk):
        rows = pl.ds(pl.multiple_of(chunk * 256, 256), 256)
        mix_grad[:, rows] = dot(grad[...], out_weight[rows], NT).astype(BF16)

    pl.loop(0, 4)(mixture_grads)
    stores[8].start()
    for copy in stores:
        copy.wait()
    for copy in copies:
        copy.wait_send()


def front(tokens, merged_grad, qkv_weight, out_weight, merge_weight):
    vmem, anywhere = pl.BlockSpec(memory_space=pltpu.VMEM), pl.BlockSpec(memory_space=pl.ANY)
    rows, turned = jax.ShapeDtypeStruct((768, 1024), BF16), jax.ShapeDtypeStruct((1024, 768), BF16)
    rows_vmem, turned_vmem = pltpu.VMEM((768, 1024), BF16), pltpu.VMEM((1024, 768), BF16)
    return pl.pallas_call(
        front_kernel,
        out_shape=(rows, turned, rows, rows, rows, rows, turned, rows, rows, jax.ShapeDtypeStruct((192, 1024), BF16)),
        in_specs=[vmem] * 2 + [anywhere] * 3 + [vmem] * 4,
        out_specs=(anywhere,) * 9 + (vmem,),
        scratch_shapes=[
            rows_vmem, rows_vmem, turned_vmem, rows_vmem, rows_vmem, rows_vmem, rows_vmem, turned_vmem, rows_vmem,
            rows_vmem,
            pltpu.VMEM((1024, 3072), BF16), pltpu.VMEM((1024, 1024), BF16), pltpu.VMEM((4096, 1024), BF16), rows_vmem,
            pltpu.VMEM((768, 1024), F32), pltpu.VMEM((768, 1024), F32), pltpu.VMEM((192, 128), F32),
            pltpu.VMEM((192, 1024), BF16),
            pltpu.VMEM((5, 7, 32, 1024), BF16),
            pltpu.VMEM((5, 7, 8, 1024), F32),
            pltpu.SemaphoreType.DMA((3,)),
            pltpu.SemaphoreType.DMA((9,)),
            pltpu.SemaphoreType.DMA((6,)),
            pltpu.SemaphoreType.DMA((6,)),
        ],
        compiler_params=pltpu.CompilerParams(collective_id=1, has_side_effects=True, vmem_limit_bytes=62 * MIB),
        name="front",
    )(tokens, merged_grad, qkv_weight, out_weight, merge_weight, *orders())


def shards(tokens, qkv_weight, out_weight, merge_weight, merged_grad):
    x, normed_turned, q, k, v, mixture, mix_turned, grad, mixture_grad, merged_groups = front(
        tokens, merged_grad.transpose(0, 2, 1, 3).reshape(192, 1024), qkv_weight, out_weight, merge_weight)
    qkv_weight_grad, out_weight_grad, tokens_grad, merged = back(
        q, k, v, mixture, mixture_grad, normed_turned, mix_turned, grad, x, qkv_weight, merged_groups)
    tokens_grad, merged, qkv_weight_grad, out_weight_grad = place_results(
        tokens_grad, merged, qkv_weight_grad, out_weight_grad)
    merged = merged.reshape(2, 12, 8, 1024).transpose(0, 2, 1, 3)
    return (merged, tokens_grad, qkv_weight_grad, out_weight_grad)


def solution(mesh):
    in_specs = (P(None, "lat", "lon", None), P(), P(), P(), P(None, "lat", "lon", None))
    out_specs = (
        P(None, "lat", "lon", None),
        P(None, "lat", "lon", None),
        P(("lat", "lon"), None),
        P(("lat", "lon"), None),
    )
    return jax.shard_map(shards, mesh=mesh, in_specs=in_specs, out_specs=out_specs, check_vma=False)
```

```python
import jax
import jax.numpy as jnp
import numpy as np
from jax import lax
from jax.experimental import pallas as pl
from jax.experimental.pallas import tpu as pltpu
from jax.sharding import PartitionSpec as P

CHUNKS = 4
ROUTES = ((0, 1, 2), (1, 0, 2), (2, 1, 0), (0, 1, 2), (1, 0, 2))
MESH = pl.DeviceIdType.MESH
F32, BF16 = jnp.float32, jnp.bfloat16
epsilon = 1e-05
SCALE = 32 ** -0.5
MIB = 1024 * 1024
NT = (((1,), (1,)), ((), ()))
TN = (((0,), (0,)), ((), ()))


def dot(left, right, dims=(((1,), (0,)), ((), ()))):
    return lax.dot_general(left, right, dims, preferred_element_type=F32)


def picks(index):
    return (index[:, None] == np.arange(len(index))[None, :]).astype(np.float32)


def window_order():
    t = np.arange(128)
    quarter, level, a, b = t // 32, t // 16 % 2, t // 4 % 4, t % 4
    return picks((level * 8 + 2 * a + quarter % 2) * 8 + 2 * b + quarter // 2)


def orders():
    n = np.arange(128)
    level, i, j = n // 64, n // 8 % 8, n % 8
    to_natural = picks((((i // 4) * 2 + j // 4) * 2 + level) * 16 + (i % 4) * 4 + j % 4)
    to_quarters = window_order() @ to_natural
    n = np.arange(192)
    level, j, i = n // 96, n // 8 % 12, n % 8
    merged_natural = picks((((i // 2) * 6 + j // 2) * 2 + level) * 4 + (i % 2) * 2 + j % 2)
    window, level, a, b = n // 32, n // 16 % 2, n // 4 % 4, n % 4
    row, column = 2 * (window // 3) + a // 2, 2 * (window % 3) + b // 2
    merged_windows = picks(((row * 6 + column) * 2 + level) * 4 + (a % 2) * 2 + b % 2)
    return tuple(jnp.asarray(order, BF16) for order in (to_natural, to_quarters, merged_natural, merged_windows))


def statistics(values):
    center = jnp.mean(values, axis=-1, keepdims=True)
    shifted_values = values - center
    spread = jnp.mean(jnp.square(shifted_values), axis=-1, keepdims=True)
    return shifted_values, lax.rsqrt(spread + epsilon)


def place():
    lat, lon = lax.axis_index("lat"), lax.axis_index("lon")
    return (lat // 4) * 2 + (lon // 2) % 2, lon // 4, lat % 4, lon % 2


def device_at(x, y, z, core):
    return ((x // 2) * 4 + z, y * 4 + (x % 2) * 2 + core)


def neighbours(step):
    lat, lon = lax.axis_index("lat"), lax.axis_index("lon")
    lat_there, lon_there = (lat + step + 8) % 8, (lon + step + 16) % 16
    return (lat_there, lon), (lat, lon_there), (lat_there, lon_there)


def greet(receive_from):
    barrier = pltpu.get_barrier_semaphore()
    for device in receive_from:
        pl.semaphore_signal(barrier, inc=1, device_id=device, device_id_type=MESH)


def await_greetings(send_to):
    pl.semaphore_wait(pltpu.get_barrier_semaphore(), len(send_to))


def remote(source, target, send, recv, device):
    return pltpu.make_async_remote_copy(src_ref=source, dst_ref=target, send_sem=send, recv_sem=recv,
                                        device_id=device, device_id_type=MESH)


def frame_copies(units, first, last, send, recv, base, devices):
    row, column, corner = devices
    return [remote(units.at[first[0], 1:6], units.at[last[0], 1:6], send.at[base], recv.at[base], row),
            remote(units.at[1:4, first[1]], units.at[1:4, last[1]], send.at[base + 1], recv.at[base + 1], column),
            remote(units.at[first[0], first[1]], units.at[last[0], last[1]], send.at[base + 2], recv.at[base + 2], corner)]


def blocks_at(dims, axis, p):
    index = ({"h": p // 2, "l": p % 2}, {"y": p}, {"z": p})[axis]
    return tuple(index.get(dim, slice(None)) for dim in dims)


def left_over(dims, axis):
    return "".join(dim for dim in dims if dim not in ("hl", "y", "z")[axis])


def sizes(dims):
    return tuple({"h": 2, "z": 4, "y": 4, "l": 2}[dim] for dim in dims)


def wide_masks():
    lane = lax.broadcasted_iota(jnp.int32, (128, 256), 1)
    return [lane % 128 // 32 == head for head in range(4)], [lane // 128 == group for group in range(2)]


def stack(values, masks):
    zero = jnp.zeros_like(values)
    return jnp.concatenate([jnp.where(mask, values, zero) for mask in masks], axis=0)


def select(stacked, masks):
    rows = [stacked[128 * head:128 * head + 128] for head in range(4)]
    return jnp.where(masks[0], rows[0], jnp.where(masks[1], rows[1], jnp.where(masks[2], rows[2], rows[3])))


def other_region(rows, columns, edge):
    row = (lax.broadcasted_iota(jnp.int32, (rows, 1), 0) // 4 % 4 < 2) & edge
    column = (lax.broadcasted_iota(jnp.int32, (1, columns), 1) // 4 % 4 < 2) & edge
    return row.astype(jnp.int32) != column.astype(jnp.int32)


def back_kernel(q_hbm, k_hbm, v_hbm, mix_hbm, mix_grad_hbm, normed_hbm, mix_turned_hbm, grad_hbm, x_hbm, weight_hbm,
                merged_in, to_natural, to_quarters, merged_natural, merged_windows,
                qkv_out, out_out, tokens_out, merged_out,
                q, k, v, mix, mix_grad, normed_turned, mix_turned, grad, x_in, qkv_weight,
                dq, dk, dv, g_x, g_y, g_z, g_p, g_r, normed_grad, units, merged_units, *rest):
    stream_buffers, (load, send, recv, strip_send, strip_recv) = rest[:-5], rest[-5:]

    def fetch(index, source, target):
        return pltpu.make_async_copy(source, target, load.at[index])

    def chunk_loads(chunk):
        columns = pl.ds(pl.multiple_of(chunk * 256, 256), 256)
        return [fetch(chunk * 5 + i, source.at[:, columns], target.at[:, columns]) for i, (source, target) in enumerate(
            ((q_hbm, q), (k_hbm, k), (v_hbm, v), (mix_hbm, mix), (mix_grad_hbm, mix_grad)))]

    normed_load, mix_load = fetch(20, normed_hbm, normed_turned), fetch(21, mix_turned_hbm, mix_turned)
    grad_load, weight_load, x_load = fetch(22, grad_hbm, grad), fetch(23, weight_hbm, qkv_weight), fetch(24, x_hbm, x_in)
    for copy in chunk_loads(0):
        copy.start()
    mix_load.start()
    grad_load.start()
    normed_load.start()

    @pl.loop(1, CHUNKS)
    def _(chunk):
        for copy in chunk_loads(chunk):
            copy.start()

    weight_load.start()
    x_load.start()

    x, y, z, core = place()
    here = (x, y, z)

    def moved(axis, step):
        there = list(here)
        there[axis] = (here[axis] + step) % 4
        return device_at(there[0], there[1], there[2], core)

    sibling = device_at(x, y, z, 1 - core)
    ring = [sibling] + [moved(axis, step) for axis in range(3) for step in (1, 2, 3)]
    before, after = neighbours(-1), neighbours(1)
    greet(ring + list(after))

    units_in = dot(merged_windows[...], merged_in[...], TN).reshape(4, 6, 8, 1024)
    for i in range(4):
        merged_units[i, 0:6] = units_in[i]
    merged_copies = frame_copies(merged_units, (0, 0), (4, 6), strip_send, strip_recv, 0, before)
    streams = ((g_x, ROUTES[0]), (g_y, ROUTES[1]), (g_z, ROUTES[2]), (g_p, ROUTES[3]), (g_r, ROUTES[4]))
    buffers = tuple(stream_buffers[7 * i:7 * i + 7] for i in range(5))

    def slot_of(kind, chunk):
        return chunk % 2 if kind < 3 else 0

    def core_copy(kind, chunk):
        return remote(streams[kind][0].at[slot_of(kind, chunk), :, 1 - core], buffers[kind][0].at[chunk],
                      send.at[kind, chunk, 0], recv.at[kind, chunk, 0], sibling)

    def level_refs(kind, chunk, level):
        acc = buffers[kind][1 + 2 * level].at[chunk]
        into = buffers[kind][2 + 2 * level].at[chunk]
        dims = "hzyl"
        for i in range(level):
            dims = left_over(dims, streams[kind][1][i])
        return acc, into, dims, streams[kind][1][level]

    def level_copies(kind, chunk, level):
        acc, into, dims, axis = level_refs(kind, chunk, level)
        return [remote(acc.at[blocks_at(dims, axis, (here[axis] + i + 1) % 4)], into.at[i],
                       send.at[kind, chunk, 1 + level * 3 + i], recv.at[kind, chunk, 1 + level * 3 + i],
                       moved(axis, i + 1)) for i in range(3)]

    def core_to_first(kind, chunk):
        core_copy(kind, chunk).wait_recv()
        g, (from_core, acc) = streams[kind][0], buffers[kind][:2]
        width = g.shape[-1]

        @pl.loop(0, 8)
        def _(i):
            blocks = pl.ds(i * 8, 8)
            total = g[slot_of(kind, chunk), blocks, core].astype(F32) + from_core[chunk, blocks].astype(F32)
            acc[chunk, i // 4, i % 4] = total.astype(BF16).reshape(4, 2, 16, width)

        for copy in level_copies(kind, chunk, 0):
            copy.start()

    def level_to_next(kind, chunk, level):
        for copy in level_copies(kind, chunk, level):
            copy.wait_recv()
        acc, into, dims, axis = level_refs(kind, chunk, level)
        total = acc[blocks_at(dims, axis, here[axis])].astype(F32)
        for i in range(3):
            total = total + into[i].astype(F32)
        if level < 2:
            buffers[kind][3 + 2 * level][chunk] = total.astype(BF16)
            for copy in level_copies(kind, chunk, level + 1):
                copy.start()
            return
        width = total.shape[-1]
        if kind < 3:
            low = pl.multiple_of(kind * 1024 + chunk * 256, 256)
            qkv_out[:, pl.ds(low, width)] = total[:8]
            qkv_out[:, pl.ds(pl.multiple_of(low + width, 128), width)] = total[8:]
        else:
            low = (kind - 3) * 512
            out_out[:, low:low + width] = total[:8]
            out_out[:, low + width:low + 2 * width] = total[8:]

    head_mask, group_mask = wide_masks()
    row8 = lax.broadcasted_iota(jnp.int32, (8, 256), 0)
    lane8 = lax.broadcasted_iota(jnp.int32, (8, 256), 1) // 32
    own_head = jnp.where(lane8 == row8, 1.0, 0.0).astype(BF16)
    edge = lax.axis_index("lat") == 0
    def put_terms(kind, chunk, i, terms):
        g = streams[kind][0]
        width = g.shape[-1]
        both = jnp.concatenate([terms[:, :, :width], terms[:, :, width:]], axis=1)
        pairs = terms.shape[0] // 2
        g[slot_of(kind, chunk), pl.ds(i * pairs, pairs)] = both.astype(BF16).reshape(pairs, 2, 16, width)

    def window_back(chunk, w):
        columns = pl.ds(pl.multiple_of(chunk * 256, 256), 256)
        rows = pl.ds(pl.multiple_of(w * 128, 128), 128)
        queries, keys, values = q[rows, columns], k[rows, columns], v[rows, columns]
        out_grad = mix_grad[rows, columns]
        product = (out_grad.astype(F32) * mix[rows, columns].astype(F32)).astype(BF16)
        spread_queries, spread_grads = stack(queries, group_mask), stack(out_grad, group_mask)
        weights = jnp.exp(dot(stack(keys, head_mask), spread_queries, NT) * SCALE)
        weights = jnp.where(other_region(512, 256, edge & (w < 3)), 0.0, weights)
        change = dot(stack(values, head_mask), spread_grads, NT)
        means = dot(own_head, product, NT)
        attention, scores_grad = [], []
        for head in range(4):
            part = weights[128 * head:128 * head + 128]
            part = part * (1.0 / jnp.sum(part, axis=0, keepdims=True))
            mean = jnp.concatenate([means[head:head + 1], means[4 + head:5 + head]], axis=1)
            attention.append(part.astype(BF16))
            scores_grad.append((part * (change[128 * head:128 * head + 128] - mean)).astype(BF16))
        dv[rows, columns] = select(dot(jnp.concatenate(attention, axis=0), spread_grads), head_mask).astype(BF16)
        dk[rows, columns] = (select(dot(jnp.concatenate(scores_grad, axis=0), spread_queries), head_mask)
                             * SCALE).astype(BF16)
        turned = keys.T
        pieces = []
        for group in range(2):
            for head in range(4):
                low = group * 128 + head * 32
                pieces.append(dot(turned[low:low + 32], scores_grad[head][:, group * 128:group * 128 + 128]))
        dq[rows, columns] = (jnp.concatenate(pieces, axis=0).T * SCALE).astype(BF16)

    def finish_window(w):
        pieces = []
        for i in range(4):
            rows = pl.ds(pl.multiple_of(w * 128 + i * 32, 32), 32)
            change = normed_grad[rows].astype(BF16).astype(F32)
            centered, inverse = statistics(x_in[rows].astype(F32))
            normed = centered * inverse
            first = jnp.mean(change, axis=-1, keepdims=True)
            second = jnp.mean(change * normed, axis=-1, keepdims=True)
            value = (inverse * (change - first - normed * second)).astype(BF16).astype(F32) + grad[rows].astype(F32)
            pieces.append(value.astype(BF16))
        quarters = dot(to_quarters[...], jnp.concatenate(pieces, axis=0), TN).astype(BF16).reshape(4, 32, 1024)
        wa, wb = w // 3, w % 3
        for u in range(2):
            for side in range(2):
                units[2 * wa + u, 2 * wb + side] = quarters[2 * u + side]

    strips = frame_copies(units, (0, 0), (4, 6), strip_send, strip_recv, 3, before)

    @pl.loop(0, 8)
    def _(t):
        @pl.when(t < CHUNKS)
        def _():
            for copy in chunk_loads(t):
                copy.wait()

            @pl.loop(0, 2)
            def _(wa):
                for wb in range(3):
                    window_back(t, wa * 3 + wb)

        @pl.when(t == 0)
        def _():
            await_greetings(ring + list(before))
            for copy in merged_copies:
                copy.start()
            mix_load.wait()
            grad_load.wait()

            @pl.loop(0, 4)
            def _(i):
                rows = pl.ds(pl.multiple_of(i * 256, 256), 256)
                for kind in (3, 4):
                    low = (kind - 3) * 512
                    put_terms(kind, 0, i, dot(mix_turned[rows], grad[:, low:low + 512]).reshape(32, 8, 512))

            for kind in (3, 4):
                core_copy(kind, 0).start()

            normed_load.wait()

        @pl.when((t == 4) | (t == 5))
        def _():
            @pl.when(t == 4)
            def _():
                weight_load.wait()
                x_load.wait()

            tokens = pl.ds(pl.multiple_of((t - 4) * 384, 384), 384)

            @pl.loop(0, 4)
            def _(i):
                rows = pl.ds(pl.multiple_of(i * 256, 256), 256)
                normed_grad[tokens, rows] = (dot(dq[tokens], qkv_weight[rows, 0:1024], NT)
                                             + dot(dk[tokens], qkv_weight[rows, 1024:2048], NT)
                                             + dot(dv[tokens], qkv_weight[rows, 2048:3072], NT))

            @pl.when(t == 4)
            def _():
                for kind in range(3):
                    core_to_first(kind, 3)

            @pl.when(t == 5)
            def _():
                for kind in range(3):
                    level_to_next(kind, 3, 0)

            @pl.loop(0, 3)
            def _(wb):
                finish_window((t - 4) * 3 + wb)

                @pl.when((t == 5) & (wb == 0))
                def _():
                    strips[1].start()

            @pl.when(t == 4)
            def _():
                strips[0].start()
                strips[2].start()

        @pl.when(t == 6)
        def _():
            for copy in merged_copies:
                copy.wait_recv()
            framed = jnp.concatenate([merged_units[i, 1:7].reshape(48, 1024) for i in range(1, 5)], axis=0)
            merged_out[...] = dot(merged_natural[...], framed.astype(BF16)).astype(BF16)
            for kind in range(3):
                level_to_next(kind, 3, 1)
            strips[1].wait_recv()

        @pl.when(t == 7)
        def _():
            strips[0].wait_recv()
            strips[2].wait_recv()

        @pl.when(t >= 6)
        def _():
            m = t - 6
            blocks = []
            for n in range(3):
                parts = [units[2 * m + 1 + u, 2 * n + 1 + side] for u in range(2) for side in range(2)]
                blocks.append(dot(to_natural[...], jnp.concatenate(parts, axis=0)).reshape(2, 8, 8, 1024))
            tokens_out[:, pl.ds(8 * m, 8)] = jnp.concatenate(blocks, axis=2).astype(BF16)

        for level in (2, 1, 0):
            chunk = t - 2 - level

            @pl.when((chunk >= 0) & (chunk < CHUNKS - (level < 2)))
            def _():
                for kind in range(3):
                    level_to_next(kind, chunk, level)

        @pl.when((t >= 1) & (t < CHUNKS))
        def _():
            for kind in range(3):
                core_to_first(kind, t - 1)

        @pl.when(t == 1)
        def _():
            for kind in (3, 4):
                core_to_first(kind, 0)

        for level in range(3):
            @pl.when(t == level + 3)
            def _():
                for kind in (3, 4):
                    level_to_next(kind, 0, level)

        @pl.when(t < CHUNKS)
        def _():
            @pl.when(t >= 2)
            def _():
                for kind in range(3):
                    core_copy(kind, t - 2).wait_send()

            columns = pl.ds(pl.multiple_of(t * 256, 256), 256)

            @pl.loop(0, 2)
            def _(i):
                rows = pl.ds(pl.multiple_of(i * 512, 512), 512)
                for kind, right in enumerate((dq, dk, dv)):
                    put_terms(kind, t, i, dot(normed_turned[rows], right[:, columns]).reshape(64, 8, 256))

            for kind in range(3):
                core_copy(kind, t).start()

    for kind in range(3):
        core_copy(kind, 2).wait_send()
        core_copy(kind, 3).wait_send()

    @pl.loop(0, CHUNKS)
    def _(chunk):
        for kind in range(3):
            for level in range(3):
                for copy in level_copies(kind, chunk, level):
                    copy.wait_send()

    for kind in (3, 4):
        core_copy(kind, 0).wait_send()
        for level in range(3):
            for copy in level_copies(kind, 0, level):
                copy.wait_send()
    for copy in merged_copies + strips:
        copy.wait_send()


def back(q, k, v, mix, mix_grad, normed_turned, mix_turned, grad, x, qkv_weight, merged_groups):
    buffers = []
    for route, count, width in zip(ROUTES, (CHUNKS,) * 3 + (1,) * 2, (128,) * 3 + (256,) * 2):
        first = left_over("hzyl", route[0])
        second = left_over(first, route[1])
        for shape in ((64,), (2, 4, 4, 2), (3, *sizes(first)), sizes(first), (3, *sizes(second)), sizes(second), (3,)):
            buffers.append(pltpu.VMEM((count, *shape, 16, width), BF16))
    vmem, anywhere = pl.BlockSpec(memory_space=pltpu.VMEM), pl.BlockSpec(memory_space=pl.ANY)
    tokens = pltpu.VMEM((768, 1024), BF16)
    turned = pltpu.VMEM((1024, 768), BF16)
    return pl.pallas_call(
        back_kernel,
        out_shape=(jax.ShapeDtypeStruct((8, 3072), F32), jax.ShapeDtypeStruct((8, 1024), F32),
                   jax.ShapeDtypeStruct((2, 16, 24, 1024), BF16), jax.ShapeDtypeStruct((192, 1024), BF16)),
        in_specs=[anywhere] * 10 + [vmem] * 5,
        out_specs=(vmem, vmem, vmem, vmem),
        scratch_shapes=[
            tokens, tokens, tokens, tokens, tokens, turned, turned, tokens, tokens, pltpu.VMEM((1024, 3072), BF16),
            tokens, tokens, tokens,
            *[pltpu.VMEM((2, 64, 2, 16, 128), BF16)] * 3, *[pltpu.VMEM((1, 64, 2, 16, 256), BF16)] * 2,
            pltpu.VMEM((768, 1024), F32),
            pltpu.VMEM((5, 7, 32, 1024), BF16),
            pltpu.VMEM((5, 7, 8, 1024), F32),
            *buffers,
            pltpu.SemaphoreType.DMA((25,)),
            pltpu.SemaphoreType.DMA((5, CHUNKS, 10)),
            pltpu.SemaphoreType.DMA((5, CHUNKS, 10)),
            pltpu.SemaphoreType.DMA((6,)),
            pltpu.SemaphoreType.DMA((6,)),
        ],
        compiler_params=pltpu.CompilerParams(collective_id=0, has_side_effects=True, vmem_limit_bytes=62 * MIB),
        name="back",
    )(q, k, v, mix, mix_grad, normed_turned, mix_turned, grad, x, qkv_weight, merged_groups, *orders())


def place_kernel(tokens, merged, qkv, out, tokens_out, merged_out, qkv_out, out_out):
    tokens_out[...] = tokens[...]
    merged_out[...] = merged[...]
    qkv_out[...] = qkv[...]
    out_out[...] = out[...]


def place_results(*results):
    blocks = (pl.BlockSpec((1, 8, 24, 1024), lambda i: (i // 2, i % 2, 0, 0)), pl.BlockSpec((48, 1024), lambda i: (i, 0)),
              pl.BlockSpec((8, 768), lambda i: (0, i)), pl.BlockSpec((8, 256), lambda i: (0, i)))
    return pl.pallas_call(
        place_kernel,
        grid=(4,),
        out_shape=tuple(jax.ShapeDtypeStruct(result.shape, result.dtype) for result in results),
        in_specs=list(blocks),
        out_specs=blocks,
        compiler_params=pltpu.CompilerParams(vmem_limit_bytes=62 * MIB),
        name="place_results",
    )(*results)


def front_kernel(tokens, merged_grad, weight_hbm, out_weight_hbm, merge_weight_hbm,
                 to_natural, to_quarters, merged_natural, merged_windows,
                 x_hbm, normed_hbm, q_hbm, k_hbm, v_hbm, mix_hbm, mix_turned_hbm, grad_hbm, mix_grad_hbm, merged_out,
                 x, normed, normed_turned, q, k, v, mix, mix_turned, grad, mix_grad,
                 qkv_weight, out_weight, merge_weight, merge_normed, scaled, change, inverses, groups, units, merged_units,
                 load, store, send, recv):
    loads = [pltpu.make_async_copy(source, target, load.at[i]) for i, (source, target) in enumerate(
        ((weight_hbm, qkv_weight), (out_weight_hbm, out_weight), (merge_weight_hbm, merge_weight)))]
    for copy in loads:
        copy.start()
    before, after = neighbours(-1), neighbours(1)
    greet(before)
    copies = (frame_copies(units, (4, 6), (0, 0), send, recv, 0, after)
              + frame_copies(merged_units, (4, 6), (0, 0), send, recv, 3, after))

    @pl.loop(0, 32)
    def _(i):
        change[pl.ds(pl.multiple_of(i * 24, 8), 24)] = tokens[i // 16, i % 16].astype(F32)

    await_greetings(after)

    @pl.loop(0, 6)
    def _(i):
        m = jnp.where((i >= 1) & (i <= 3), 1, 0)
        n = jnp.where(i < 2, 2, 1 - i % 2)
        natural = [change[pl.ds(pl.multiple_of((level * 16 + 8 * m + row) * 24 + 8 * n, 8), 8)]
                   for level in range(2) for row in range(8)]
        quarters = dot(to_natural[...], jnp.concatenate(natural, axis=0).astype(BF16), TN)
        quarters = quarters.astype(BF16).reshape(4, 32, 1024)
        for u in range(2):
            for side in range(2):
                units[2 * m + 1 + u, 2 * n + 1 + side] = quarters[2 * u + side]

        @pl.when(i == 1)
        def _():
            copies[1].start()

        @pl.when(i == 3)
        def _():
            copies[0].start()
            copies[2].start()

    merged_in = dot(merged_natural[...], merged_grad[...], TN).reshape(4, 6, 8, 1024)
    for i in range(4):
        merged_units[i + 1, 1:7] = merged_in[i]
    for copy in copies[3:]:
        copy.start()

    def window(w):
        wa, wb = w // 3, w % 3
        quarters = [units[2 * wa + u, 2 * wb + side] for u in range(2) for side in range(2)]
        values = dot(to_quarters[...], jnp.concatenate(quarters, axis=0))
        rows = pl.ds(pl.multiple_of(w * 128, 128), 128)
        x[rows] = values.astype(BF16)
        for i in range(4):
            centered, inverse = statistics(values[32 * i:32 * i + 32])
            normed[pl.ds(pl.multiple_of(w * 128 + 32 * i, 32), 32)] = (centered * inverse).astype(BF16)
        normed_turned[:, rows] = normed[rows].T

    head_mask, group_mask = wide_masks()
    edge = lax.axis_index("lat") == 0

    def project(half, chunk):
        rows = pl.ds(pl.multiple_of(half * 384, 384), 384)
        columns = pl.ds(pl.multiple_of(chunk * 256, 256), 256)
        for third, target in enumerate((q, k, v)):
            low = pl.multiple_of(third * 1024 + chunk * 256, 256)
            target[rows, columns] = dot(normed[rows], qkv_weight[:, pl.ds(low, 256)]).astype(BF16)

    def attend(half, chunk):
        columns = pl.ds(pl.multiple_of(chunk * 256, 256), 256)
        for wb in range(3):
            rows = pl.ds(pl.multiple_of(half * 384 + wb * 128, 128), 128)
            scores = dot(stack(q[rows, columns], head_mask), stack(k[rows, columns], group_mask), NT)
            weights = jnp.exp(scores * SCALE)
            weights = jnp.where(other_region(512, 256, edge & (half == 0)), 0.0, weights)
            pieces = []
            for group in range(2):
                piece = weights[:, group * 128:group * 128 + 128]
                pieces.append((piece * (1.0 / jnp.sum(piece, axis=-1, keepdims=True))).astype(BF16))
            mixture = select(dot(jnp.concatenate(pieces, axis=1), stack(v[rows, columns], group_mask)), head_mask)
            mixture = mixture.astype(BF16)
            mix[rows, columns] = mixture
            mix_turned[columns, rows] = mixture.T

    keeps = [(x, x_hbm), (normed_turned, normed_hbm), (q, q_hbm), (k, k_hbm), (v, v_hbm), (mix, mix_hbm),
             (mix_turned, mix_turned_hbm), (grad, grad_hbm), (mix_grad, mix_grad_hbm)]
    stores = [pltpu.make_async_copy(source, target, store.at[i]) for i, (source, target) in enumerate(keeps)]

    def add_branch(half, chunk):
        rows = pl.ds(pl.multiple_of(half * 384, 384), 384)
        columns = pl.ds(pl.multiple_of(chunk * 256, 256), 256)
        scaled[rows, columns] = x[rows, columns].astype(F32) + dot(mix[rows], out_weight[:, columns])

    def quarter_rows(i):
        return [pl.ds(pl.multiple_of(i // 2 * 128 + j * 32 + i % 2 * 16, 16), 16) for j in range(4)]

    def group_rows(i):
        return [pl.ds(pl.multiple_of(j * 192 + i * 16, 16), 16) for j in range(4)]

    def normalize_groups(i):
        parts = [scaled[rows].astype(BF16).astype(F32) for rows in quarter_rows(i)]
        center = sum(jnp.sum(part, axis=-1, keepdims=True) for part in parts) * (1 / 4096)
        parts = [part - center for part in parts]
        spread = sum(jnp.sum(jnp.square(part), axis=-1, keepdims=True) for part in parts) * (1 / 4096)
        inverse = lax.rsqrt(spread + epsilon)
        inverses[pl.ds(pl.multiple_of(i * 16, 16), 16)] = jnp.broadcast_to(inverse, (16, 128))
        for part, rows in zip(parts, group_rows(i)):
            merge_normed[rows] = (part * inverse).astype(BF16)
        for part, rows in zip(parts, quarter_rows(i)):
            scaled[rows] = part * inverse

    @pl.loop(0, 2)
    def _(phase):
        half = 1 - phase

        @pl.loop(0, 3)
        def _(i):
            @pl.when((phase == 0) & (i == 2))
            def _():
                copies[1].wait_recv()

            @pl.when((phase == 1) & (i == 0))
            def _():
                copies[0].wait_recv()

            @pl.when((phase == 1) & (i == 2))
            def _():
                copies[2].wait_recv()

            window(half * 3 + (i + 1) % 3)

        @pl.when(phase == 0)
        def _():
            loads[0].wait()

        @pl.when(phase == 1)
        def _():
            stores[0].start()
            stores[1].start()

        project(half, 0)

        @pl.loop(0, 3)
        def _(chunk):
            project(half, chunk + 1)
            attend(half, chunk)

        attend(half, 3)

        @pl.when(phase == 0)
        def _():
            loads[1].wait()

        @pl.loop(0, 4)
        def _(chunk):
            add_branch(half, chunk)

        @pl.loop(0, 6)
        def _(i):
            normalize_groups(half * 6 + i)

    for copy in stores[2:7]:
        copy.start()
    for copy in copies[3:]:
        copy.wait_recv()
    framed = jnp.concatenate([merged_units[i, 0:6].reshape(48, 1024) for i in range(4)], axis=0)
    groups[...] = dot(merged_windows[...], framed.astype(BF16)).astype(BF16)
    loads[2].wait()

    def merge_columns(chunk):
        columns = pl.ds(pl.multiple_of(chunk * 256, 256), 256)
        total = dot(merge_normed[0:192], merge_weight[0:1024, columns])
        for j in range(1, 4):
            total = total + dot(merge_normed[192 * j:192 * j + 192], merge_weight[1024 * j:1024 * j + 1024, columns])
        merged_out[:, columns] = total.astype(BF16)
        for j in range(4):
            rows = pl.ds(pl.multiple_of(j * 1024 + chunk * 256, 256), 256)
            change[192 * j:192 * j + 192, columns] = dot(groups[...], merge_weight[rows], NT)

    pl.loop(0, 4)(merge_columns)

    def group_grads(i):
        changes = [change[rows].astype(BF16).astype(F32) for rows in group_rows(i)]
        values = [scaled[rows] for rows in quarter_rows(i)]
        first = sum(jnp.sum(part, axis=-1, keepdims=True) for part in changes) * (1 / 4096)
        second = sum(jnp.sum(part * value, axis=-1, keepdims=True) for part, value in zip(changes, values)) * (1 / 4096)
        inverse = inverses[pl.ds(pl.multiple_of(i * 16, 16), 16), 0:1]
        for part, value, rows in zip(changes, values, quarter_rows(i)):
            grad[rows] = (inverse * (part - first - value * second)).astype(BF16)

    pl.loop(0, 12)(group_grads)
    stores[7].start()

    def mixture_grads(chunk):
        rows = pl.ds(pl.multiple_of(chunk * 256, 256), 256)
        mix_grad[:, rows] = dot(grad[...], out_weight[rows], NT).astype(BF16)

    pl.loop(0, 4)(mixture_grads)
    stores[8].start()
    for copy in stores:
        copy.wait()
    for copy in copies:
        copy.wait_send()


def front(tokens, merged_grad, qkv_weight, out_weight, merge_weight):
    vmem, anywhere = pl.BlockSpec(memory_space=pltpu.VMEM), pl.BlockSpec(memory_space=pl.ANY)
    rows, turned = jax.ShapeDtypeStruct((768, 1024), BF16), jax.ShapeDtypeStruct((1024, 768), BF16)
    rows_vmem, turned_vmem = pltpu.VMEM((768, 1024), BF16), pltpu.VMEM((1024, 768), BF16)
    return pl.pallas_call(
        front_kernel,
        out_shape=(rows, turned, rows, rows, rows, rows, turned, rows, rows, jax.ShapeDtypeStruct((192, 1024), BF16)),
        in_specs=[vmem] * 2 + [anywhere] * 3 + [vmem] * 4,
        out_specs=(anywhere,) * 9 + (vmem,),
        scratch_shapes=[
            rows_vmem, rows_vmem, turned_vmem, rows_vmem, rows_vmem, rows_vmem, rows_vmem, turned_vmem, rows_vmem,
            rows_vmem,
            pltpu.VMEM((1024, 3072), BF16), pltpu.VMEM((1024, 1024), BF16), pltpu.VMEM((4096, 1024), BF16), rows_vmem,
            pltpu.VMEM((768, 1024), F32), pltpu.VMEM((768, 1024), F32), pltpu.VMEM((192, 128), F32),
            pltpu.VMEM((192, 1024), BF16),
            pltpu.VMEM((5, 7, 32, 1024), BF16),
            pltpu.VMEM((5, 7, 8, 1024), F32),
            pltpu.SemaphoreType.DMA((3,)),
            pltpu.SemaphoreType.DMA((9,)),
            pltpu.SemaphoreType.DMA((6,)),
            pltpu.SemaphoreType.DMA((6,)),
        ],
        compiler_params=pltpu.CompilerParams(collective_id=1, has_side_effects=True, vmem_limit_bytes=62 * MIB),
        name="front",
    )(tokens, merged_grad, qkv_weight, out_weight, merge_weight, *orders())


def shards(tokens, qkv_weight, out_weight, merge_weight, merged_grad):
    x, normed_turned, q, k, v, mixture, mix_turned, grad, mixture_grad, merged_groups = front(
        tokens, merged_grad.transpose(0, 2, 1, 3).reshape(192, 1024), qkv_weight, out_weight, merge_weight)
    qkv_weight_grad, out_weight_grad, tokens_grad, merged = back(
        q, k, v, mixture, mixture_grad, normed_turned, mix_turned, grad, x, qkv_weight, merged_groups)
    tokens_grad, merged, qkv_weight_grad, out_weight_grad = place_results(
        tokens_grad, merged, qkv_weight_grad, out_weight_grad)
    merged = merged.reshape(2, 12, 8, 1024).transpose(0, 2, 1, 3)
    return (merged, tokens_grad, qkv_weight_grad, out_weight_grad)


def solution(mesh):
    in_specs = (P(None, "lat", "lon", None), P(), P(), P(), P(None, "lat", "lon", None))
    out_specs = (
        P(None, "lat", "lon", None),
        P(None, "lat", "lon", None),
        P(("lat", "lon"), None),
        P(("lat", "lon"), None),
    )
    return jax.shard_map(shards, mesh=mesh, in_specs=in_specs, out_specs=out_specs, check_vma=False)
```

```python
import jax
import jax.numpy as jnp
import numpy as np
from jax import lax
from jax.experimental import pallas as pl
from jax.experimental.pallas import tpu as pltpu
from jax.sharding import PartitionSpec as P

CHUNKS = 4
ROUTES = ((0, 1, 2), (1, 0, 2), (2, 1, 0), (0, 1, 2), (1, 0, 2))
MESH = pl.DeviceIdType.MESH
F32, BF16 = jnp.float32, jnp.bfloat16
epsilon = 1e-05
SCALE = 32 ** -0.5
SCALE2 = SCALE * 1.4426950408889634
MIB = 1024 * 1024
NT = (((1,), (1,)), ((), ()))
TN = (((0,), (0,)), ((), ()))


def dot(left, right, dims=(((1,), (0,)), ((), ()))):
    return lax.dot_general(left, right, dims, preferred_element_type=F32)


def picks(index):
    return (index[:, None] == np.arange(len(index))[None, :]).astype(np.float32)


def window_order():
    t = np.arange(128)
    quarter, level, a, b = t // 32, t // 16 % 2, t // 4 % 4, t % 4
    return picks((level * 8 + 2 * a + quarter % 2) * 8 + 2 * b + quarter // 2)


def orders():
    n = np.arange(128)
    level, i, j = n // 64, n // 8 % 8, n % 8
    to_natural = picks((((i // 4) * 2 + j // 4) * 2 + level) * 16 + (i % 4) * 4 + j % 4)
    to_quarters = window_order() @ to_natural
    n = np.arange(192)
    level, j, i = n // 96, n // 8 % 12, n % 8
    merged_natural = picks((((i // 2) * 6 + j // 2) * 2 + level) * 4 + (i % 2) * 2 + j % 2)
    window, level, a, b = n // 32, n // 16 % 2, n // 4 % 4, n % 4
    row, column = 2 * (window // 3) + a // 2, 2 * (window % 3) + b // 2
    merged_windows = picks(((row * 6 + column) * 2 + level) * 4 + (a % 2) * 2 + b % 2)
    return tuple(jnp.asarray(order, BF16) for order in (to_natural, to_quarters, merged_natural, merged_windows))


def statistics(values):
    center = jnp.mean(values, axis=-1, keepdims=True)
    shifted_values = values - center
    spread = jnp.mean(jnp.square(shifted_values), axis=-1, keepdims=True)
    return shifted_values, lax.rsqrt(spread + epsilon)


def place():
    lat, lon = lax.axis_index("lat"), lax.axis_index("lon")
    return (lat // 4) * 2 + (lon // 2) % 2, lon // 4, lat % 4, lon % 2


def device_at(x, y, z, core):
    return ((x // 2) * 4 + z, y * 4 + (x % 2) * 2 + core)


def neighbours(step):
    lat, lon = lax.axis_index("lat"), lax.axis_index("lon")
    lat_there, lon_there = (lat + step + 8) % 8, (lon + step + 16) % 16
    return (lat_there, lon), (lat, lon_there), (lat_there, lon_there)


def greet(receive_from):
    barrier = pltpu.get_barrier_semaphore()
    for device in receive_from:
        pl.semaphore_signal(barrier, inc=1, device_id=device, device_id_type=MESH)


def await_greetings(send_to):
    pl.semaphore_wait(pltpu.get_barrier_semaphore(), len(send_to))


def remote(source, target, send, recv, device):
    return pltpu.make_async_remote_copy(src_ref=source, dst_ref=target, send_sem=send, recv_sem=recv,
                                        device_id=device, device_id_type=MESH)


def frame_copies(units, first, last, send, recv, base, devices):
    row, column, corner = devices
    return [remote(units.at[first[0], 1:6], units.at[last[0], 1:6], send.at[base], recv.at[base], row),
            remote(units.at[1:4, first[1]], units.at[1:4, last[1]], send.at[base + 1], recv.at[base + 1], column),
            remote(units.at[first[0], first[1]], units.at[last[0], last[1]], send.at[base + 2], recv.at[base + 2], corner)]


def blocks_at(dims, axis, p):
    index = ({"h": p // 2, "l": p % 2}, {"y": p}, {"z": p})[axis]
    return tuple(index.get(dim, slice(None)) for dim in dims)


def left_over(dims, axis):
    return "".join(dim for dim in dims if dim not in ("hl", "y", "z")[axis])


def sizes(dims):
    return tuple({"h": 2, "z": 4, "y": 4, "l": 2}[dim] for dim in dims)


def wide_masks():
    lane = lax.broadcasted_iota(jnp.int32, (128, 256), 1)
    return [lane % 128 // 32 == head for head in range(4)], [lane // 128 == group for group in range(2)]


def stack(values, masks):
    zero = jnp.zeros_like(values)
    return jnp.concatenate([jnp.where(mask, values, zero) for mask in masks], axis=0)


def select(stacked, masks):
    rows = [stacked[128 * head:128 * head + 128] for head in range(4)]
    return jnp.where(masks[0], rows[0], jnp.where(masks[1], rows[1], jnp.where(masks[2], rows[2], rows[3])))


def other_region(rows, columns, edge):
    row = (lax.broadcasted_iota(jnp.int32, (rows, 1), 0) // 4 % 4 < 2) & edge
    column = (lax.broadcasted_iota(jnp.int32, (1, columns), 1) // 4 % 4 < 2) & edge
    return row.astype(jnp.int32) != column.astype(jnp.int32)


def back_kernel(q_hbm, k_hbm, v_hbm, mix_hbm, mix_grad_hbm, normed_hbm, mix_turned_hbm, grad_hbm, x_hbm, weight_hbm,
                merged_in, to_natural, to_quarters, merged_natural, merged_windows,
                qkv_out, out_out, tokens_out, merged_out,
                q, k, v, mix, mix_grad, normed_turned, mix_turned, grad, x_in, qkv_weight,
                dq, dk, dv, g_x, g_y, g_z, g_p, g_r, normed_grad, units, merged_units, *rest):
    stream_buffers, (load, send, recv, strip_send, strip_recv) = rest[:-5], rest[-5:]

    def fetch(index, source, target):
        return pltpu.make_async_copy(source, target, load.at[index])

    def chunk_loads(chunk):
        columns = pl.ds(pl.multiple_of(chunk * 256, 256), 256)
        return [fetch(chunk * 5 + i, source.at[:, columns], target.at[:, columns]) for i, (source, target) in enumerate(
            ((q_hbm, q), (k_hbm, k), (v_hbm, v), (mix_hbm, mix), (mix_grad_hbm, mix_grad)))]

    normed_load, mix_load = fetch(20, normed_hbm, normed_turned), fetch(21, mix_turned_hbm, mix_turned)
    grad_load, weight_load, x_load = fetch(22, grad_hbm, grad), fetch(23, weight_hbm, qkv_weight), fetch(24, x_hbm, x_in)
    for copy in chunk_loads(0):
        copy.start()
    mix_load.start()
    grad_load.start()
    normed_load.start()

    @pl.loop(1, CHUNKS)
    def _(chunk):
        for copy in chunk_loads(chunk):
            copy.start()

    weight_load.start()
    x_load.start()

    x, y, z, core = place()
    here = (x, y, z)

    def moved(axis, step):
        there = list(here)
        there[axis] = (here[axis] + step) % 4
        return device_at(there[0], there[1], there[2], core)

    sibling = device_at(x, y, z, 1 - core)
    ring = [sibling] + [moved(axis, step) for axis in range(3) for step in (1, 2, 3)]
    before, after = neighbours(-1), neighbours(1)
    greet(ring + list(after))

    units_in = dot(merged_windows[...], merged_in[...], TN).reshape(4, 6, 8, 1024)
    for i in range(4):
        merged_units[i, 0:6] = units_in[i]
    merged_copies = frame_copies(merged_units, (0, 0), (4, 6), strip_send, strip_recv, 0, before)
    streams = ((g_x, ROUTES[0]), (g_y, ROUTES[1]), (g_z, ROUTES[2]), (g_p, ROUTES[3]), (g_r, ROUTES[4]))
    buffers = tuple(stream_buffers[7 * i:7 * i + 7] for i in range(5))

    def slot_of(kind, chunk):
        return chunk % 2 if kind < 3 else 0

    def core_copy(kind, chunk):
        return remote(streams[kind][0].at[slot_of(kind, chunk), :, 1 - core], buffers[kind][0].at[chunk],
                      send.at[kind, chunk, 0], recv.at[kind, chunk, 0], sibling)

    def level_refs(kind, chunk, level):
        acc = buffers[kind][1 + 2 * level].at[chunk]
        into = buffers[kind][2 + 2 * level].at[chunk]
        dims = "hzyl"
        for i in range(level):
            dims = left_over(dims, streams[kind][1][i])
        return acc, into, dims, streams[kind][1][level]

    def level_copies(kind, chunk, level):
        acc, into, dims, axis = level_refs(kind, chunk, level)
        return [remote(acc.at[blocks_at(dims, axis, (here[axis] + i + 1) % 4)], into.at[i],
                       send.at[kind, chunk, 1 + level * 3 + i], recv.at[kind, chunk, 1 + level * 3 + i],
                       moved(axis, i + 1)) for i in range(3)]

    def core_to_first(kind, chunk):
        core_copy(kind, chunk).wait_recv()
        g, (from_core, acc) = streams[kind][0], buffers[kind][:2]
        width = g.shape[-1]

        @pl.loop(0, 8)
        def _(i):
            blocks = pl.ds(i * 8, 8)
            total = g[slot_of(kind, chunk), blocks, core].astype(F32) + from_core[chunk, blocks].astype(F32)
            acc[chunk, i // 4, i % 4] = total.astype(BF16).reshape(4, 2, 16, width)

        for copy in level_copies(kind, chunk, 0):
            copy.start()

    def level_to_next(kind, chunk, level):
        for copy in level_copies(kind, chunk, level):
            copy.wait_recv()
        acc, into, dims, axis = level_refs(kind, chunk, level)
        total = acc[blocks_at(dims, axis, here[axis])].astype(F32)
        for i in range(3):
            total = total + into[i].astype(F32)
        if level < 2:
            buffers[kind][3 + 2 * level][chunk] = total.astype(BF16)
            for copy in level_copies(kind, chunk, level + 1):
                copy.start()
            return
        width = total.shape[-1]
        if kind < 3:
            low = pl.multiple_of(kind * 1024 + chunk * 256, 256)
            qkv_out[:, pl.ds(low, width)] = total[:8]
            qkv_out[:, pl.ds(pl.multiple_of(low + width, 128), width)] = total[8:]
        else:
            low = (kind - 3) * 512
            out_out[:, low:low + width] = total[:8]
            out_out[:, low + width:low + 2 * width] = total[8:]

    head_mask, group_mask = wide_masks()
    row8 = lax.broadcasted_iota(jnp.int32, (8, 256), 0)
    lane8 = lax.broadcasted_iota(jnp.int32, (8, 256), 1) // 32
    own_head = jnp.where(lane8 == row8, 1.0, 0.0).astype(BF16)
    edge = lax.axis_index("lat") == 0
    def put_terms(kind, chunk, i, terms):
        g = streams[kind][0]
        width = g.shape[-1]
        both = jnp.concatenate([terms[:, :, :width], terms[:, :, width:]], axis=1)
        pairs = terms.shape[0] // 2
        g[slot_of(kind, chunk), pl.ds(i * pairs, pairs)] = both.astype(BF16).reshape(pairs, 2, 16, width)

    def window_back(chunk, w):
        columns = pl.ds(pl.multiple_of(chunk * 256, 256), 256)
        rows = pl.ds(pl.multiple_of(w * 128, 128), 128)
        queries, keys, values = q[rows, columns], k[rows, columns], v[rows, columns]
        out_grad = mix_grad[rows, columns]
        product = (out_grad.astype(F32) * mix[rows, columns].astype(F32)).astype(BF16)
        spread_queries, spread_grads = stack(queries, group_mask), stack(out_grad, group_mask)
        weights = jnp.exp2(dot(stack(keys, head_mask), spread_queries, NT) * SCALE2)
        weights = jnp.where(other_region(512, 256, edge & (w < 3)), 0.0, weights)
        change = dot(stack(values, head_mask), spread_grads, NT)
        means = dot(own_head, product, NT)
        attention, scores_grad = [], []
        for head in range(4):
            part = weights[128 * head:128 * head + 128]
            part = part * (1.0 / jnp.sum(part, axis=0, keepdims=True))
            mean = jnp.concatenate([means[head:head + 1], means[4 + head:5 + head]], axis=1)
            attention.append(part.astype(BF16))
            scores_grad.append((part * (change[128 * head:128 * head + 128] - mean)).astype(BF16))
        dv[rows, columns] = select(dot(jnp.concatenate(attention, axis=0), spread_grads), head_mask).astype(BF16)
        dk[rows, columns] = (select(dot(jnp.concatenate(scores_grad, axis=0), spread_queries), head_mask)
                             * SCALE).astype(BF16)
        turned = keys.T
        pieces = []
        for group in range(2):
            for head in range(4):
                low = group * 128 + head * 32
                pieces.append(dot(turned[low:low + 32], scores_grad[head][:, group * 128:group * 128 + 128]))
        dq[rows, columns] = (jnp.concatenate(pieces, axis=0).T * SCALE).astype(BF16)

    def finish_window(w):
        pieces = []
        for i in range(4):
            rows = pl.ds(pl.multiple_of(w * 128 + i * 32, 32), 32)
            change = normed_grad[rows].astype(BF16).astype(F32)
            centered, inverse = statistics(x_in[rows].astype(F32))
            normed = centered * inverse
            first = jnp.mean(change, axis=-1, keepdims=True)
            second = jnp.mean(change * normed, axis=-1, keepdims=True)
            value = (inverse * (change - first - normed * second)).astype(BF16).astype(F32) + grad[rows].astype(F32)
            pieces.append(value.astype(BF16))
        quarters = dot(to_quarters[...], jnp.concatenate(pieces, axis=0), TN).astype(BF16).reshape(4, 32, 1024)
        wa, wb = w // 3, w % 3
        for u in range(2):
            for side in range(2):
                units[2 * wa + u, 2 * wb + side] = quarters[2 * u + side]

    strips = frame_copies(units, (0, 0), (4, 6), strip_send, strip_recv, 3, before)

    @pl.loop(0, 8)
    def _(t):
        @pl.when(t < CHUNKS)
        def _():
            for copy in chunk_loads(t):
                copy.wait()

            @pl.loop(0, 2)
            def _(wa):
                for wb in range(3):
                    window_back(t, wa * 3 + wb)

        @pl.when(t == 0)
        def _():
            await_greetings(ring + list(before))
            for copy in merged_copies:
                copy.start()
            mix_load.wait()
            grad_load.wait()

            @pl.loop(0, 4)
            def _(i):
                rows = pl.ds(pl.multiple_of(i * 256, 256), 256)
                for kind in (3, 4):
                    low = (kind - 3) * 512
                    put_terms(kind, 0, i, dot(mix_turned[rows], grad[:, low:low + 512]).reshape(32, 8, 512))

            for kind in (3, 4):
                core_copy(kind, 0).start()

            normed_load.wait()

        @pl.when((t == 4) | (t == 5))
        def _():
            @pl.when(t == 4)
            def _():
                weight_load.wait()
                x_load.wait()

            tokens = pl.ds(pl.multiple_of((t - 4) * 384, 384), 384)

            @pl.loop(0, 4)
            def _(i):
                rows = pl.ds(pl.multiple_of(i * 256, 256), 256)
                normed_grad[tokens, rows] = (dot(dq[tokens], qkv_weight[rows, 0:1024], NT)
                                             + dot(dk[tokens], qkv_weight[rows, 1024:2048], NT)
                                             + dot(dv[tokens], qkv_weight[rows, 2048:3072], NT))

            @pl.when(t == 4)
            def _():
                for kind in range(3):
                    core_to_first(kind, 3)

            @pl.when(t == 5)
            def _():
                for kind in range(3):
                    level_to_next(kind, 3, 0)

            @pl.loop(0, 3)
            def _(wb):
                finish_window((t - 4) * 3 + wb)

                @pl.when((t == 5) & (wb == 0))
                def _():
                    strips[1].start()

            @pl.when(t == 4)
            def _():
                strips[0].start()
                strips[2].start()

        @pl.when(t == 6)
        def _():
            for copy in merged_copies:
                copy.wait_recv()
            framed = jnp.concatenate([merged_units[i, 1:7].reshape(48, 1024) for i in range(1, 5)], axis=0)
            merged_out[...] = dot(merged_natural[...], framed.astype(BF16)).astype(BF16)
            for kind in range(3):
                level_to_next(kind, 3, 1)
            strips[1].wait_recv()

        @pl.when(t == 7)
        def _():
            strips[0].wait_recv()
            strips[2].wait_recv()

        @pl.when(t >= 6)
        def _():
            m = t - 6
            blocks = []
            for n in range(3):
                parts = [units[2 * m + 1 + u, 2 * n + 1 + side] for u in range(2) for side in range(2)]
                blocks.append(dot(to_natural[...], jnp.concatenate(parts, axis=0)).reshape(2, 8, 8, 1024))
            tokens_out[:, pl.ds(8 * m, 8)] = jnp.concatenate(blocks, axis=2).astype(BF16)

        for level in (2, 1, 0):
            chunk = t - 2 - level

            @pl.when((chunk >= 0) & (chunk < CHUNKS - (level < 2)))
            def _():
                for kind in range(3):
                    level_to_next(kind, chunk, level)

        @pl.when((t >= 1) & (t < CHUNKS))
        def _():
            for kind in range(3):
                core_to_first(kind, t - 1)

        @pl.when(t == 1)
        def _():
            for kind in (3, 4):
                core_to_first(kind, 0)

        for level in range(3):
            @pl.when(t == level + 3)
            def _():
                for kind in (3, 4):
                    level_to_next(kind, 0, level)

        @pl.when(t < CHUNKS)
        def _():
            @pl.when(t >= 2)
            def _():
                for kind in range(3):
                    core_copy(kind, t - 2).wait_send()

            columns = pl.ds(pl.multiple_of(t * 256, 256), 256)

            for kind, right in enumerate((dq, dk, dv)):
                @pl.loop(0, 2)
                def _(i):
                    rows = pl.ds(pl.multiple_of(i * 512, 512), 512)
                    put_terms(kind, t, i, dot(normed_turned[rows], right[:, columns]).reshape(64, 8, 256))

                core_copy(kind, t).start()

    for kind in range(3):
        core_copy(kind, 2).wait_send()
        core_copy(kind, 3).wait_send()

    @pl.loop(0, CHUNKS)
    def _(chunk):
        for kind in range(3):
            for level in range(3):
                for copy in level_copies(kind, chunk, level):
                    copy.wait_send()

    for kind in (3, 4):
        core_copy(kind, 0).wait_send()
        for level in range(3):
            for copy in level_copies(kind, 0, level):
                copy.wait_send()
    for copy in merged_copies + strips:
        copy.wait_send()


def back(q, k, v, mix, mix_grad, normed_turned, mix_turned, grad, x, qkv_weight, merged_groups):
    buffers = []
    for route, count, width in zip(ROUTES, (CHUNKS,) * 3 + (1,) * 2, (128,) * 3 + (256,) * 2):
        first = left_over("hzyl", route[0])
        second = left_over(first, route[1])
        for shape in ((64,), (2, 4, 4, 2), (3, *sizes(first)), sizes(first), (3, *sizes(second)), sizes(second), (3,)):
            buffers.append(pltpu.VMEM((count, *shape, 16, width), BF16))
    vmem, anywhere = pl.BlockSpec(memory_space=pltpu.VMEM), pl.BlockSpec(memory_space=pl.ANY)
    tokens = pltpu.VMEM((768, 1024), BF16)
    turned = pltpu.VMEM((1024, 768), BF16)
    return pl.pallas_call(
        back_kernel,
        out_shape=(jax.ShapeDtypeStruct((8, 3072), F32), jax.ShapeDtypeStruct((8, 1024), F32),
                   jax.ShapeDtypeStruct((2, 16, 24, 1024), BF16), jax.ShapeDtypeStruct((192, 1024), BF16)),
        in_specs=[anywhere] * 10 + [vmem] * 5,
        out_specs=(vmem, vmem, vmem, vmem),
        scratch_shapes=[
            tokens, tokens, tokens, tokens, tokens, turned, turned, tokens, tokens, pltpu.VMEM((1024, 3072), BF16),
            tokens, tokens, tokens,
            *[pltpu.VMEM((2, 64, 2, 16, 128), BF16)] * 3, *[pltpu.VMEM((1, 64, 2, 16, 256), BF16)] * 2,
            pltpu.VMEM((768, 1024), F32),
            pltpu.VMEM((5, 7, 32, 1024), BF16),
            pltpu.VMEM((5, 7, 8, 1024), F32),
            *buffers,
            pltpu.SemaphoreType.DMA((25,)),
            pltpu.SemaphoreType.DMA((5, CHUNKS, 10)),
            pltpu.SemaphoreType.DMA((5, CHUNKS, 10)),
            pltpu.SemaphoreType.DMA((6,)),
            pltpu.SemaphoreType.DMA((6,)),
        ],
        compiler_params=pltpu.CompilerParams(collective_id=0, has_side_effects=True, vmem_limit_bytes=62 * MIB),
        name="back",
    )(q, k, v, mix, mix_grad, normed_turned, mix_turned, grad, x, qkv_weight, merged_groups, *orders())


def place_kernel(tokens, merged, qkv, out, tokens_out, merged_out, qkv_out, out_out):
    tokens_out[...] = tokens[...]
    merged_out[...] = merged[...]
    qkv_out[...] = qkv[...]
    out_out[...] = out[...]


def place_results(*results):
    blocks = (pl.BlockSpec((1, 8, 24, 1024), lambda i: (i // 2, i % 2, 0, 0)), pl.BlockSpec((48, 1024), lambda i: (i, 0)),
              pl.BlockSpec((8, 768), lambda i: (0, i)), pl.BlockSpec((8, 256), lambda i: (0, i)))
    return pl.pallas_call(
        place_kernel,
        grid=(4,),
        out_shape=tuple(jax.ShapeDtypeStruct(result.shape, result.dtype) for result in results),
        in_specs=list(blocks),
        out_specs=blocks,
        compiler_params=pltpu.CompilerParams(vmem_limit_bytes=62 * MIB),
        name="place_results",
    )(*results)


def front_kernel(tokens, merged_grad, weight_hbm, out_weight_hbm, merge_weight_hbm,
                 to_natural, to_quarters, merged_natural, merged_windows,
                 x_hbm, normed_hbm, q_hbm, k_hbm, v_hbm, mix_hbm, mix_turned_hbm, grad_hbm, mix_grad_hbm, merged_out,
                 x, normed, normed_turned, q, k, v, mix, mix_turned, grad, mix_grad,
                 qkv_weight, out_weight, merge_weight, merge_normed, scaled, change, inverses, groups, units, merged_units,
                 load, store, send, recv):
    loads = [pltpu.make_async_copy(source, target, load.at[i]) for i, (source, target) in enumerate(
        ((weight_hbm, qkv_weight), (out_weight_hbm, out_weight), (merge_weight_hbm, merge_weight)))]
    for copy in loads:
        copy.start()
    before, after = neighbours(-1), neighbours(1)
    greet(before)
    copies = (frame_copies(units, (4, 6), (0, 0), send, recv, 0, after)
              + frame_copies(merged_units, (4, 6), (0, 0), send, recv, 3, after))

    @pl.loop(0, 32)
    def _(i):
        change[pl.ds(pl.multiple_of(i * 24, 8), 24)] = tokens[i // 16, i % 16].astype(F32)

    await_greetings(after)

    @pl.loop(0, 6)
    def _(i):
        m = jnp.where((i >= 1) & (i <= 3), 1, 0)
        n = jnp.where(i < 2, 2, 1 - i % 2)
        natural = [change[pl.ds(pl.multiple_of((level * 16 + 8 * m + row) * 24 + 8 * n, 8), 8)]
                   for level in range(2) for row in range(8)]
        quarters = dot(to_natural[...], jnp.concatenate(natural, axis=0).astype(BF16), TN)
        quarters = quarters.astype(BF16).reshape(4, 32, 1024)
        for u in range(2):
            for side in range(2):
                units[2 * m + 1 + u, 2 * n + 1 + side] = quarters[2 * u + side]

        @pl.when(i == 1)
        def _():
            copies[1].start()

        @pl.when(i == 3)
        def _():
            copies[0].start()
            copies[2].start()

    merged_in = dot(merged_natural[...], merged_grad[...], TN).reshape(4, 6, 8, 1024)
    for i in range(4):
        merged_units[i + 1, 1:7] = merged_in[i]
    for copy in copies[3:]:
        copy.start()

    def window(w):
        wa, wb = w // 3, w % 3
        quarters = [units[2 * wa + u, 2 * wb + side] for u in range(2) for side in range(2)]
        values = dot(to_quarters[...], jnp.concatenate(quarters, axis=0))
        rows = pl.ds(pl.multiple_of(w * 128, 128), 128)
        x[rows] = values.astype(BF16)
        for i in range(4):
            centered, inverse = statistics(values[32 * i:32 * i + 32])
            normed[pl.ds(pl.multiple_of(w * 128 + 32 * i, 32), 32)] = (centered * inverse).astype(BF16)
        normed_turned[:, rows] = normed[rows].T

    head_mask, group_mask = wide_masks()
    edge = lax.axis_index("lat") == 0

    def project(half, chunk):
        rows = pl.ds(pl.multiple_of(half * 384, 384), 384)
        columns = pl.ds(pl.multiple_of(chunk * 256, 256), 256)
        for third, target in enumerate((q, k, v)):
            low = pl.multiple_of(third * 1024 + chunk * 256, 256)
            target[rows, columns] = dot(normed[rows], qkv_weight[:, pl.ds(low, 256)]).astype(BF16)

    def attend(half, chunk):
        columns = pl.ds(pl.multiple_of(chunk * 256, 256), 256)
        for wb in range(3):
            rows = pl.ds(pl.multiple_of(half * 384 + wb * 128, 128), 128)
            scores = dot(stack(q[rows, columns], head_mask), stack(k[rows, columns], group_mask), NT)
            weights = jnp.exp2(scores * SCALE2)
            weights = jnp.where(other_region(512, 256, edge & (half == 0)), 0.0, weights)
            pieces = []
            for group in range(2):
                piece = weights[:, group * 128:group * 128 + 128]
                pieces.append((piece * (1.0 / jnp.sum(piece, axis=-1, keepdims=True))).astype(BF16))
            mixture = select(dot(jnp.concatenate(pieces, axis=1), stack(v[rows, columns], group_mask)), head_mask)
            mixture = mixture.astype(BF16)
            mix[rows, columns] = mixture
            mix_turned[columns, rows] = mixture.T

    keeps = [(x, x_hbm), (normed_turned, normed_hbm), (q, q_hbm), (k, k_hbm), (v, v_hbm), (mix, mix_hbm),
             (mix_turned, mix_turned_hbm), (grad, grad_hbm), (mix_grad, mix_grad_hbm)]
    stores = [pltpu.make_async_copy(source, target, store.at[i]) for i, (source, target) in enumerate(keeps)]

    def add_branch(half, chunk):
        rows = pl.ds(pl.multiple_of(half * 384, 384), 384)
        columns = pl.ds(pl.multiple_of(chunk * 256, 256), 256)
        scaled[rows, columns] = x[rows, columns].astype(F32) + dot(mix[rows], out_weight[:, columns])

    def quarter_rows(i):
        return [pl.ds(pl.multiple_of(i // 2 * 128 + j * 32 + i % 2 * 16, 16), 16) for j in range(4)]

    def group_rows(i):
        return [pl.ds(pl.multiple_of(j * 192 + i * 16, 16), 16) for j in range(4)]

    def normalize_groups(i):
        parts = [scaled[rows].astype(BF16).astype(F32) for rows in quarter_rows(i)]
        center = sum(jnp.sum(part, axis=-1, keepdims=True) for part in parts) * (1 / 4096)
        parts = [part - center for part in parts]
        spread = sum(jnp.sum(jnp.square(part), axis=-1, keepdims=True) for part in parts) * (1 / 4096)
        inverse = lax.rsqrt(spread + epsilon)
        inverses[pl.ds(pl.multiple_of(i * 16, 16), 16)] = jnp.broadcast_to(inverse, (16, 128))
        for part, rows in zip(parts, group_rows(i)):
            merge_normed[rows] = (part * inverse).astype(BF16)
        for part, rows in zip(parts, quarter_rows(i)):
            scaled[rows] = part * inverse

    @pl.loop(0, 2)
    def _(phase):
        half = 1 - phase

        @pl.loop(0, 3)
        def _(i):
            @pl.when((phase == 0) & (i == 2))
            def _():
                copies[1].wait_recv()

            @pl.when((phase == 1) & (i == 0))
            def _():
                copies[0].wait_recv()

            @pl.when((phase == 1) & (i == 2))
            def _():
                copies[2].wait_recv()

            window(half * 3 + (i + 1) % 3)

        @pl.when(phase == 0)
        def _():
            loads[0].wait()

        @pl.when(phase == 1)
        def _():
            stores[0].start()
            stores[1].start()

        project(half, 0)

        @pl.loop(0, 3)
        def _(chunk):
            project(half, chunk + 1)
            attend(half, chunk)

        attend(half, 3)

        @pl.when(phase == 0)
        def _():
            loads[1].wait()

        @pl.loop(0, 4)
        def _(chunk):
            add_branch(half, chunk)

        @pl.loop(0, 6)
        def _(i):
            normalize_groups(half * 6 + i)

    for copy in stores[2:7]:
        copy.start()
    for copy in copies[3:]:
        copy.wait_recv()
    framed = jnp.concatenate([merged_units[i, 0:6].reshape(48, 1024) for i in range(4)], axis=0)
    groups[...] = dot(merged_windows[...], framed.astype(BF16)).astype(BF16)
    loads[2].wait()

    def merge_columns(chunk):
        columns = pl.ds(pl.multiple_of(chunk * 256, 256), 256)
        total = dot(merge_normed[0:192], merge_weight[0:1024, columns])
        for j in range(1, 4):
            total = total + dot(merge_normed[192 * j:192 * j + 192], merge_weight[1024 * j:1024 * j + 1024, columns])
        merged_out[:, columns] = total.astype(BF16)
        for j in range(4):
            rows = pl.ds(pl.multiple_of(j * 1024 + chunk * 256, 256), 256)
            change[192 * j:192 * j + 192, columns] = dot(groups[...], merge_weight[rows], NT)

    pl.loop(0, 4)(merge_columns)

    def group_grads(i):
        changes = [change[rows].astype(BF16).astype(F32) for rows in group_rows(i)]
        values = [scaled[rows] for rows in quarter_rows(i)]
        first = sum(jnp.sum(part, axis=-1, keepdims=True) for part in changes) * (1 / 4096)
        second = sum(jnp.sum(part * value, axis=-1, keepdims=True) for part, value in zip(changes, values)) * (1 / 4096)
        inverse = inverses[pl.ds(pl.multiple_of(i * 16, 16), 16), 0:1]
        for part, value, rows in zip(changes, values, quarter_rows(i)):
            grad[rows] = (inverse * (part - first - value * second)).astype(BF16)

    pl.loop(0, 12)(group_grads)
    stores[7].start()

    def mixture_grads(chunk):
        rows = pl.ds(pl.multiple_of(chunk * 256, 256), 256)
        mix_grad[:, rows] = dot(grad[...], out_weight[rows], NT).astype(BF16)

    pl.loop(0, 4)(mixture_grads)
    stores[8].start()
    for copy in stores:
        copy.wait()
    for copy in copies:
        copy.wait_send()


def front(tokens, merged_grad, qkv_weight, out_weight, merge_weight):
    vmem, anywhere = pl.BlockSpec(memory_space=pltpu.VMEM), pl.BlockSpec(memory_space=pl.ANY)
    rows, turned = jax.ShapeDtypeStruct((768, 1024), BF16), jax.ShapeDtypeStruct((1024, 768), BF16)
    rows_vmem, turned_vmem = pltpu.VMEM((768, 1024), BF16), pltpu.VMEM((1024, 768), BF16)
    return pl.pallas_call(
        front_kernel,
        out_shape=(rows, turned, rows, rows, rows, rows, turned, rows, rows, jax.ShapeDtypeStruct((192, 1024), BF16)),
        in_specs=[vmem] * 2 + [anywhere] * 3 + [vmem] * 4,
        out_specs=(anywhere,) * 9 + (vmem,),
        scratch_shapes=[
            rows_vmem, rows_vmem, turned_vmem, rows_vmem, rows_vmem, rows_vmem, rows_vmem, turned_vmem, rows_vmem,
            rows_vmem,
            pltpu.VMEM((1024, 3072), BF16), pltpu.VMEM((1024, 1024), BF16), pltpu.VMEM((4096, 1024), BF16), rows_vmem,
            pltpu.VMEM((768, 1024), F32), pltpu.VMEM((768, 1024), F32), pltpu.VMEM((192, 128), F32),
            pltpu.VMEM((192, 1024), BF16),
            pltpu.VMEM((5, 7, 32, 1024), BF16),
            pltpu.VMEM((5, 7, 8, 1024), F32),
            pltpu.SemaphoreType.DMA((3,)),
            pltpu.SemaphoreType.DMA((9,)),
            pltpu.SemaphoreType.DMA((6,)),
            pltpu.SemaphoreType.DMA((6,)),
        ],
        compiler_params=pltpu.CompilerParams(collective_id=1, has_side_effects=True, vmem_limit_bytes=62 * MIB),
        name="front",
    )(tokens, merged_grad, qkv_weight, out_weight, merge_weight, *orders())


def shards(tokens, qkv_weight, out_weight, merge_weight, merged_grad):
    x, normed_turned, q, k, v, mixture, mix_turned, grad, mixture_grad, merged_groups = front(
        tokens, merged_grad.transpose(0, 2, 1, 3).reshape(192, 1024), qkv_weight, out_weight, merge_weight)
    qkv_weight_grad, out_weight_grad, tokens_grad, merged = back(
        q, k, v, mixture, mixture_grad, normed_turned, mix_turned, grad, x, qkv_weight, merged_groups)
    tokens_grad, merged, qkv_weight_grad, out_weight_grad = place_results(
        tokens_grad, merged, qkv_weight_grad, out_weight_grad)
    merged = merged.reshape(2, 12, 8, 1024).transpose(0, 2, 1, 3)
    return (merged, tokens_grad, qkv_weight_grad, out_weight_grad)


def solution(mesh):
    in_specs = (P(None, "lat", "lon", None), P(), P(), P(), P(None, "lat", "lon", None))
    out_specs = (
        P(None, "lat", "lon", None),
        P(None, "lat", "lon", None),
        P(("lat", "lon"), None),
        P(("lat", "lon"), None),
    )
    return jax.shard_map(shards, mesh=mesh, in_specs=in_specs, out_specs=out_specs, check_vma=False)
```
